32 devices in a mesh: wide: 8 (over z, y), narrow: 4 (over x, core).
Axes of the slice: x: 2, y: 2, z: 4, core: 2. Of those that a mesh axis runs over, the one named last changes fastest.
Arguments:
- hidden: bfloat16 [32768, 768], P(('wide', 'narrow')), may hold values from -6 to 6
- segment: int32 [64, 512], P(('wide', 'narrow')), may hold values from 0 to 3, never falling along the last dimension, each value on 1 to 256 neighbouring positions
- w_qkv: bfloat16 [768, 2304], P('wide', 'narrow'), may hold values from -0.21875 to 0.21875
- w_out: bfloat16 [768, 768], P('wide', 'narrow'), may hold values from -0.875 to 0.875
- w_in: bfloat16 [768, 3072], P('wide', 'narrow'), may hold values from -0.21875 to 0.21875
- w_back: bfloat16 [3072, 768], P('wide', 'narrow'), may hold values from -0.109375 to 0.109375
- vectors: float32 [9216], P(('wide', 'narrow')), may hold values from -0.5 to 1.4, as said below
- cotangent: bfloat16 [32768, 768], P(('wide', 'narrow')), may hold values from -6 to 6
Outputs:
- output: bfloat16 [32768, 768], P(('wide', 'narrow'))
- grad_hidden: float32 [32768, 768], P(('wide', 'narrow'))
- grad_w_qkv: float32 [768, 2304], P('wide', 'narrow')
- grad_w_out: float32 [768, 768], P('wide', 'narrow')
- grad_w_in: float32 [768, 3072], P('wide', 'narrow')
- grad_w_back: float32 [3072, 768], P('wide', 'narrow')
- grad_vectors: float32 [9216], P(('wide', 'narrow'))
The draws below stay inside these ranges and needn't reach their ends.
Inputs may be any that keep to these rules, and one draw needn't show every extreme that they name: segment numbers never fall along a packed row; each document covers 1 to 256 tokens. `vectors`: the gains lie from 0.6 to 1.4, the biases and shifts from -0.5 to 0.5.
All inputs are finite; a program needn't handle non-finite values.
Results may differ from the reference program's by a relative error of at most 0.015.
Values may be sent and summed in bfloat16 or wider, within the bound.
No kernel may reach another device: no remote copies, remote signals or barrier semaphores. Data moves between devices by JAX's collectives and lax.ppermute only.
A program may use at most 192 MiB of HBM per device.

```python
import math
import jax
import jax.numpy as jnp
import numpy as np
from jax import lax

D = 768
HEADS = 12
FF = 3072
SEQ = 512
SEGS = 4
MOST_SEG = 256
ROWS = 64
TOKENS = 32768


def draw_vectors(key, part):
    key = jax.random.fold_in(key, 5)
    first_key, second_key = jax.random.split(key)
    total = 8 * D + FF
    biases = jax.random.uniform(first_key, (total,), jnp.float32, -0.5, 0.5)
    gains = jax.random.uniform(second_key, (total,), jnp.float32, 0.6, 1.4)
    index = jnp.arange(total)
    is_gain = (index >= 3 * D) & (index < 4 * D) | (index >= 6 * D + FF) & (index < 7 * D + FF)
    return jnp.where(is_gain, gains, biases).astype(jnp.float32)


def spiked(entries, stream_key, source, target, blocks, factor):
    owner, partner = [(jnp.arange(entries.shape[axis_at]) // (entries.shape[axis_at] // blocks)).reshape([-1 if axis == axis_at else 1 for axis in range(entries.ndim)]) for axis_at in (source, target)]
    chosen = jax.random.permutation(stream_key, blocks)[partner]
    strong = (owner == chosen) | (owner == (partner + blocks // 2) % blocks)
    return jnp.where(strong, factor * entries, entries)


def levels(key, extent, shards, low, top_value):
    def one(axis_at, blocks):
        steps = jax.random.uniform(jax.random.fold_in(jax.random.fold_in(key, 6), axis_at), (blocks,), jnp.float32, low / len(shards), top_value / len(shards))
        return jnp.repeat(jnp.exp(steps), extent[axis_at] // blocks).reshape((-1,) + (1,) * (len(extent) - axis_at - 1))

    factor_of = one(*shards[0])
    for cut in shards[1:]:
        factor_of = factor_of * one(*cut)
    return factor_of


def split_up(count, total, limit, slope):
    weights = [(1 << 20) // math.isqrt(rank ** slope) + 1 for rank in range(2, count + 1)]
    rest, given = total - limit - (count - 1), [1] * (count - 1)
    while rest > 0:
        free = [i for i in range(count - 1) if given[i] < limit]
        pool, left = sum([weights[i] for i in free]), rest
        for i in free:
            more = min(limit - given[i], max(1, left * weights[i] // pool), rest)
            given[i] = given[i] + more
            rest = rest - more
    return np.array([limit] + given)


def uneven(rng, amount, total, limit, slope):
    if amount == 2:
        one = jax.random.randint(rng, (), max(1, total - limit), min(limit, total - 1) + 1)
        return jnp.stack([one, total - one])
    tallies = jnp.asarray(split_up(amount, total, limit, slope), jnp.int32)
    twos = (amount - 1) // 2
    giver, receiver = tallies[1:1 + 2 * twos:2], tallies[2:2 + 2 * twos:2]
    slack = jnp.minimum(giver - 1, limit - receiver)
    passed = jax.random.randint(jax.random.fold_in(rng, 1), (twos,), 0, 1 << 20) % (slack + 1)
    tallies = tallies.at[1:1 + 2 * twos:2].set(giver - passed).at[2:2 + 2 * twos:2].set(receiver + passed)
    return tallies[jax.random.permutation(jax.random.fold_in(rng, 2), amount)]


def bell_draw(key, extent, scale, reach, cuts=(), held_as=jnp.bfloat16):
    drawn = jax.random.normal(key, extent, jnp.float32) * scale
    if len(cuts) > 0:
        drawn = levels(key, extent, cuts, -0.22, 0.18) * drawn
    return jnp.clip(drawn, min=-reach, max=reach).astype(held_as)


def noise_with(key, extent, scale, bound, cuts, heavy, dtype=jnp.bfloat16):
    array = scale * jax.random.normal(key, extent, jnp.float32)
    if cuts:
        array = array * levels(key, extent, cuts, -0.22, 0.18)
    return jnp.clip(spiked(array, jax.random.fold_in(key, 3), *heavy), -bound, bound).astype(dtype)


def setup_inputs(seed: int = 0) -> dict:
    splits = jax.random.split(jax.random.key(seed), 9)
    return {
        "hidden": noise_with(splits[0], (TOKENS, D), 1.0, 6.0, ((0, 32),), (0, 1, 32, 2.75)),
        "segment": jax.vmap(lambda own: jnp.searchsorted(jnp.cumsum(uneven(own, SEGS, SEQ, MOST_SEG, 0)), jnp.arange(SEQ), side="right"))(jax.random.split(splits[1], ROWS)).reshape((ROWS, SEQ)).astype(jnp.int32),
        "w_qkv": bell_draw(splits[2], (D, 3 * D), D ** -0.5, 0.21875, ((0, 8), (1, 4))),
        "w_out": bell_draw(splits[3], (D, D), (D // 16) ** -0.5, 0.875, ((0, 8), (1, 4))),
        "w_in": bell_draw(splits[4], (D, FF), D ** -0.5, 0.21875, ((0, 8), (1, 4))),
        "w_back": bell_draw(splits[5], (FF, D), FF ** -0.5, 0.109375, ((0, 8), (1, 4))),
        "vectors": draw_vectors(jax.random.fold_in(splits[8], 71), 0),
        "cotangent": noise_with(splits[7], (TOKENS, D), 1.0, 6.0, ((0, 32),), (0, 1, 32, 2.75)),
    }


@jax.custom_vjp
def low(v):
    return lax.optimization_barrier(v.astype(jnp.bfloat16)).astype(jnp.float32)

@jax.custom_vjp
def low_back(v):
    return v

def low_keep(v):
    return (low(v), None)

def low_pass(kept, grad):
    return (grad,)

def back_keep(v):
    return (v, None)

def back_low(kept, grad):
    return (low(grad),)
low.defvjp(low_keep, low_pass)
low_back.defvjp(back_keep, back_low)
epsilon = 1e-06
highest = lax.Precision.HIGHEST

def normalize(values, gain, shift):
    center = values - lax.optimization_barrier(jnp.mean(values, -1, keepdims=True))
    spread = lax.optimization_barrier(jnp.mean(center * center, -1, keepdims=True))
    return center * lax.rsqrt(spread + epsilon) * gain + shift

def split_vectors(vectors):
    return (vectors[0:D], vectors[D:2 * D], vectors[2 * D:3 * D], vectors[3 * D:4 * D], vectors[4 * D:5 * D], vectors[5 * D:5 * D + FF], vectors[5 * D + FF:6 * D + FF], vectors[6 * D + FF:7 * D + FF], vectors[7 * D + FF:8 * D + FF])

def layer_group(params, hidden, segment):
    w_qkv, w_out, w_in, w_back, vectors = params
    bias_query, bias_value, bias_out, gain_first, shift_first, bias_inner, bias_back, gain_second, shift_second = split_vectors(vectors)
    groups = hidden.shape[0]
    head_dim = D // HEADS
    projected = jnp.einsum('gsd,de->gse', hidden, w_qkv, precision=highest)
    qkv_bias = jnp.concatenate([bias_query, jnp.zeros((D,), jnp.float32), bias_value])
    packed = low(low_back(projected) + qkv_bias).reshape(groups, SEQ, 3, HEADS, head_dim)
    queries = packed[:, :, 0]
    keys_all = packed[:, :, 1]
    value_rows = packed[:, :, 2]
    scores = jnp.einsum('gqhd,gkhd->ghqk', queries, keys_all, precision=highest)
    scores = low_back(scores * head_dim ** (-0.5))
    same_segment = segment[:, None, :, None] == segment[:, None, None, :]
    scores = jnp.where(same_segment, scores, -1000000000.0)
    largest = lax.optimization_barrier(jnp.max(scores, -1, keepdims=True))
    weights = jnp.exp(scores - largest)
    weights = weights / lax.optimization_barrier(jnp.sum(weights, -1, keepdims=True))
    attended = jnp.einsum('ghqk,gkhd->gqhd', low(weights), value_rows, precision=highest)
    attended = low_back(low(attended.reshape(groups, SEQ, D)))
    branch = low_back(jnp.einsum('gsd,de->gse', attended, w_out, precision=highest)) + bias_out
    first_out = normalize(hidden + branch, gain_first, shift_first)
    inner_act = low_back(jnp.einsum('gsd,df->gsf', low(first_out), w_in, precision=highest)) + bias_inner
    activated = low(jax.nn.gelu(inner_act, approximate=False))
    outward = low_back(jnp.einsum('gsf,fd->gsd', activated, w_back, precision=highest)) + bias_back
    return normalize(first_out + outward, gain_second, shift_second)

def reference(hidden, segment, w_qkv, w_out, w_in, w_back, vectors, cotangent):
    rows_all = hidden.shape[0] // SEQ
    group_rows = max([g for g in range(1, rows_all + 1) if rows_all % g == 0 and g * SEQ <= 4096])
    blocks = rows_all // group_rows
    segments = segment.reshape(blocks, group_rows, SEQ)

    def forward(inputs_all, weight_qkv, weight_out, weight_in, weight_back, vector_all):
        params = (weight_qkv, weight_out, weight_in, weight_back, vector_all)

        def group_step(carried, block_item):
            return (carried, jax.checkpoint(layer_group)(params, block_item[0], block_item[1]))
        shaped = inputs_all.reshape(blocks, group_rows, SEQ, D)
        _, outputs = lax.scan(group_step, jnp.zeros((), jnp.float32), (shaped, segments))
        return outputs.reshape(rows_all * SEQ, D)
    output, pullback = jax.vjp(forward, hidden.astype(jnp.float32), w_qkv.astype(jnp.float32), w_out.astype(jnp.float32), w_in.astype(jnp.float32), w_back.astype(jnp.float32), vectors)
    gradients = pullback(cotangent.astype(jnp.float32))
    return (output.astype(jnp.bfloat16), gradients[0], gradients[1], gradients[2], gradients[3], gradients[4], gradients[5])
```

```python
import functools

import jax
import jax.numpy as jnp
from jax import lax
from jax.experimental import pallas as pl
from jax.experimental.pallas import tpu as pltpu
from jax.sharding import PartitionSpec as P

D = 768
HEADS = 12
FF = 3072
ALL = ("wide", "narrow")
CHIP_STEPS = ((0, 0), (1, 0), (0, 1), (1, 1))

epsilon = 1e-06


def send(values, z=0, y=0, x=0, core=0):
    flip_wide, flip_narrow = 2 * z + y, 2 * x + core
    pairs = [
        (w * 4 + n, (w ^ flip_wide) * 4 + (n ^ flip_narrow)) for w in range(8) for n in range(4)
    ]
    return lax.ppermute(values, ALL, pairs)


def position():
    wide, narrow = lax.axis_index("wide"), lax.axis_index("narrow")
    return wide // 2, wide % 2, narrow // 2, narrow % 2


def gather_z(values):
    return jnp.stack([values] + [send(values, z=k) for k in (1, 2, 3)])


def gather_chips(lines):
    return [lines] + [send(lines, x=i, y=j) for i, j in CHIP_STEPS[1:]]


def gather_cores(blocks):
    return blocks + [send(block, core=1) for block in blocks]


def pair_kernel(*refs):
    count = len(refs) // 3
    core = lax.rem(lax.axis_index("narrow"), 2)
    for own, other, out in zip(refs[:count], refs[count : 2 * count], refs[2 * count :]):
        rows, columns = own.shape[0] // 2, own.shape[1]
        half = pl.ds(pl.multiple_of(core * rows, rows), rows)

        @pl.when(core == 0)
        def _(own=own, other=other, out=out, half=half, columns=columns):
            out[:, :columns] = own[half, :]
            out[:, columns:] = other[half, :]

        @pl.when(core == 1)
        def _(own=own, other=other, out=out, half=half, columns=columns):
            out[:, :columns] = other[half, :]
            out[:, columns:] = own[half, :]


def pair_up(*pieces):
    others = [send(piece, core=1) for piece in pieces]
    return pl.pallas_call(
        pair_kernel,
        out_shape=[
            jax.ShapeDtypeStruct((piece.shape[0] // 2, piece.shape[1] * 2), piece.dtype)
            for piece in pieces
        ],
        name="pair_up",
    )(*pieces, *others)


def assemble_kernel(widths, *refs):
    blocks, outs, sems = refs[:8], refs[8:-1], refs[-1]
    z, y, x, core = position()
    rows = blocks[0].shape[1]
    copies = []
    for other in range(2):
        for step, (i, j) in enumerate(CHIP_STEPS):
            block = blocks[other * 4 + step]
            for k in range(4):
                row = (((z ^ k) * 2 + (y ^ j)) * 2 + (core ^ other)) * rows
                left = 0
                for width, out in zip(widths, outs):
                    copies.append(
                        pltpu.make_async_copy(
                            block.at[k, :, pl.ds(left, width)],
                            out.at[
                                pl.ds(pl.multiple_of(row, rows), rows),
                                pl.ds(pl.multiple_of((x ^ i) * width, width), width),
                            ],
                            sems.at[len(copies)],
                        )
                    )
                    left += width
    for copy in copies:
        copy.start()
    for copy in copies:
        copy.wait()


def assemble(blocks, widths, name):
    rows = blocks[0].shape[1] * 16
    return pl.pallas_call(
        functools.partial(assemble_kernel, widths),
        out_shape=[jax.ShapeDtypeStruct((rows, 2 * w), blocks[0].dtype) for w in widths],
        in_specs=[pl.BlockSpec(memory_space=pl.ANY)] * 8,
        out_specs=[pl.BlockSpec(memory_space=pl.ANY)] * len(widths),
        scratch_shapes=[pltpu.SemaphoreType.DMA((32 * len(widths),))],
        name=name,
    )(*blocks)


def gather_vectors(vectors):
    z, y, x, core = position()
    lines = gather_z(vectors)
    blocks = gather_cores(gather_chips(lines))
    table = jnp.stack(blocks).reshape(2, 2, 2, 4, -1)

    def turn(values, bit, axis):
        return jnp.where(bit == 1, jnp.flip(values, axis), values)

    table = turn(turn(turn(table, core, 0), y, 1), x, 2)
    table = table.reshape(2, 2, 2, 2, 2, -1)
    table = turn(turn(table, z // 2, 3), z % 2, 4)
    return table.transpose(3, 4, 1, 2, 0, 5).reshape(-1)


def split_kernel(place, full, kept, sent, sems):
    z, y, x, core = position()
    copies = []
    for other, out in ((0, kept), (1, sent)):
        for step, (i, j) in enumerate(CHIP_STEPS):
            for k in range(4):
                row, column = place((z ^ k) * 2 + (y ^ j), x ^ i, core ^ other)
                copies.append(
                    pltpu.make_async_copy(
                        full.at[
                            pl.ds(pl.multiple_of(row, 16), out.shape[2]),
                            pl.ds(pl.multiple_of(column, 128), out.shape[3]),
                        ],
                        out.at[step, k],
                        sems.at[len(copies)],
                    )
                )
    for copy in copies:
        copy.start()
    for copy in copies:
        copy.wait()


def split_up(full, shape, place, name):
    return pl.pallas_call(
        functools.partial(split_kernel, place),
        out_shape=[jax.ShapeDtypeStruct((4, 4) + shape, full.dtype)] * 2,
        in_specs=[pl.BlockSpec(memory_space=pl.ANY)],
        out_specs=[pl.BlockSpec(memory_space=pl.ANY)] * 2,
        scratch_shapes=[pltpu.SemaphoreType.DMA((32,))],
        name=name,
    )(full)


def wide_sum(*terms):
    return functools.reduce(lambda a, b: a + b, [t.astype(jnp.float32) for t in terms])


def scatter_sum(full, shape, place, name):
    kept, sent = split_up(full, shape, place, name)
    received = send(sent, core=1)
    parts = [wide_sum(kept[s], received[s]).astype(full.dtype) for s in range(4)]
    others = [send(parts[s], x=i, y=j) for s, (i, j) in enumerate(CHIP_STEPS) if s]
    line = [
        wide_sum(parts[0][k], *[other[k] for other in others]).astype(full.dtype) for k in range(4)
    ]
    others = [send(line[k], z=k) for k in (1, 2, 3)]
    return wide_sum(line[0], *others)


def row_halves(rows, columns):
    def place(wide, x, core):
        return (wide * 2 + core) * rows, x * columns

    return place


def swap_columns(summed):
    core = lax.axis_index("narrow") % 2
    columns = summed.shape[1] // 2
    left, right = summed[:, :columns], summed[:, columns:]
    mine = jnp.where(core == 0, left, right)
    other = send(jnp.where(core == 0, right, left).astype(jnp.bfloat16), core=1).astype(jnp.float32)
    return jnp.concatenate(
        [jnp.where(core == 0, mine, other), jnp.where(core == 0, other, mine)], 0
    )


def scatter_vectors(values):
    z, y, x, core = position()
    table = values.reshape(2, 2, 2, 2, 2, -1)

    def turn(values, bit, axis):
        return jnp.where(bit == 1, jnp.flip(values, axis), values)

    for axis, bit in enumerate((z // 2, z % 2, y, x, core)):
        table = turn(table, bit, axis)
    table = table.transpose(4, 3, 2, 0, 1, 5).reshape(2, 2, 2, 4, -1)
    table = table[0] + send(table[1], core=1)
    total = table[0, 0]
    for i, j in CHIP_STEPS[1:]:
        total = total + send(table[i, j], x=i, y=j)
    own = total[0]
    for k in (1, 2, 3):
        own = own + send(total[k], z=k)
    return own


def split_vectors(vectors):
    return (
        vectors[0:D],
        vectors[D : 2 * D],
        vectors[2 * D : 3 * D],
        vectors[3 * D : 4 * D],
        vectors[4 * D : 5 * D],
        vectors[5 * D : 5 * D + FF],
        vectors[5 * D + FF : 6 * D + FF],
        vectors[6 * D + FF : 7 * D + FF],
        vectors[7 * D + FF : 8 * D + FF],
    )


def normalize(values):
    center = values - jnp.mean(values, -1, keepdims=True)
    inverse = lax.rsqrt(jnp.mean(center * center, -1, keepdims=True) + epsilon)
    return (center * inverse, inverse)


def normalize_back(grad_norm, normed, inverse):
    return inverse * (
        grad_norm
        - jnp.mean(grad_norm, -1, keepdims=True)
        - normed * jnp.mean(grad_norm * normed, -1, keepdims=True)
    )


def contract_rows(left_side, right_side):
    return lax.dot_general(
        left_side, right_side, (((0,), (0,)), ((), ())), preferred_element_type=jnp.float32
    ).astype(jnp.bfloat16)


def contract_cols(left_side, right_side):
    return lax.dot_general(
        left_side, right_side, (((1,), (1,)), ((), ())), preferred_element_type=jnp.float32
    )


def smooth(values):
    return jax.nn.gelu(values, approximate=False)


def unpack(packed):
    length = packed.shape[0]
    head_dim = packed.shape[1] // (3 * HEADS)
    shaped = packed.reshape(length, 3, HEADS, head_dim)
    return (shaped[:, 0], shaped[:, 1], shaped[:, 2])


def masked_scores(queries, key_rows, segment_row):
    score_scale = queries.shape[-1] ** (-0.5)
    scores = (
        jnp.einsum("qhd,khd->hqk", queries, key_rows, preferred_element_type=jnp.float32)
        * score_scale
    )
    same_segment = segment_row[:, None] == segment_row[None, :]
    return jnp.where(same_segment[None], scores, -1000000000.0)


def attend(block_item):
    packed, segment_row = block_item
    queries, key_rows, value_rows = unpack(packed)
    scores = masked_scores(queries, key_rows, segment_row)
    largest = jnp.max(scores, -1, keepdims=True)
    weights = jnp.exp(scores - largest)
    totals = jnp.sum(weights, -1, keepdims=True)
    probs_low = (weights / totals).astype(jnp.bfloat16)
    attended = jnp.einsum("hqk,khd->qhd", probs_low, value_rows, preferred_element_type=jnp.float32)
    logsum = (largest + jnp.log(totals))[..., 0]
    return (attended.reshape(packed.shape[0], -1).astype(jnp.bfloat16), logsum)


def attend_back(block_item):
    packed, segment_row, logsum, grad_att = block_item
    queries, key_rows, value_rows = unpack(packed)
    score_scale = queries.shape[-1] ** (-0.5)
    scores = masked_scores(queries, key_rows, segment_row)
    probs = jnp.exp(scores - logsum[..., None])
    grad_heads = grad_att.reshape(queries.shape)
    grad_probs = jnp.einsum(
        "qhd,khd->hqk", grad_heads, value_rows, preferred_element_type=jnp.float32
    )
    inner_sum = jnp.sum(probs * grad_probs, -1, keepdims=True)
    grad_scores = (probs * (grad_probs - inner_sum)).astype(jnp.bfloat16)
    grad_query = (
        jnp.einsum("hqk,khd->qhd", grad_scores, key_rows, preferred_element_type=jnp.float32)
        * score_scale
    )
    grad_key = (
        jnp.einsum("hqk,qhd->khd", grad_scores, queries, preferred_element_type=jnp.float32)
        * score_scale
    )
    grad_value = jnp.einsum(
        "hqk,qhd->khd", probs.astype(jnp.bfloat16), grad_heads, preferred_element_type=jnp.float32
    )
    return jnp.stack([grad_query, grad_key, grad_value], 1).reshape(packed.shape[0], -1)


def gather_all(trees, w_qkv, w_out, w_in, w_back, vectors):
    if not trees:

        def whole(piece):
            return lax.all_gather(
                lax.all_gather(piece, "narrow", axis=1, tiled=True), "wide", axis=0, tiled=True
            )

        full = tuple(whole(piece) for piece in (w_qkv, w_out, w_in, w_back))
        return full + (lax.all_gather(vectors, ALL, axis=0, tiled=True),)
    qkv, out, inner, back = pair_up(w_qkv, w_out, w_in, w_back)
    qkv_lines = gather_z(qkv)
    all_vectors = gather_vectors(vectors)
    qkv_lines, out, inner, back = lax.optimization_barrier((qkv_lines, out, inner, back))
    full_qkv = assemble(gather_cores(gather_chips(qkv_lines)), (1152,), "assemble_qkv")[0]
    mid_lines = gather_z(jnp.concatenate([inner, out], 1))
    back_lines = gather_z(back)
    mid = [mid_lines, send(mid_lines, x=1)]
    mid = mid + [send(block, y=1) for block in mid]
    full_in, full_out = assemble(gather_cores(mid), (1536, 384), "assemble_in")
    rear = [back_lines, send(back_lines, y=1)]
    rear = rear + [send(block, x=1) for block in rear]
    rear = [rear[0], rear[2], rear[1], rear[3]]
    full_back = assemble(gather_cores(rear), (384,), "assemble_back")[0]
    return full_qkv, full_out, full_in, full_back, all_vectors


def per_device(trees, hidden, segment, w_qkv, w_out, w_in, w_back, vectors, cotangent):
    full_qkv, full_out, full_in, full_back, all_vectors = gather_all(
        trees, w_qkv, w_out, w_in, w_back, vectors
    )
    (
        bias_query,
        bias_value,
        bias_out,
        gain_first,
        shift_first,
        bias_inner,
        bias_back,
        gain_second,
        shift_second,
    ) = split_vectors(all_vectors)
    rows_dev = segment.shape[0]
    length = segment.shape[1]
    projected = jnp.dot(hidden, full_qkv, preferred_element_type=jnp.float32)
    qkv_bias = jnp.concatenate([bias_query, jnp.zeros((D,), jnp.float32), bias_value])
    packed = (projected + qkv_bias).astype(jnp.bfloat16)
    packed_rows = packed.reshape(rows_dev, length, 3 * D)
    attended, logsum = lax.map(attend, (packed_rows, segment))
    attended = attended.reshape(rows_dev * length, D)
    branch = jnp.dot(attended, full_out, preferred_element_type=jnp.float32) + bias_out
    first_normed, first_inverse = normalize(hidden.astype(jnp.float32) + branch)
    first_out = first_normed * gain_first + shift_first
    first_low = first_out.astype(jnp.bfloat16)
    inner_act = jnp.dot(first_low, full_in, preferred_element_type=jnp.float32) + bias_inner
    activated, gelu_back = jax.vjp(smooth, inner_act)
    activated_low = activated.astype(jnp.bfloat16)
    outward = jnp.dot(activated_low, full_back, preferred_element_type=jnp.float32) + bias_back
    second_normed, second_inverse = normalize(first_out + outward)
    output = (second_normed * gain_second + shift_second).astype(jnp.bfloat16)
    grad_output = cotangent.astype(jnp.float32)
    grad_gain_second = jnp.sum(grad_output * second_normed, 0)
    grad_shift_second = jnp.sum(grad_output, 0)
    grad_second = normalize_back(grad_output * gain_second, second_normed, second_inverse)
    grad_bias_back = jnp.sum(grad_second, 0)
    second_low = grad_second.astype(jnp.bfloat16)
    grad_w_back = contract_rows(second_low, activated_low)
    grad_activated = contract_cols(second_low, full_back)
    grad_inner = gelu_back(grad_activated)[0]
    grad_bias_inner = jnp.sum(grad_inner, 0)
    inner_low = grad_inner.astype(jnp.bfloat16)
    grad_w_in = contract_rows(first_low, inner_low)
    grad_first = grad_second + contract_cols(inner_low, full_in)
    grad_gain_first = jnp.sum(grad_first * first_normed, 0)
    grad_shift_first = jnp.sum(grad_first, 0)
    grad_branch = normalize_back(grad_first * gain_first, first_normed, first_inverse)
    grad_bias_out = jnp.sum(grad_branch, 0)
    branch_low = grad_branch.astype(jnp.bfloat16)
    grad_w_out = contract_rows(attended, branch_low)
    grad_att = contract_cols(branch_low, full_out).astype(jnp.bfloat16)
    grad_packed = lax.map(
        attend_back, (packed_rows, segment, logsum, grad_att.reshape(rows_dev, length, D))
    )
    grad_packed = grad_packed.reshape(rows_dev * length, 3 * D)
    grad_bias_query = jnp.sum(grad_packed[:, :D], 0)
    grad_bias_value = jnp.sum(grad_packed[:, 2 * D :], 0)
    packed_low = grad_packed.astype(jnp.bfloat16)
    grad_w_qkv = contract_rows(hidden, packed_low)
    grad_hidden = grad_branch + contract_cols(packed_low, full_qkv)
    grad_all_vectors = jnp.concatenate(
        [
            grad_bias_query,
            grad_bias_value,
            grad_bias_out,
            grad_gain_first,
            grad_shift_first,
            grad_bias_inner,
            grad_bias_back,
            grad_gain_second,
            grad_shift_second,
        ]
    )
    if trees:
        own_back = scatter_sum(
            grad_w_back, (192, 384), lambda wide, x, core: (x * 384 + core * 192, wide * 384), "split_back"
        ).T
        own_in = scatter_sum(
            grad_w_in, (96, 768), lambda wide, x, core: (wide * 96, x * 1536 + core * 768), "split_in"
        )
        own_out = swap_columns(scatter_sum(grad_w_out, (48, 384), row_halves(48, 384), "split_out"))
        own_qkv = swap_columns(
            scatter_sum(grad_w_qkv, (48, 1152), row_halves(48, 1152), "split_qkv")
        )
        own_vectors = scatter_vectors(grad_all_vectors)
    else:

        def own(values):
            part = lax.psum_scatter(values, "wide", scatter_dimension=0, tiled=True)
            part = lax.psum_scatter(part, "narrow", scatter_dimension=1, tiled=True)
            return part.astype(jnp.float32)

        own_qkv, own_out, own_in = own(grad_w_qkv), own(grad_w_out), own(grad_w_in)
        own_back = own(grad_w_back.T)
        own_vectors = lax.psum_scatter(grad_all_vectors, ALL, scatter_dimension=0, tiled=True)
    return (output, grad_hidden, own_qkv, own_out, own_in, own_back, own_vectors)


def solution(mesh):
    trees = mesh.shape["wide"] == 8 and mesh.shape["narrow"] == 4
    return jax.shard_map(
        functools.partial(per_device, trees),
        mesh=mesh,
        in_specs=(
            P(ALL, None),
            P(ALL, None),
            P("wide", "narrow"),
            P("wide", "narrow"),
            P("wide", "narrow"),
            P("wide", "narrow"),
            P(ALL),
            P(ALL, None),
        ),
        out_specs=(
            P(ALL, None),
            P(ALL, None),
            P("wide", "narrow"),
            P("wide", "narrow"),
            P("wide", "narrow"),
            P("wide", "narrow"),
            P(ALL),
        ),
        check_vma=False,
    )
```

```python
import functools

import jax
import jax.numpy as jnp
from jax import lax
from jax.experimental import pallas as pl
from jax.experimental.pallas import tpu as pltpu
from jax.sharding import PartitionSpec as P

D = 768
HEADS = 12
FF = 3072
TILE = 256
ALL = ("wide", "narrow")
CHIP_STEPS = ((0, 0), (1, 0), (0, 1), (1, 1))
VMEM_LIMIT = 60 * 2**20
bf16, f32 = jnp.bfloat16, jnp.float32
Shape = jax.ShapeDtypeStruct

epsilon = 1e-06


def cost(us):
    return pl.CostEstimate(flops=int(us * 1.15e9), bytes_accessed=0, transcendentals=0)


def params():
    return pltpu.CompilerParams(vmem_limit_bytes=VMEM_LIMIT)


def send(values, z=0, y=0, x=0, core=0):
    flip_wide, flip_narrow = 2 * z + y, 2 * x + core
    pairs = [
        (w * 4 + n, (w ^ flip_wide) * 4 + (n ^ flip_narrow)) for w in range(8) for n in range(4)
    ]
    return lax.ppermute(values, ALL, pairs)


def position():
    wide, narrow = lax.axis_index("wide"), lax.axis_index("narrow")
    return wide // 2, wide % 2, narrow // 2, narrow % 2


def origin():
    zero = jnp.int32(0)
    return zero, zero, zero, zero


def gather_z(values):
    return jnp.stack([values] + [send(values, z=k) for k in (1, 2, 3)])


def gather_chips(lines):
    return [lines] + [send(lines, x=i, y=j) for i, j in CHIP_STEPS[1:]]


def gather_cores(blocks):
    return blocks + [send(block, core=1) for block in blocks]


def pair_kernel(*refs):
    count = len(refs) // 3
    core = lax.rem(lax.axis_index("narrow"), 2)
    for own, other, out in zip(refs[:count], refs[count : 2 * count], refs[2 * count :]):
        rows, columns = own.shape[0] // 2, own.shape[1]
        half = pl.ds(pl.multiple_of(core * rows, rows), rows)

        @pl.when(core == 0)
        def _(own=own, other=other, out=out, half=half, columns=columns):
            out[:, :columns] = own[half, :]
            out[:, columns:] = other[half, :]

        @pl.when(core == 1)
        def _(own=own, other=other, out=out, half=half, columns=columns):
            out[:, :columns] = other[half, :]
            out[:, columns:] = own[half, :]


def pair_up(*pieces):
    others = [send(piece, core=1) for piece in pieces]
    return pl.pallas_call(
        pair_kernel,
        out_shape=[
            Shape((piece.shape[0] // 2, piece.shape[1] * 2), piece.dtype) for piece in pieces
        ],
        cost_estimate=cost(2),
        name="pair_up",
    )(*pieces, *others)


def assemble_kernel(widths, *refs):
    blocks, outs, sems = refs[:8], refs[8:-1], refs[-1]
    z, y, x, core = position()
    rows = blocks[0].shape[1]
    copies = []
    for other in range(2):
        for step, (i, j) in enumerate(CHIP_STEPS):
            block = blocks[other * 4 + step]
            for k in range(4):
                row = (((z ^ k) * 2 + (y ^ j)) * 2 + (core ^ other)) * rows
                left = 0
                for width, out in zip(widths, outs):
                    copies.append(
                        pltpu.make_async_copy(
                            block.at[k, :, pl.ds(left, width)],
                            out.at[
                                pl.ds(pl.multiple_of(row, rows), rows),
                                pl.ds(pl.multiple_of((x ^ i) * width, width), width),
                            ],
                            sems.at[len(copies)],
                        )
                    )
                    left += width
    for copy in copies:
        copy.start()
    for copy in copies:
        copy.wait()


def assemble(blocks, widths, name):
    rows = blocks[0].shape[1] * 16
    return pl.pallas_call(
        functools.partial(assemble_kernel, widths),
        out_shape=[Shape((rows, 2 * w), blocks[0].dtype) for w in widths],
        in_specs=[pl.BlockSpec(memory_space=pl.ANY)] * 8,
        out_specs=[pl.BlockSpec(memory_space=pltpu.VMEM)] * len(widths),
        scratch_shapes=[pltpu.SemaphoreType.DMA((32 * len(widths),))],
        compiler_params=params(),
        cost_estimate=cost(4),
        name=name,
    )(*blocks)


def place_kernel(*refs):
    z, y, x, core = position()
    out = refs[8]
    for other in range(2):
        for step, (i, j) in enumerate(CHIP_STEPS):
            for k in range(4):
                row = ((z ^ k) * 2 + (y ^ j)) * 4 + (x ^ i) * 2 + (core ^ other)
                out[pl.ds(row, 1), :] = refs[other * 4 + step][k : k + 1, :]


def gather_vectors(vectors):
    piece = vectors.reshape(1, -1)
    lines = jnp.concatenate([piece] + [send(piece, z=k) for k in (1, 2, 3)])
    blocks = gather_cores(gather_chips(lines))
    table = pl.pallas_call(
        place_kernel,
        out_shape=Shape((32, vectors.shape[0]), f32),
        cost_estimate=cost(1),
        name="place_vectors",
    )(*blocks)
    return table.reshape(12, D)


def order_kernel(table, kept, sent):
    z, y, x, core = position()
    for other, out in ((0, kept), (1, sent)):
        for step, (i, j) in enumerate(CHIP_STEPS):
            for k in range(4):
                row = ((z ^ k) * 2 + (y ^ j)) * 4 + (x ^ i) * 2 + (core ^ other)
                out[step, k : k + 1, :] = table[pl.ds(row, 1), :]


def scatter_vectors(values):
    table = values.reshape(32, -1)
    width = table.shape[1]
    kept, sent = pl.pallas_call(
        order_kernel,
        out_shape=[Shape((4, 4, width), f32)] * 2,
        cost_estimate=cost(1),
        name="order_vectors",
    )(table)
    return scatter_sum(kept, sent).reshape(-1)


def wide_sum(*terms):
    return functools.reduce(lambda a, b: a + b, [t.astype(f32) for t in terms])


def scatter_sum(kept, sent):
    received = send(sent, core=1)
    parts = [wide_sum(kept[s], received[s]).astype(kept.dtype) for s in range(4)]
    others = [send(parts[s], x=i, y=j) for s, (i, j) in enumerate(CHIP_STEPS) if s]
    line = [
        wide_sum(parts[0][k], *[other[k] for other in others]).astype(kept.dtype)
        for k in range(4)
    ]
    others = [send(line[k], z=k) for k in (1, 2, 3)]
    return wide_sum(line[0], *others)


def swap_columns(summed):
    core = lax.axis_index("narrow") % 2
    columns = summed.shape[1] // 2
    left, right = summed[:, :columns], summed[:, columns:]
    mine = jnp.where(core == 0, left, right)
    other = send(jnp.where(core == 0, right, left).astype(bf16), core=1).astype(f32)
    return jnp.concatenate(
        [jnp.where(core == 0, mine, other), jnp.where(core == 0, other, mine)], 0
    )


def dot(left_side, right_side):
    return jnp.dot(left_side, right_side, preferred_element_type=f32)


def dot_t(left_side, right_side):
    return lax.dot_general(
        left_side, right_side, (((1,), (1,)), ((), ())), preferred_element_type=f32
    )


def column_sum(values):
    return jnp.sum(values, 0, keepdims=True)


def normalize(values):
    center = values - jnp.mean(values, -1, keepdims=True)
    inverse = lax.rsqrt(jnp.mean(center * center, -1, keepdims=True) + epsilon)
    return center * inverse, inverse


def normalize_back(grad_norm, normed, inverse):
    return inverse * (
        grad_norm
        - jnp.mean(grad_norm, -1, keepdims=True)
        - normed * jnp.mean(grad_norm * normed, -1, keepdims=True)
    )


def smooth(values):
    density = jnp.exp(-0.5 * values * values) * 0.3989422804014327
    below = 0.5 + 0.5 * lax.erf(values * 0.7071067811865476)
    return values * below, below + values * density


def fixed(shape):
    return pl.BlockSpec(shape, lambda i: (0,) * len(shape))


def tile(columns, rows=TILE):
    return pl.BlockSpec((rows, columns), lambda i: (i, 0))


def rows_of(count, *parts):
    missing = count - sum(part.shape[0] for part in parts)
    return jnp.concatenate(list(parts) + [jnp.zeros((missing, parts[0].shape[1]), f32)], 0)


def segment_marks(segment):
    kinds = lax.broadcasted_iota(jnp.int32, (1, 64), 1)
    mark = (segment.reshape(-1, 1) == kinds).astype(bf16)
    tall = lax.broadcasted_iota(jnp.int32, (1, 64, 1), 1)
    away = (segment[:, None, :] != tall) & (tall < 4)
    return jnp.concatenate([mark, mark], 1), jnp.where(away, -(2.0**30), 0.0).astype(bf16)


def attend_kernel(hidden, weight, vectors, key_marks, query_marks, packed, att, att_t, probs):
    length = hidden.shape[0]
    for part in range(3):
        columns = slice(part * D, (part + 1) * D)
        block = dot(hidden[...], weight[:, columns])
        if part != 1:
            block = block + vectors[part // 2 : part // 2 + 1, :]
        block = block.astype(bf16)
        if part == 0:
            block = block * jnp.asarray(0.125, bf16)
        packed[:, columns] = block
    lanes = lax.broadcasted_iota(jnp.int32, (length, 128), 1)

    def pair(p, _):
        at = pl.multiple_of(p * 128, 128)
        q_t = packed[:, pl.ds(at, 128)].T
        k = packed[:, pl.ds(D + at, 128)]
        v_t = packed[:, pl.ds(2 * D + at, 128)].T
        scores = []
        for odd in range(2):
            keys = jnp.where((lanes >= 64) == bool(odd), k, key_marks[...])
            own = q_t[64 * odd : 64 * odd + 64]
            marks = query_marks[0]
            scores.append(dot(keys, jnp.concatenate([marks, own] if odd else [own, marks], 0)))
        outs = []
        for odd in range(2):
            weights = jnp.exp(scores[odd] - jnp.max(scores[odd], 0, keepdims=True))
            low = (weights * (1.0 / column_sum(weights))).astype(bf16)
            probs[p * 2 + odd] = low
            outs.append(dot(v_t[64 * odd : 64 * odd + 64], low))
        out = jnp.concatenate(outs, 0).astype(bf16)
        att_t[pl.ds(at, 128), :] = out
        att[:, pl.ds(at, 128)] = out.T
        return 0

    lax.fori_loop(0, HEADS // 2, pair, 0, unroll=True)


def attend(hidden, weight, vectors, key_marks, query_marks):
    rows, length = query_marks.shape[0], query_marks.shape[2]
    tokens = rows * length
    return pl.pallas_call(
        attend_kernel,
        grid=(rows,),
        in_specs=[
            tile(D, length),
            fixed((D, 3 * D)),
            fixed((12, D)),
            tile(128, length),
            pl.BlockSpec((1, 64, length), lambda i: (i, 0, 0)),
        ],
        out_specs=[
            tile(3 * D, length),
            tile(D, length),
            pl.BlockSpec((D, length), lambda i: (0, i)),
            pl.BlockSpec((HEADS, length, length), lambda i: (i, 0, 0)),
        ],
        out_shape=[
            Shape((tokens, 3 * D), bf16),
            Shape((tokens, D), bf16),
            Shape((D, tokens), bf16),
            Shape((rows * HEADS, length, length), bf16),
        ],
        compiler_params=params(),
        cost_estimate=cost(20),
        name="attend",
    )(hidden, weight, vectors, key_marks, query_marks)


def forward_kernel(place, *refs):
    att, hidden, cotangent, vectors, w_out, w_in, w_back = refs[:7]
    output, first_low, normed, inverse, grad_second, slope, sums, kept, sent = refs[7:16]
    activated, grad_t = refs[16:]
    step = pl.program_id(0)
    z, y, x, core = place()

    def row(i):
        return vectors[i : i + 1, :]

    here = pl.ds(pl.multiple_of(step * TILE, TILE), TILE)
    n1, r1 = normalize(hidden[...].astype(f32) + dot(att[...], w_out[...]) + row(2))
    first = n1 * row(3) + row(4)
    low = first.astype(bf16)
    first_low[...] = low
    normed[...] = n1
    inverse[...] = jnp.broadcast_to(r1, inverse.shape)
    outward = first + row(9)
    for c in range(FF // D):
        columns = slice(c * D, c * D + D)
        act, back = smooth(dot(low, w_in[:, columns]) + row(5 + c))
        act = act.astype(bf16)
        slope[:, columns] = back.astype(bf16)
        activated[here, columns] = act
        outward = outward + dot(act, w_back[columns, :])
    n2, r2 = normalize(outward)
    output[...] = (n2 * row(10) + row(11)).astype(bf16)
    cot = cotangent[...].astype(f32)
    g2 = normalize_back(cot * row(10), n2, r2)
    grad_second[...] = g2
    part = rows_of(8, column_sum(g2), column_sum(cot * n2), column_sum(cot))

    @pl.when(step == 0)
    def _():
        sums[...] = part

    @pl.when(step > 0)
    def _():
        sums[...] += part

    g2_t = g2.astype(bf16).T
    for i in range(2):
        for c in range(2):
            at = ((c ^ core) * 2 + (i ^ x)) * 192
            piece = (i * 2 + c) * 192
            grad_t[pl.ds(pl.multiple_of(at, 192), 192), here] = g2_t[piece : piece + 192]

    @pl.when(step == pl.num_programs(0) - 1)
    def _():
        for k in range(4):
            columns = pl.ds(pl.multiple_of((z ^ k) * D, D), D)
            res = dot(grad_t[...], activated[:, columns]).astype(bf16)
            for other, out in enumerate((kept, sent)):
                for i in range(2):
                    piece = res[(other * 2 + i) * 192 : (other * 2 + i) * 192 + 192]

                    @pl.when(y == 0)
                    def _(out=out, i=i, k=k, piece=piece):
                        out[i, k] = piece[:, :384]
                        out[2 + i, k] = piece[:, 384:]

                    @pl.when(y == 1)
                    def _(out=out, i=i, k=k, piece=piece):
                        out[2 + i, k] = piece[:, :384]
                        out[i, k] = piece[:, 384:]


def forward(place, att, hidden, cotangent, vectors, w_out, w_in, w_back):
    tokens = hidden.shape[0]
    return pl.pallas_call(
        functools.partial(forward_kernel, place),
        grid=(tokens // TILE,),
        in_specs=[tile(D)] * 3 + [fixed((12, D)), fixed((D, D)), fixed((D, FF)), fixed((FF, D))],
        out_specs=[tile(D), tile(D), tile(D), tile(128), tile(D), tile(FF), fixed((8, D))]
        + [fixed((4, 4, 192, 384))] * 2,
        out_shape=[
            Shape((tokens, D), bf16),
            Shape((tokens, D), bf16),
            Shape((tokens, D), f32),
            Shape((tokens, 128), f32),
            Shape((tokens, D), f32),
            Shape((tokens, FF), bf16),
            Shape((8, D), f32),
        ]
        + [Shape((4, 4, 192, 384), bf16)] * 2,
        scratch_shapes=[pltpu.VMEM((tokens, FF), bf16), pltpu.VMEM((D, tokens), bf16)],
        compiler_params=params(),
        cost_estimate=cost(32),
        name="forward",
    )(att, hidden, cotangent, vectors, w_out, w_in, w_back)


def backward_kernel(place, *refs):
    grad_second, slope, normed, inverse, first_low, att_t, vectors, w_out, w_in, w_back = refs[:10]
    grad_att, grad_branch, sums, sums_inner, kept_in, sent_in, kept_out, sent_out = refs[10:18]
    inner_low, first_t, grad_low, turned = refs[18:]
    step = pl.program_id(0)
    z, y, x, core = place()
    here = pl.ds(pl.multiple_of(step * TILE, TILE), TILE)
    g2 = grad_second[...]
    g2_low = g2.astype(bf16)
    grad_first = g2
    inner_sums = []
    for c in range(FF // D):
        columns = slice(c * D, c * D + D)
        gi = dot_t(g2_low, w_back[columns, :]) * slope[:, columns].astype(f32)
        inner_sums.append(column_sum(gi))
        gi = gi.astype(bf16)
        inner_low[here, columns] = gi
        grad_first = grad_first + dot_t(gi, w_in[:, columns])
    n1 = normed[...]
    g1 = normalize_back(grad_first * vectors[3:4, :], n1, inverse[:, :1])
    grad_branch[...] = g1
    g1_low = g1.astype(bf16)
    grad_low[here, :] = g1_low
    grad_att[...] = dot_t(g1_low, w_out[...]).astype(bf16)
    part = rows_of(8, column_sum(g1), column_sum(grad_first * n1), column_sum(grad_first))
    part_inner = rows_of(8, *inner_sums)

    @pl.when(step == 0)
    def _():
        sums[...] = part
        sums_inner[...] = part_inner

    @pl.when(step > 0)
    def _():
        sums[...] += part
        sums_inner[...] += part_inner

    low_t = first_low[...].T
    for w in range(8):
        at = ((w % 2) ^ y) * 4 + ((w // 2) ^ z)
        first_t[pl.ds(pl.multiple_of(at * 96, 96), 96), here] = low_t[w * 96 : w * 96 + 96]

    @pl.when(step == pl.num_programs(0) - 1)
    def _():
        for i in range(2):
            for other, out in enumerate((kept_in, sent_in)):
                at = ((x ^ i) * 2 + (core ^ other)) * D
                res = dot(first_t[...], inner_low[:, pl.ds(pl.multiple_of(at, D), D)])
                res = res.astype(bf16)
                for j in range(2):
                    for k in range(4):
                        out[i + 2 * j, k] = res[(j * 4 + k) * 96 : (j * 4 + k) * 96 + 96]
        turn_rows(place, att_t, turned)
        res = dot(turned[...], grad_low[...]).astype(bf16)
        for other, out in enumerate((kept_out, sent_out)):
            for j in range(2):
                for k in range(4):
                    at = (other * 8 + j * 4 + k) * 48
                    piece = res[at : at + 48]

                    @pl.when(x == 0)
                    def _(out=out, j=j, k=k, piece=piece):
                        out[2 * j, k] = piece[:, :384]
                        out[1 + 2 * j, k] = piece[:, 384:]

                    @pl.when(x == 1)
                    def _(out=out, j=j, k=k, piece=piece):
                        out[1 + 2 * j, k] = piece[:, :384]
                        out[2 * j, k] = piece[:, 384:]


def turn_rows(place, source, turned):
    z, y, _, core = place()
    for w in range(8):
        for half in range(2):
            at = (half ^ core) * 8 + ((w % 2) ^ y) * 4 + ((w // 2) ^ z)
            piece = (w * 2 + half) * 48
            turned[pl.ds(pl.multiple_of(at * 48, 48), 48), :] = source[piece : piece + 48, :]


def backward(place, grad_second, slope, normed, inverse, first_low, att_t, vectors, *weights):
    tokens = normed.shape[0]
    outs = [(4, 4, 96, D)] * 2 + [(4, 4, 48, 384)] * 2
    return pl.pallas_call(
        functools.partial(backward_kernel, place),
        grid=(tokens // TILE,),
        in_specs=[tile(D), tile(FF), tile(D), tile(128), tile(D)]
        + [fixed(s) for s in ((D, tokens), (12, D), (D, D), (D, FF), (FF, D))],
        out_specs=[tile(D), tile(D)] + [fixed(s) for s in [(8, D)] * 2 + outs],
        out_shape=[Shape((tokens, D), bf16), Shape((tokens, D), f32)]
        + [Shape((8, D), f32)] * 2
        + [Shape(s, bf16) for s in outs],
        scratch_shapes=[
            pltpu.VMEM((tokens, FF), bf16),
            pltpu.VMEM((D, tokens), bf16),
            pltpu.VMEM((tokens, D), bf16),
            pltpu.VMEM((D, tokens), bf16),
        ],
        compiler_params=params(),
        cost_estimate=cost(30),
        name="backward",
    )(grad_second, slope, normed, inverse, first_low, att_t, vectors, *weights)


def attend_back_kernel(packed, grad_att, probs, grad_low, sums):
    length = packed.shape[0]
    lanes = lax.broadcasted_iota(jnp.int32, (length, 128), 1)
    zero = jnp.zeros((length, 128), bf16)
    blank = jnp.zeros((64, length), bf16)

    def pair(p, _):
        at = pl.multiple_of(p * 128, 128)
        q = packed[:, pl.ds(at, 128)]
        k_t = packed[:, pl.ds(D + at, 128)].T
        v = packed[:, pl.ds(2 * D + at, 128)]
        g = grad_att[:, pl.ds(at, 128)]
        g_t = g.T
        grad_probs = []
        for odd in range(2):
            own = g_t[64 * odd : 64 * odd + 64]
            grad_probs.append(dot(v, jnp.concatenate([blank, own] if odd else [own, blank], 0)))
        dk = dv = 0.0
        dq_t = []
        for odd in range(2):
            mine = (lanes >= 64) == bool(odd)
            low = probs[p * 2 + odd]
            wide = low.astype(f32)
            gp = grad_probs[odd]
            ds = (wide * (gp - column_sum(wide * gp))).astype(bf16)
            dv = dv + dot(low, jnp.where(mine, g, zero))
            dk = dk + dot(ds, jnp.where(mine, q, zero))
            dq_t.append(dot(k_t[64 * odd : 64 * odd + 64], ds))
        dq = jnp.concatenate(dq_t, 0).T * 0.125
        sums[0, :, pl.ds(at, 128)] = rows_of(8, column_sum(dq), column_sum(dv))
        grad_low[:, pl.ds(at, 128)] = dq.astype(bf16)
        grad_low[:, pl.ds(D + at, 128)] = dk.astype(bf16)
        grad_low[:, pl.ds(2 * D + at, 128)] = dv.astype(bf16)
        return 0

    lax.fori_loop(0, HEADS // 2, pair, 0, unroll=True)


def attend_back(packed, grad_att, probs, rows):
    length = probs.shape[1]
    return pl.pallas_call(
        attend_back_kernel,
        grid=(rows,),
        in_specs=[
            tile(3 * D, length),
            tile(D, length),
            pl.BlockSpec((HEADS, length, length), lambda i: (i, 0, 0)),
        ],
        out_specs=[tile(3 * D, length), pl.BlockSpec((1, 8, D), lambda i: (i, 0, 0))],
        out_shape=[Shape((rows * length, 3 * D), bf16), Shape((rows, 8, D), f32)],
        compiler_params=params(),
        cost_estimate=cost(21),
        name="attend_back",
    )(packed, grad_att, probs)


def grad_qkv_kernel(place, hidden, low, kept, sent, turned):
    _, _, x, _ = place()
    turn_rows(place, hidden[...].T, turned)
    for i in range(2):
        columns = pl.ds(pl.multiple_of((x ^ i) * 1152, 128), 1152)
        res = dot(turned[...], low[:, columns]).astype(bf16)
        for other, out in enumerate((kept, sent)):
            for j in range(2):
                for k in range(4):
                    at = (other * 8 + j * 4 + k) * 48
                    out[i + 2 * j, k] = res[at : at + 48]


def grad_qkv(place, hidden, low):
    return pl.pallas_call(
        functools.partial(grad_qkv_kernel, place),
        out_shape=[Shape((4, 4, 48, 1152), bf16)] * 2,
        scratch_shapes=[pltpu.VMEM((D, hidden.shape[0]), bf16)],
        compiler_params=params(),
        cost_estimate=cost(9),
        name="grad_qkv",
    )(hidden, low)


def hidden_kernel(low, weight, grad_branch, out):
    out[...] = grad_branch[...] + dot_t(low[...], weight[...])


def grad_of_hidden(low, weight, grad_branch):
    tokens = low.shape[0]
    return pl.pallas_call(
        hidden_kernel,
        grid=(tokens // TILE,),
        in_specs=[tile(3 * D), fixed((D, 3 * D)), tile(D)],
        out_specs=tile(D),
        out_shape=Shape((tokens, D), f32),
        compiler_params=params(),
        cost_estimate=cost(9),
        name="grad_hidden",
    )(low, weight, grad_branch)


def gather_all(trees, w_qkv, w_out, w_in, w_back, vectors):
    if not trees:

        def whole(piece):
            return lax.all_gather(
                lax.all_gather(piece, "narrow", axis=1, tiled=True), "wide", axis=0, tiled=True
            )

        full = tuple(whole(piece) for piece in (w_qkv, w_out, w_in, w_back))
        return full + (lax.all_gather(vectors, ALL, axis=0, tiled=True).reshape(12, D),)
    qkv, out, inner, back = pair_up(w_qkv, w_out, w_in, w_back)
    qkv_lines = gather_z(qkv)
    all_vectors = gather_vectors(vectors)
    qkv_lines, out, inner, back = lax.optimization_barrier((qkv_lines, out, inner, back))
    full_qkv = assemble(gather_cores(gather_chips(qkv_lines)), (1152,), "assemble_qkv")[0]
    mid_lines = gather_z(jnp.concatenate([inner, out], 1))
    back_lines = gather_z(back)
    mid = [mid_lines, send(mid_lines, x=1)]
    mid = mid + [send(block, y=1) for block in mid]
    full_in, full_out = assemble(gather_cores(mid), (1536, 384), "assemble_in")
    rear = [back_lines, send(back_lines, y=1)]
    rear = rear + [send(block, x=1) for block in rear]
    rear = [rear[0], rear[2], rear[1], rear[3]]
    full_back = assemble(gather_cores(rear), (384,), "assemble_back")[0]
    return full_qkv, full_out, full_in, full_back, all_vectors


def unfold(table, order, shape):
    kept, sent = table
    full = jnp.stack([kept, sent]).reshape((2, 2, 2, 4) + kept.shape[2:])
    return full.transpose(order).reshape(shape)


def scatter_whole(matrix):
    part = lax.psum_scatter(matrix, "wide", scatter_dimension=0, tiled=True)
    part = lax.psum_scatter(part, "narrow", scatter_dimension=1, tiled=True)
    return part.astype(f32)


def per_device(trees, hidden, segment, w_qkv, w_out, w_in, w_back, vectors, cotangent):
    place = position if trees else origin
    rows_dev = segment.shape[0]
    key_marks, query_marks = segment_marks(segment)
    full_qkv, full_out, full_in, full_back, all_vectors = gather_all(
        trees, w_qkv, w_out, w_in, w_back, vectors
    )
    packed, att, att_t, probs = attend(hidden, full_qkv, all_vectors, key_marks, query_marks)
    output, first_low, normed, inverse, grad_second, slope, sums_second, kept, sent = forward(
        place, att, hidden, cotangent, all_vectors, full_out, full_in, full_back
    )
    back_table = (kept, sent)
    grad_att, grad_branch, sums_first, sums_inner, kept, sent, kept_out, sent_out = backward(
        place,
        grad_second,
        slope,
        normed,
        inverse,
        first_low,
        att_t,
        all_vectors,
        full_out,
        full_in,
        full_back,
    )
    in_table, out_table = (kept, sent), (kept_out, sent_out)
    packed_low, sums_packed = attend_back(packed, grad_att, probs, rows_dev)
    qkv_table = grad_qkv(place, hidden, packed_low)
    grad_hidden = grad_of_hidden(packed_low, full_qkv, grad_branch)
    sums_packed = jnp.sum(sums_packed, 0)
    grad_vectors = jnp.concatenate(
        [sums_packed[:2], sums_first[:3], sums_inner[:4], sums_second[:3]], 0
    )
    if trees:
        own_back = scatter_sum(*back_table).T
        own_in = scatter_sum(*in_table)
        own_out = swap_columns(scatter_sum(*out_table))
        own_qkv = swap_columns(scatter_sum(*qkv_table))
        own_vectors = scatter_vectors(grad_vectors)
    else:
        own_qkv = scatter_whole(unfold(qkv_table, (3, 1, 0, 4, 2, 5), (D, 3 * D)))
        own_out = scatter_whole(unfold(out_table, (3, 1, 0, 4, 2, 5), (D, D)))
        own_in = scatter_whole(unfold(in_table, (3, 1, 4, 2, 0, 5), (D, FF)))
        own_back = scatter_whole(unfold(back_table, (2, 0, 4, 3, 1, 5), (D, FF)).T)
        own_vectors = lax.psum_scatter(
            grad_vectors.reshape(-1), ALL, scatter_dimension=0, tiled=True
        )
    return (output, grad_hidden, own_qkv, own_out, own_in, own_back, own_vectors)


def solution(mesh):
    trees = mesh.shape["wide"] == 8 and mesh.shape["narrow"] == 4
    return jax.shard_map(
        functools.partial(per_device, trees),
        mesh=mesh,
        in_specs=(P(ALL, None),) * 2 + (P("wide", "narrow"),) * 4 + (P(ALL), P(ALL, None)),
        out_specs=(P(ALL, None),) * 2 + (P("wide", "narrow"),) * 4 + (P(ALL),),
        check_vma=False,
    )
```

```python
import functools

import jax
import jax.numpy as jnp
from jax import lax
from jax.experimental import pallas as pl
from jax.experimental.pallas import tpu as pltpu
from jax.sharding import PartitionSpec as P

D = 768
HEADS = 12
FF = 3072
TILE = 256
ALL = ("wide", "narrow")
CHIP_STEPS = ((0, 0), (1, 0), (0, 1), (1, 1))
VMEM_LIMIT = 60 * 2**20
bf16, f32 = jnp.bfloat16, jnp.float32
Shape = jax.ShapeDtypeStruct

epsilon = 1e-06


def cost(us):
    return pl.CostEstimate(flops=0 * us, bytes_accessed=0, transcendentals=0)


def params():
    return pltpu.CompilerParams(vmem_limit_bytes=VMEM_LIMIT)


def send(values, z=0, y=0, x=0, core=0):
    flip_wide, flip_narrow = 2 * z + y, 2 * x + core
    pairs = [
        (w * 4 + n, (w ^ flip_wide) * 4 + (n ^ flip_narrow)) for w in range(8) for n in range(4)
    ]
    return lax.ppermute(values, ALL, pairs)


def position():
    wide, narrow = lax.axis_index("wide"), lax.axis_index("narrow")
    return wide // 2, wide % 2, narrow // 2, narrow % 2


def origin():
    zero = jnp.int32(0)
    return zero, zero, zero, zero


def gather_z(values):
    return [values] + [send(values, z=k) for k in (1, 2, 3)]


def gather_chips(lines):
    return [lines] + [send(lines, x=i, y=j) for i, j in CHIP_STEPS[1:]]


def gather_cores(blocks):
    return blocks + [send(block, core=1) for block in blocks]


def pair_kernel(count, *refs):
    core = lax.rem(lax.axis_index("narrow"), 2)
    more, outs = refs[2 * count : -count], refs[-count:]
    for own, other, out in zip(refs[:count], refs[count : 2 * count], outs):
        rows, columns = own.shape[0] // 2, own.shape[1]
        half = pl.ds(pl.multiple_of(core * rows, rows), rows)

        @pl.when(core == 0)
        def _(own=own, other=other, out=out, half=half, columns=columns):
            out[:, :columns] = own[half, :]
            out[:, columns : 2 * columns] = other[half, :]

        @pl.when(core == 1)
        def _(own=own, other=other, out=out, half=half, columns=columns):
            out[:, :columns] = other[half, :]
            out[:, columns : 2 * columns] = own[half, :]

    for vector in more:
        rest, parts = vector[...], []
        for _ in range(3):
            parts.append(rest.astype(bf16).astype(f32))
            rest = rest - parts[-1]
        outs[0][:, 1152:] = rows_of(48, *parts).astype(bf16)


def pair_up(pieces, others, vectors=None):
    more = [0] * len(pieces)
    rows = ()
    if vectors is not None:
        rows = (jnp.pad(vectors, (0, 384 - vectors.shape[0])).reshape(3, 128),)
        more[0] = 128
    return pl.pallas_call(
        functools.partial(pair_kernel, len(pieces)),
        out_shape=[
            Shape((piece.shape[0] // 2, piece.shape[1] * 2 + extra), piece.dtype)
            for piece, extra in zip(pieces, more)
        ],
        cost_estimate=cost(2),
        name="pair_up",
    )(*pieces, *others, *rows)


def assemble_kernel(widths, *refs):
    blocks, outs, sems = refs[:8], refs[8:-1], refs[-1]
    z, y, x, core = position()
    rows = blocks[0].shape[1]
    copies = []
    for other in range(2):
        for step, (i, j) in enumerate(CHIP_STEPS):
            block = blocks[other * 4 + step]
            for k in range(4):
                row = (((z ^ k) * 2 + (y ^ j)) * 2 + (core ^ other)) * rows
                left = 0
                for width, out in zip(widths, outs):
                    copies.append(
                        pltpu.make_async_copy(
                            block.at[k, :, pl.ds(left, width)],
                            out.at[
                                pl.ds(pl.multiple_of(row, rows), rows),
                                pl.ds(pl.multiple_of((x ^ i) * width, width), width),
                            ],
                            sems.at[len(copies)],
                        )
                    )
                    left += width
    for copy in copies:
        copy.start()
    for copy in copies:
        copy.wait()


def assemble(blocks, widths, name):
    rows = blocks[0].shape[1] * 16
    return pl.pallas_call(
        functools.partial(assemble_kernel, widths),
        out_shape=[Shape((rows, 2 * w), blocks[0].dtype) for w in widths],
        in_specs=[pl.BlockSpec(memory_space=pl.ANY)] * 8,
        out_specs=[pl.BlockSpec(memory_space=pltpu.VMEM)] * len(widths),
        scratch_shapes=[pltpu.SemaphoreType.DMA((32 * len(widths),))],
        compiler_params=params(),
        cost_estimate=cost(4),
        name=name,
    )(*blocks)


def table_kernel(table, out, sems):
    rows, columns = table.shape[1:]
    copies = []
    for w in range(8):
        for n in range(4):
            at = (w * 2 + n % 2) * rows
            copies.append(
                pltpu.make_async_copy(
                    table.at[w * 4 + n],
                    out.at[pl.ds(at, rows), pl.ds(n // 2 * columns, columns)],
                    sems.at[len(copies)],
                )
            )
    for copy in copies:
        copy.start()
    for copy in copies:
        copy.wait()


def assemble_table(table, name):
    rows, columns = table.shape[1:]
    return pl.pallas_call(
        table_kernel,
        out_shape=Shape((16 * rows, 2 * columns), table.dtype),
        in_specs=[pl.BlockSpec(memory_space=pl.ANY)],
        out_specs=pl.BlockSpec(memory_space=pltpu.VMEM),
        scratch_shapes=[pltpu.SemaphoreType.DMA((32,))],
        compiler_params=params(),
        cost_estimate=cost(5),
        name=name,
    )(table)


def place_kernel(*refs):
    z, y, x, core = position()
    out = refs[8]
    for other in range(2):
        for step, (i, j) in enumerate(CHIP_STEPS):
            for k in range(4):
                row = ((z ^ k) * 2 + (y ^ j)) * 4 + (x ^ i) * 2 + (core ^ other)
                parts = refs[other * 4 + step][k].astype(f32)
                out[row] = parts[:3] + parts[3:6] + parts[6:9]


def place_vectors(blocks):
    table = pl.pallas_call(
        place_kernel,
        grid=(1,),
        in_specs=[pl.BlockSpec((4, 16, 128), lambda i: (0, 0, 9))] * 8,
        out_specs=fixed((32, 3, 128)),
        out_shape=Shape((32, 3, 128), f32),
        cost_estimate=cost(1),
        name="place_vectors",
    )(*blocks)
    return table.reshape(32, 384)[:, :288].reshape(12, D)


def wide_sum(*terms):
    return functools.reduce(lambda a, b: a + b, [t.astype(f32) for t in terms])


def chip_parts(kept, received):
    return [wide_sum(kept[s], received[s]).astype(kept.dtype) for s in range(4)]


def chip_sends(parts):
    return [send(parts[s], x=i, y=j) for s, (i, j) in enumerate(CHIP_STEPS) if s]


def line_parts(own, others):
    return [
        wide_sum(own[k], *[other[k] for other in others]).astype(own.dtype) for k in range(4)
    ]


def line_sends(line):
    return [send(line[k], z=k) for k in (1, 2, 3)]


def line_halves(own, others):
    parts = line_parts(own, others)
    return parts[:2], jnp.stack(parts[2:])


def near_parts(near, received):
    return [wide_sum(near[k], received[k]).astype(near[k].dtype) for k in range(2)]


def swap_columns(summed):
    core = lax.axis_index("narrow") % 2
    columns = summed.shape[1] // 2
    left, right = summed[:, :columns], summed[:, columns:]
    mine = jnp.where(core == 0, left, right)
    other = send(jnp.where(core == 0, right, left).astype(bf16), core=1).astype(f32)
    return jnp.concatenate(
        [jnp.where(core == 0, mine, other), jnp.where(core == 0, other, mine)], 0
    )


def dot(left_side, right_side):
    return jnp.dot(left_side, right_side, preferred_element_type=f32)


def dot_t(left_side, right_side):
    return lax.dot_general(
        left_side, right_side, (((1,), (1,)), ((), ())), preferred_element_type=f32
    )


def column_sum(values):
    return jnp.sum(values, 0, keepdims=True)


def normalize(values):
    center = values - jnp.mean(values, -1, keepdims=True)
    inverse = lax.rsqrt(jnp.mean(center * center, -1, keepdims=True) + epsilon)
    return center * inverse, inverse


def normalize_back(grad_norm, normed, inverse):
    return inverse * (
        grad_norm
        - jnp.mean(grad_norm, -1, keepdims=True)
        - normed * jnp.mean(grad_norm * normed, -1, keepdims=True)
    )


def smooth(values):
    density = jnp.exp(-0.5 * values * values) * 0.3989422804014327
    below = 0.5 + 0.5 * lax.erf(values * 0.7071067811865476)
    return values * below, below + values * density


def fixed(shape):
    return pl.BlockSpec(shape, lambda i: (0,) * len(shape))


def tile(columns, rows=TILE):
    return pl.BlockSpec((rows, columns), lambda i: (i, 0))


def rows_of(count, *parts):
    missing = count - sum(part.shape[0] for part in parts)
    return jnp.concatenate(list(parts) + [jnp.zeros((missing, parts[0].shape[1]), f32)], 0)


def segment_marks(segment):
    kinds = lax.broadcasted_iota(jnp.int32, (1, 64), 1)
    mark = (segment.reshape(-1, 1) == kinds).astype(bf16)
    tall = lax.broadcasted_iota(jnp.int32, (1, 64, 1), 1)
    away = (segment[:, None, :] != tall) & (tall < 4)
    return jnp.concatenate([mark, mark], 1), jnp.where(away, -(2.0**30), 0.0).astype(bf16)


def attend_kernel(hidden, weight, vectors, key_marks, query_marks, packed, att, att_t, probs):
    length = hidden.shape[0]
    for part in range(3):
        columns = slice(part * D, (part + 1) * D)
        block = dot(hidden[...], weight[:, columns])
        if part != 1:
            block = block + vectors[part // 2 : part // 2 + 1, :]
        block = block.astype(bf16)
        if part == 0:
            block = block * jnp.asarray(0.125, bf16)
        packed[:, columns] = block
    lanes = lax.broadcasted_iota(jnp.int32, (length, 128), 1)

    def pair(p, _):
        at = pl.multiple_of(p * 128, 128)
        q_t = packed[:, pl.ds(at, 128)].T
        k = packed[:, pl.ds(D + at, 128)]
        v_t = packed[:, pl.ds(2 * D + at, 128)].T
        scores = []
        for odd in range(2):
            keys = jnp.where((lanes >= 64) == bool(odd), k, key_marks[...])
            own = q_t[64 * odd : 64 * odd + 64]
            marks = query_marks[0]
            scores.append(dot(keys, jnp.concatenate([marks, own] if odd else [own, marks], 0)))
        outs = []
        for odd in range(2):
            weights = jnp.exp(scores[odd] - jnp.max(scores[odd], 0, keepdims=True))
            low = (weights * (1.0 / column_sum(weights))).astype(bf16)
            probs[p * 2 + odd] = low
            outs.append(dot(v_t[64 * odd : 64 * odd + 64], low))
        out = jnp.concatenate(outs, 0).astype(bf16)
        att_t[pl.ds(at, 128), :] = out
        att[:, pl.ds(at, 128)] = out.T
        return 0

    lax.fori_loop(0, HEADS // 2, pair, 0, unroll=True)


def attend(hidden, weight, vectors, key_marks, query_marks):
    rows, length = query_marks.shape[0], query_marks.shape[2]
    tokens = rows * length
    return pl.pallas_call(
        attend_kernel,
        grid=(rows,),
        in_specs=[
            tile(D, length),
            fixed((D, 3 * D)),
            fixed((12, D)),
            tile(128, length),
            pl.BlockSpec((1, 64, length), lambda i: (i, 0, 0)),
        ],
        out_specs=[
            tile(3 * D, length),
            tile(D, length),
            pl.BlockSpec((D, length), lambda i: (0, i)),
            pl.BlockSpec((HEADS, length, length), lambda i: (i, 0, 0)),
        ],
        out_shape=[
            Shape((tokens, 3 * D), bf16),
            Shape((tokens, D), bf16),
            Shape((D, tokens), bf16),
            Shape((rows * HEADS, length, length), bf16),
        ],
        compiler_params=params(),
        cost_estimate=cost(20),
        name="attend",
    )(hidden, weight, vectors, key_marks, query_marks)


def inner_kernel(att, hidden, vectors, w_out, w_in, first_low, normed, inverse, activated, slope):
    def row(i):
        return vectors[i : i + 1, :]

    n1, r1 = normalize(hidden[...].astype(f32) + dot(att[...], w_out[...]) + row(2))
    low = (n1 * row(3) + row(4)).astype(bf16)
    first_low[...] = low
    normed[...] = n1
    inverse[...] = jnp.broadcast_to(r1, inverse.shape)
    for c in range(FF // D):
        columns = slice(c * D, c * D + D)
        act, back = smooth(dot(low, w_in[:, columns]) + row(5 + c))
        activated[:, columns] = act.astype(bf16)
        slope[:, columns] = back.astype(bf16)


def inner_forward(att, hidden, vectors, w_out, w_in):
    tokens = hidden.shape[0]
    return pl.pallas_call(
        inner_kernel,
        grid=(tokens // TILE,),
        in_specs=[tile(D)] * 2 + [fixed((12, D)), fixed((D, D)), fixed((D, FF))],
        out_specs=[tile(D), tile(D), tile(128), tile(FF), tile(FF)],
        out_shape=[
            Shape((tokens, D), bf16),
            Shape((tokens, D), f32),
            Shape((tokens, 128), f32),
            Shape((tokens, FF), bf16),
            Shape((tokens, FF), bf16),
        ],
        compiler_params=params(),
        cost_estimate=cost(16),
        name="inner_forward",
    )(att, hidden, vectors, w_out, w_in)


def outer_kernel(place, *refs):
    act, normed, cotangent, vectors, w_back = refs[:5]
    output, grad_second, sums, kept, sent, activated, grad_t = refs[5:]
    step = pl.program_id(0)
    z, y, x, core = place()

    def row(i):
        return vectors[i : i + 1, :]

    here = pl.ds(pl.multiple_of(step * TILE, TILE), TILE)
    activated[here, :] = act[...]
    outward = normed[...] * row(3) + row(4) + dot(act[...], w_back[...]) + row(9)
    n2, r2 = normalize(outward)
    output[...] = (n2 * row(10) + row(11)).astype(bf16)
    cot = cotangent[...].astype(f32)
    g2 = normalize_back(cot * row(10), n2, r2)
    grad_second[...] = g2
    part = rows_of(8, column_sum(g2), column_sum(cot * n2), column_sum(cot))

    @pl.when(step == 0)
    def _():
        sums[...] = part

    @pl.when(step > 0)
    def _():
        sums[...] += part

    g2_t = g2.astype(bf16).T
    for n in range(4):
        at = ((n % 2) ^ core) * 2 + ((n // 2) ^ x)
        piece = g2_t[n * 192 : n * 192 + 192]
        grad_t[pl.ds(pl.multiple_of(at * 192, 192), 192), here] = piece

    @pl.when(step == pl.num_programs(0) - 1)
    def _():
        for k in range(4):
            columns = pl.ds(pl.multiple_of((z ^ k) * D, D), D)
            res = dot(grad_t[...], activated[:, columns]).astype(bf16)
            for other, out in enumerate((kept, sent)):
                for i in range(2):
                    at = (other * 2 + i) * 192
                    for half in range(2):
                        piece = res[at : at + 192, half * 384 : half * 384 + 384]
                        out[i + 2 * (half ^ y), k] = piece


def outer_forward(place, activated, normed, cotangent, vectors, w_back):
    tokens = normed.shape[0]
    return pl.pallas_call(
        functools.partial(outer_kernel, place),
        grid=(tokens // TILE,),
        in_specs=[tile(FF), tile(D), tile(D), fixed((12, D)), fixed((FF, D))],
        out_specs=[tile(D), tile(D), fixed((8, D))] + [fixed((4, 4, 192, 384))] * 2,
        out_shape=[
            Shape((tokens, D), bf16),
            Shape((tokens, D), f32),
            Shape((8, D), f32),
        ]
        + [Shape((4, 4, 192, 384), bf16)] * 2,
        scratch_shapes=[pltpu.VMEM((tokens, FF), bf16), pltpu.VMEM((D, tokens), bf16)],
        compiler_params=params(),
        cost_estimate=cost(18),
        name="outer_forward",
    )(activated, normed, cotangent, vectors, w_back)


def backward_kernel(*refs):
    grad_second, slope, normed, inverse, vectors, w_out, w_in, w_back = refs[:8]
    grad_att, grad_branch, grad_low, inner_low, sums, sums_inner = refs[8:]
    step = pl.program_id(0)
    g2 = grad_second[...]
    g2_low = g2.astype(bf16)
    grad_first = g2
    inner_sums = []
    for c in range(FF // D):
        columns = slice(c * D, c * D + D)
        gi = dot_t(g2_low, w_back[columns, :]) * slope[:, columns].astype(f32)
        inner_sums.append(column_sum(gi))
        gi = gi.astype(bf16)
        inner_low[:, columns] = gi
        grad_first = grad_first + dot_t(gi, w_in[:, columns])
    n1 = normed[...]
    g1 = normalize_back(grad_first * vectors[3:4, :], n1, inverse[:, :1])
    grad_branch[...] = g1
    g1_low = g1.astype(bf16)
    grad_low[...] = g1_low
    grad_att[...] = dot_t(g1_low, w_out[...]).astype(bf16)
    part = rows_of(8, column_sum(g1), column_sum(grad_first * n1), column_sum(grad_first))
    part_inner = rows_of(8, *inner_sums)

    @pl.when(step == 0)
    def _():
        sums[...] = part
        sums_inner[...] = part_inner

    @pl.when(step > 0)
    def _():
        sums[...] += part
        sums_inner[...] += part_inner


def backward(grad_second, slope, normed, inverse, vectors, *weights):
    tokens = normed.shape[0]
    return pl.pallas_call(
        backward_kernel,
        grid=(tokens // TILE,),
        in_specs=[tile(D), tile(FF), tile(D), tile(128)]
        + [fixed(s) for s in ((12, D), (D, D), (D, FF), (FF, D))],
        out_specs=[tile(D), tile(D), tile(D), tile(FF), fixed((8, D)), fixed((8, D))],
        out_shape=[
            Shape((tokens, D), bf16),
            Shape((tokens, D), f32),
            Shape((tokens, D), bf16),
            Shape((tokens, FF), bf16),
            Shape((8, D), f32),
            Shape((8, D), f32),
        ],
        compiler_params=params(),
        cost_estimate=cost(22),
        name="backward",
    )(grad_second, slope, normed, inverse, vectors, *weights)


def grad_in_kernel(place, first_low, inner_low, kept, sent, first_t):
    step = pl.program_id(0)
    z, y, x, core = place()

    @pl.when(step == 0)
    def _():
        low_t = first_low[...].T
        for w in range(8):
            at = ((w % 2) ^ y) * 4 + ((w // 2) ^ z)
            first_t[pl.ds(pl.multiple_of(at * 96, 96), 96), :] = low_t[w * 96 : w * 96 + 96]

    res = dot(first_t[...], inner_low[...]).astype(bf16)
    i = (step // 2) ^ x
    for other, out in enumerate((kept, sent)):

        @pl.when((step % 2) ^ core == other)
        def _(out=out):
            for j in range(2):
                for k in range(4):
                    out[i + 2 * j, k] = res[(j * 4 + k) * 96 : (j * 4 + k) * 96 + 96]


def grad_in(place, first_low, inner_low):
    tokens = first_low.shape[0]
    out = (4, 4, 96, D)
    return pl.pallas_call(
        functools.partial(grad_in_kernel, place),
        grid=(FF // D,),
        in_specs=[fixed((tokens, D)), pl.BlockSpec((tokens, D), lambda i: (0, i))],
        out_specs=[fixed(out)] * 2,
        out_shape=[Shape(out, bf16)] * 2,
        scratch_shapes=[pltpu.VMEM((D, tokens), bf16)],
        compiler_params=params(),
        cost_estimate=cost(10),
        name="grad_in",
    )(first_low, inner_low)


def grad_out_kernel(place, att_t, grad_low, kept, sent, turned):
    _, _, x, _ = place()
    turn_rows(place, att_t, turned)
    res = dot(turned[...], grad_low[...]).astype(bf16)
    for other, out in enumerate((kept, sent)):
        for j in range(2):
            for k in range(4):
                at = (other * 8 + j * 4 + k) * 48
                for half in range(2):
                    piece = res[at : at + 48, half * 384 : half * 384 + 384]
                    out[(half ^ x) + 2 * j, k] = piece


def grad_out(place, att_t, grad_low):
    tokens = grad_low.shape[0]
    return pl.pallas_call(
        functools.partial(grad_out_kernel, place),
        out_shape=[Shape((4, 4, 48, 384), bf16)] * 2,
        scratch_shapes=[pltpu.VMEM((D, tokens), bf16)],
        compiler_params=params(),
        cost_estimate=cost(3),
        name="grad_out",
    )(att_t, grad_low)


def turn_rows(place, source, turned):
    z, y, _, core = place()
    for w in range(8):
        for half in range(2):
            at = (half ^ core) * 8 + ((w % 2) ^ y) * 4 + ((w // 2) ^ z)
            piece = (w * 2 + half) * 48
            turned[pl.ds(pl.multiple_of(at * 48, 48), 48), :] = source[piece : piece + 48, :]


def attend_back_kernel(packed, grad_att, probs, grad_low, sums):
    length = packed.shape[0]
    lanes = lax.broadcasted_iota(jnp.int32, (length, 128), 1)
    zero = jnp.zeros((length, 128), bf16)
    blank = jnp.zeros((64, length), bf16)

    def pair(p, _):
        at = pl.multiple_of(p * 128, 128)
        q = packed[:, pl.ds(at, 128)]
        k_t = packed[:, pl.ds(D + at, 128)].T
        v = packed[:, pl.ds(2 * D + at, 128)]
        g = grad_att[:, pl.ds(at, 128)]
        g_t = g.T
        grad_probs = []
        for odd in range(2):
            own = g_t[64 * odd : 64 * odd + 64]
            grad_probs.append(dot(v, jnp.concatenate([blank, own] if odd else [own, blank], 0)))
        dk = dv = 0.0
        dq_t = []
        for odd in range(2):
            mine = (lanes >= 64) == bool(odd)
            low = probs[p * 2 + odd]
            wide = low.astype(f32)
            gp = grad_probs[odd]
            ds = (wide * (gp - column_sum(wide * gp))).astype(bf16)
            dv = dv + dot(low, jnp.where(mine, g, zero))
            dk = dk + dot(ds, jnp.where(mine, q, zero))
            dq_t.append(dot(k_t[64 * odd : 64 * odd + 64], ds))
        dq = jnp.concatenate(dq_t, 0).T * 0.125
        sums[0, :, pl.ds(at, 128)] = rows_of(8, column_sum(dq), column_sum(dv))
        grad_low[:, pl.ds(at, 128)] = dq.astype(bf16)
        grad_low[:, pl.ds(D + at, 128)] = dk.astype(bf16)
        grad_low[:, pl.ds(2 * D + at, 128)] = dv.astype(bf16)
        return 0

    lax.fori_loop(0, HEADS // 2, pair, 0, unroll=True)


def attend_back(row, packed, grad_att, probs, low=None):
    length = probs.shape[1]
    kernel, more, specs, alias = attend_back_kernel, (), [], {}
    if low is not None:
        more, specs, alias = (low,), [pl.BlockSpec(memory_space=pl.ANY)], {3: 0}

        def kernel(packed, grad_att, probs, low, grad_low, sums):
            attend_back_kernel(packed, grad_att, probs, grad_low, sums)

    return pl.pallas_call(
        kernel,
        grid=(1,),
        in_specs=[
            pl.BlockSpec((length, 3 * D), lambda i: (row, 0)),
            pl.BlockSpec((length, D), lambda i: (row, 0)),
            pl.BlockSpec((HEADS, length, length), lambda i: (row, 0, 0)),
        ]
        + specs,
        out_specs=[
            pl.BlockSpec((length, 3 * D), lambda i: (row, 0)),
            pl.BlockSpec((1, 8, D), lambda i: (0, 0, 0)),
        ],
        out_shape=[Shape(packed.shape, bf16), Shape((1, 8, D), f32)],
        input_output_aliases=alias,
        compiler_params=params(),
        cost_estimate=cost(12),
        name="attend_back",
    )(packed, grad_att, probs, *more)


def grad_qkv_kernel(place, hidden, low, table, kept_out, sent_out, kept, sent, turned):
    z, y, x, core = place()
    turn_rows(place, hidden[...].T, turned)
    for i in range(2):
        columns = pl.ds(pl.multiple_of((x ^ i) * 1152, 128), 1152)
        res = dot(turned[...], low[:, columns]).astype(bf16)
        for other, out, more in ((0, kept, kept_out), (1, sent, sent_out)):
            for j in range(2):
                step = i + 2 * j
                for k in range(4):
                    at = (other * 8 + j * 4 + k) * 48
                    out[step, k, :, :1152] = res[at : at + 48]
                    out[step, k, :, 1152:1536] = more[step, k]
                    device = ((z ^ k) * 2 + (y ^ j)) * 4 + (x ^ i) * 2 + (core ^ other)
                    out[step, k, :16, 1536:] = table[device]
                    out[step, k, 16:, 1536:] = jnp.zeros((32, 128), bf16)


def grad_qkv(place, hidden, low, vectors, out_tables):
    table = jnp.pad(vectors.astype(bf16).reshape(32, 288), ((0, 0), (0, 96)))
    table = jnp.pad(table.reshape(32, 3, 128), ((0, 0), (0, 13), (0, 0)))
    return pl.pallas_call(
        functools.partial(grad_qkv_kernel, place),
        out_shape=[Shape((4, 4, 48, 1664), bf16)] * 2,
        scratch_shapes=[pltpu.VMEM((D, hidden.shape[0]), bf16)],
        compiler_params=params(),
        cost_estimate=cost(9),
        name="grad_qkv",
    )(hidden, low, table, *out_tables)


def hidden_kernel(low, weight, grad_branch, out):
    out[...] = grad_branch[...] + dot_t(low[...], weight[...])


def grad_of_hidden(low, weight, grad_branch):
    tokens = low.shape[0]
    return pl.pallas_call(
        hidden_kernel,
        grid=(tokens // TILE,),
        in_specs=[tile(3 * D), fixed((D, 3 * D)), tile(D)],
        out_specs=tile(D),
        out_shape=Shape((tokens, D), f32),
        compiler_params=params(),
        cost_estimate=cost(9),
        name="grad_hidden",
    )(low, weight, grad_branch)


def gather_plain(w_qkv, w_out, w_in, w_back, vectors):
    def whole(piece):
        return lax.all_gather(
            lax.all_gather(piece, "narrow", axis=1, tiled=True), "wide", axis=0, tiled=True
        )

    full = tuple(whole(piece) for piece in (w_qkv, w_out, w_in, w_back))
    return full + (lax.all_gather(vectors, ALL, axis=0, tiled=True).reshape(12, D),)


def tie(*values):
    return lax.optimization_barrier(values)


def unfold(table, order, shape):
    return table.reshape((2, 2, 2, 4) + table.shape[3:]).transpose(order).reshape(shape)


def scatter_whole(matrix):
    part = lax.psum_scatter(matrix, "wide", scatter_dimension=0, tiled=True)
    part = lax.psum_scatter(part, "narrow", scatter_dimension=1, tiled=True)
    return part.astype(f32)


def per_device(hidden, segment, w_qkv, w_out, w_in, w_back, vectors, cotangent):
    (qkv,) = pair_up([w_qkv], [send(w_qkv, core=1)], vectors)
    rest = [w_out, w_in, w_back]
    other_rest = [send(piece, core=1) for piece in rest]
    qkv, other_rest, segment = tie(qkv, other_rest, segment)
    key_marks, query_marks = segment_marks(segment)
    qkv_line = gather_z(qkv)
    out, inner, back = pair_up(rest, other_rest)
    mid = jnp.concatenate([inner, out], 1)
    qkv_line, mid, back, key_marks, query_marks = tie(
        jnp.stack(qkv_line), mid, back, key_marks, query_marks
    )

    qkv_blocks = gather_chips(qkv_line)
    mid_line = gather_z(mid)
    qkv_blocks, mid_line, back = tie(qkv_blocks, mid_line, back)

    back_table = lax.all_gather(back, ALL, axis=0, tiled=False)
    mid_blocks = gather_chips(jnp.stack(mid_line))
    qkv_blocks = gather_cores(qkv_blocks)
    full_qkv = assemble(qkv_blocks, (1152,), "assemble_qkv")[0]
    all_vectors = place_vectors(qkv_blocks)
    attended = attend(hidden, full_qkv, all_vectors, key_marks, query_marks)
    attended, mid_blocks = tie(attended, mid_blocks)
    packed, att, att_t, probs = attended

    full_in, full_out = assemble(gather_cores(mid_blocks), (1536, 384), "assemble_in")
    inner_outs = inner_forward(att, hidden, all_vectors, full_out, full_in)
    inner_outs, back_table = tie(inner_outs, back_table)
    first_low, normed, inverse, activated, slope = inner_outs

    full_back = assemble_table(back_table, "assemble_back")
    output, grad_second, sums_second, kept_back, sent_back = outer_forward(
        position, activated, normed, cotangent, all_vectors, full_back
    )

    received_back = send(sent_back, core=1)
    back_outs = backward(
        grad_second, slope, normed, inverse, all_vectors, full_out, full_in, full_back
    )
    back_outs, received_back = tie(back_outs, received_back)
    grad_att, grad_branch, branch_low, inner_low, sums_first, sums_inner = back_outs

    parts_back = chip_parts(kept_back, received_back)
    parts_back, inner_low = tie(parts_back, inner_low)
    plane_back = [send(parts_back[1], x=1), send(parts_back[2], y=1)]
    kept_in, sent_in = grad_in(position, first_low, inner_low)
    kept_in, sent_in, plane_back, corner_back = tie(kept_in, sent_in, plane_back, parts_back[3])

    corner_back = send(corner_back, x=1, y=1)
    received_in = send(sent_in, core=1)
    out_tables = grad_out(position, att_t, branch_low)
    out_tables, received_in = tie(out_tables, received_in)

    parts_in = chip_parts(kept_in, received_in)
    parts_in, grad_att, out_tables = tie(parts_in, grad_att, out_tables)
    others_in = chip_sends(parts_in)
    packed_low, sums_zero = attend_back(0, packed, grad_att, probs)
    packed_low, corner_back = tie(packed_low, corner_back)

    near_back, far_back = line_halves(parts_back[0], plane_back + [corner_back])
    near_back, far_back, packed_low = tie(near_back, far_back, packed_low)
    far_back = send(far_back, z=2)
    packed_low, sums_one = attend_back(1, packed, grad_att, probs, packed_low)
    packed_low, far_back, sums_one = tie(packed_low, far_back, sums_one)

    near_back = near_parts(near_back, far_back)
    next_back = send(near_back[1], z=1)
    grad_vectors = jnp.concatenate(
        [(sums_zero + sums_one)[0, :2], sums_first[:3], sums_inner[:4], sums_second[:3]], 0
    )
    kept_qkv, sent_qkv = grad_qkv(position, hidden, packed_low, grad_vectors, out_tables)
    kept_qkv, sent_qkv, next_back, others_in = tie(kept_qkv, sent_qkv, next_back, others_in)

    received_qkv = send(sent_qkv, core=1)
    near_in, far_in = line_halves(parts_in[0], others_in)
    far_in = send(far_in, z=2)
    parts_qkv = chip_parts(kept_qkv, received_qkv)
    parts_qkv, grad_branch = tie(parts_qkv, grad_branch)
    others_qkv = chip_sends(parts_qkv)
    grad_hidden = grad_of_hidden(packed_low, full_qkv, grad_branch)
    own_back = wide_sum(near_back[0], next_back).T
    grad_hidden, far_in, own_back = tie(grad_hidden, far_in, own_back)

    near_in = near_parts(near_in, far_in)
    next_in = send(near_in[1], z=1)
    others_qkv, near_in = tie(others_qkv, near_in)
    line_qkv = line_parts(parts_qkv[0], others_qkv)
    lines_qkv = line_sends(line_qkv)
    own_in = wide_sum(near_in[0], next_in)
    own_in, lines_qkv = tie(own_in, lines_qkv)
    own_qkv = wide_sum(line_qkv[0], *lines_qkv)
    own_vectors = own_qkv[:3, 1536:].reshape(-1)[:288]
    own_out = swap_columns(own_qkv[:, 1152:1536])
    own_qkv = swap_columns(own_qkv[:, :1152])
    return (output, grad_hidden, own_qkv, own_out, own_in, own_back, own_vectors)


def per_device_plain(hidden, segment, w_qkv, w_out, w_in, w_back, vectors, cotangent):
    key_marks, query_marks = segment_marks(segment)
    full_qkv, full_out, full_in, full_back, all_vectors = gather_plain(
        w_qkv, w_out, w_in, w_back, vectors
    )
    packed, att, att_t, probs = attend(hidden, full_qkv, all_vectors, key_marks, query_marks)
    first_low, normed, inverse, activated, slope = inner_forward(
        att, hidden, all_vectors, full_out, full_in
    )
    output, grad_second, sums_second, *back_table = outer_forward(
        origin, activated, normed, cotangent, all_vectors, full_back
    )
    grad_att, grad_branch, branch_low, inner_low, sums_first, sums_inner = backward(
        grad_second, slope, normed, inverse, all_vectors, full_out, full_in, full_back
    )
    in_table = jnp.stack(grad_in(origin, first_low, inner_low))
    out_table = grad_out(origin, att_t, branch_low)
    packed_low, sums_zero = attend_back(0, packed, grad_att, probs)
    packed_low, sums_one = attend_back(1, packed, grad_att, probs, packed_low)
    grad_hidden = grad_of_hidden(packed_low, full_qkv, grad_branch)
    grad_vectors = jnp.concatenate(
        [(sums_zero + sums_one)[0, :2], sums_first[:3], sums_inner[:4], sums_second[:3]], 0
    )
    qkv_table = jnp.stack(grad_qkv(origin, hidden, packed_low, grad_vectors, out_table))
    full_qkv, full_out = qkv_table[..., :1152], qkv_table[..., 1152:1536]
    own_qkv = scatter_whole(unfold(full_qkv, (3, 1, 0, 4, 2, 5), (D, 3 * D)))
    own_out = scatter_whole(unfold(full_out, (3, 1, 0, 4, 2, 5), (D, D)))
    own_in = scatter_whole(unfold(in_table, (3, 1, 4, 2, 0, 5), (D, FF)))
    back_t = unfold(jnp.stack(back_table), (2, 0, 4, 3, 1, 5), (D, FF))
    own_back = scatter_whole(back_t.T)
    own_vectors = lax.psum_scatter(
        grad_vectors.reshape(-1), ALL, scatter_dimension=0, tiled=True
    )
    return (output, grad_hidden, own_qkv, own_out, own_in, own_back, own_vectors)


def solution(mesh):
    trees = mesh.shape["wide"] == 8 and mesh.shape["narrow"] == 4
    return jax.shard_map(
        per_device if trees else per_device_plain,
        mesh=mesh,
        in_specs=(P(ALL, None),) * 2 + (P("wide", "narrow"),) * 4 + (P(ALL), P(ALL, None)),
        out_specs=(P(ALL, None),) * 2 + (P("wide", "narrow"),) * 4 + (P(ALL),),
        check_vma=False,
    )
```

```python
import functools

import jax
import jax.numpy as jnp
from jax import lax
from jax.experimental import pallas as pl
from jax.experimental.pallas import tpu as pltpu
from jax.sharding import PartitionSpec as P

D = 768
HEADS = 12
FF = 3072
TILE = 256
ALL = ("wide", "narrow")
CHIP_STEPS = ((0, 0), (1, 0), (0, 1), (1, 1))
VMEM_LIMIT = 60 * 2**20
bf16, f32 = jnp.bfloat16, jnp.float32
Shape = jax.ShapeDtypeStruct

epsilon = 1e-06


def cost(us):
    return pl.CostEstimate(flops=0 * us, bytes_accessed=0, transcendentals=0)


def params():
    return pltpu.CompilerParams(vmem_limit_bytes=VMEM_LIMIT)


def send(values, z=0, y=0, x=0, core=0):
    flip_wide, flip_narrow = 2 * z + y, 2 * x + core
    pairs = [
        (w * 4 + n, (w ^ flip_wide) * 4 + (n ^ flip_narrow)) for w in range(8) for n in range(4)
    ]
    return lax.ppermute(values, ALL, pairs)


def position():
    wide, narrow = lax.axis_index("wide"), lax.axis_index("narrow")
    return wide // 2, wide % 2, narrow // 2, narrow % 2


def origin():
    zero = jnp.int32(0)
    return zero, zero, zero, zero


def gather_z(values):
    return [values] + [send(values, z=k) for k in (1, 2, 3)]


def gather_chips(lines):
    return [lines] + [send(lines, x=i, y=j) for i, j in CHIP_STEPS[1:]]


def gather_cores(blocks):
    return blocks + [send(block, core=1) for block in blocks]


def pair_kernel(count, *refs):
    core = lax.rem(lax.axis_index("narrow"), 2)
    more, outs = refs[2 * count : -count], refs[-count:]
    for own, other, out in zip(refs[:count], refs[count : 2 * count], outs):
        rows, columns = own.shape[0] // 2, own.shape[1]
        half = pl.ds(pl.multiple_of(core * rows, rows), rows)

        @pl.when(core == 0)
        def _(own=own, other=other, out=out, half=half, columns=columns):
            out[:, :columns] = own[half, :]
            out[:, columns : 2 * columns] = other[half, :]

        @pl.when(core == 1)
        def _(own=own, other=other, out=out, half=half, columns=columns):
            out[:, :columns] = other[half, :]
            out[:, columns : 2 * columns] = own[half, :]

    for vector in more:
        rest, parts = vector[...], []
        for _ in range(3):
            parts.append(rest.astype(bf16).astype(f32))
            rest = rest - parts[-1]
        outs[0][:, 1152:] = rows_of(48, *parts).astype(bf16)


def pair_up(pieces, others, vectors=None):
    more = [0] * len(pieces)
    rows = ()
    if vectors is not None:
        rows = (jnp.pad(vectors, (0, 384 - vectors.shape[0])).reshape(3, 128),)
        more[0] = 128
    return pl.pallas_call(
        functools.partial(pair_kernel, len(pieces)),
        out_shape=[
            Shape((piece.shape[0] // 2, piece.shape[1] * 2 + extra), piece.dtype)
            for piece, extra in zip(pieces, more)
        ],
        cost_estimate=cost(2),
        name="pair_up",
    )(*pieces, *others, *rows)


def block_copies(place, blocks, left, out, sems):
    z, y, x, core = place()
    rows, width = blocks[0].shape[1], out.shape[1] // 2
    copies = []
    for other in range(2):
        for step, (i, j) in enumerate(CHIP_STEPS):
            for k in range(4):
                row = (((z ^ k) * 2 + (y ^ j)) * 2 + (core ^ other)) * rows
                copies.append(
                    pltpu.make_async_copy(
                        blocks[other * 4 + step].at[k, :, pl.ds(left, width)],
                        out.at[
                            pl.ds(pl.multiple_of(row, rows), rows),
                            pl.ds(pl.multiple_of((x ^ i) * width, width), width),
                        ],
                        sems.at[len(copies)],
                    )
                )
    return copies


def table_copies(table, out, sems):
    rows, columns = table.shape[1:]
    return [
        pltpu.make_async_copy(
            table.at[w * 4 + n],
            out.at[pl.ds((w * 2 + n % 2) * rows, rows), pl.ds(n // 2 * columns, columns)],
            sems.at[w * 4 + n],
        )
        for w in range(8)
        for n in range(4)
    ]


def start(copies):
    for copy in copies:
        copy.start()


def wait(copies):
    for copy in copies:
        copy.wait()


def anywhere(count):
    return [pl.BlockSpec(memory_space=pl.ANY)] * count


def split_blocks(matrix, rows, columns):
    parts = matrix.reshape(4, 2, 2, rows, 2, columns).transpose(2, 1, 4, 0, 3, 5)
    return [parts[other, j, i] for other in range(2) for i, j in CHIP_STEPS]


def place_kernel(*refs):
    z, y, x, core = position()
    out = refs[8]
    for other in range(2):
        for step, (i, j) in enumerate(CHIP_STEPS):
            for k in range(4):
                row = ((z ^ k) * 2 + (y ^ j)) * 4 + (x ^ i) * 2 + (core ^ other)
                parts = refs[other * 4 + step][k].astype(f32)
                out[row] = parts[:3] + parts[3:6] + parts[6:9]


def place_vectors(blocks):
    table = pl.pallas_call(
        place_kernel,
        grid=(1,),
        in_specs=[pl.BlockSpec((4, 16, 128), lambda i: (0, 0, 9))] * 8,
        out_specs=fixed((32, 3, 128)),
        out_shape=Shape((32, 3, 128), f32),
        cost_estimate=cost(1),
        name="place_vectors",
    )(*blocks)
    return table.reshape(32, 384)[:, :288].reshape(12, D)


def wide_sum(*terms):
    return functools.reduce(lambda a, b: a + b, [t.astype(f32) for t in terms])


def chip_parts(kept, received):
    return [wide_sum(kept[s], received[s]).astype(bf16) for s in range(4)]


def chip_kernel(*refs):
    for kept, received, out in zip(refs[:4], refs[4:8], refs[8:]):
        out[...] = wide_sum(kept[...], received[...]).astype(bf16)


def chip_parts_of(kept, received):
    rows, columns = kept[0].shape[1:]
    line = pl.BlockSpec((1, rows, columns), lambda k: (k, 0, 0))
    return pl.pallas_call(
        chip_kernel,
        grid=(4,),
        in_specs=[line] * 8,
        out_specs=[line] * 4,
        out_shape=[Shape((4, rows, columns), bf16)] * 4,
        compiler_params=params(),
        cost_estimate=cost(3),
        name="chip_parts",
    )(*kept, *received)


def chip_sends(parts):
    return [send(parts[s], x=i, y=j) for s, (i, j) in enumerate(CHIP_STEPS) if s]


def line_kernel(far, *refs):
    terms, outs = refs[:4], refs[4:]
    for k in range(4):
        total = wide_sum(*[term[k] for term in terms]).astype(bf16)
        if far and k >= 2:
            outs[2][k - 2] = total
        else:
            outs[k][...] = total


def line_parts(own, others, far=False):
    piece = Shape(own.shape[1:], bf16)
    shapes = [piece] * 2 + [Shape((2,) + own.shape[1:], bf16)] if far else [piece] * 4
    return pl.pallas_call(
        functools.partial(line_kernel, far),
        out_shape=shapes,
        compiler_params=params(),
        cost_estimate=cost(2),
        name="line_parts",
    )(own, *others)


def line_sends(line):
    return [send(line[k], z=k) for k in (1, 2, 3)]


def line_halves(own, others):
    *near, far = line_parts(own, others, True)
    return near, far


def near_parts(near, received):
    return [wide_sum(near[k], received[k]).astype(near[k].dtype) for k in range(2)]


def swap_columns(summed):
    core = lax.axis_index("narrow") % 2
    columns = summed.shape[1] // 2
    left, right = summed[:, :columns], summed[:, columns:]
    mine = jnp.where(core == 0, left, right)
    other = send(jnp.where(core == 0, right, left).astype(bf16), core=1).astype(f32)
    return jnp.concatenate(
        [jnp.where(core == 0, mine, other), jnp.where(core == 0, other, mine)], 0
    )


def dot(left_side, right_side):
    return jnp.dot(left_side, right_side, preferred_element_type=f32)


def dot_t(left_side, right_side):
    return lax.dot_general(
        left_side, right_side, (((1,), (1,)), ((), ())), preferred_element_type=f32
    )


def column_sum(values):
    return jnp.sum(values, 0, keepdims=True)


def normalize(values):
    center = values - jnp.mean(values, -1, keepdims=True)
    inverse = lax.rsqrt(jnp.mean(center * center, -1, keepdims=True) + epsilon)
    return center * inverse, inverse


def normalize_back(grad_norm, normed, inverse):
    return inverse * (
        grad_norm
        - jnp.mean(grad_norm, -1, keepdims=True)
        - normed * jnp.mean(grad_norm * normed, -1, keepdims=True)
    )


def smooth(values):
    density = jnp.exp(-0.5 * values * values) * 0.3989422804014327
    below = 0.5 + 0.5 * lax.erf(values * 0.7071067811865476)
    return values * below, below + values * density


def fixed(shape):
    return pl.BlockSpec(shape, lambda i: (0,) * len(shape))


def tile(columns, rows=TILE):
    return pl.BlockSpec((rows, columns), lambda i: (i, 0))


def rows_of(count, *parts):
    missing = count - sum(part.shape[0] for part in parts)
    return jnp.concatenate(list(parts) + [jnp.zeros((missing, parts[0].shape[1]), f32)], 0)


def segment_marks(segment):
    kinds = lax.broadcasted_iota(jnp.int32, (1, 64), 1)
    mark = (segment.reshape(-1, 1) == kinds).astype(bf16)
    tall = lax.broadcasted_iota(jnp.int32, (1, 64, 1), 1)
    away = (segment[:, None, :] != tall) & (tall < 4)
    return jnp.concatenate([mark, mark], 1), jnp.where(away, -(2.0**30), 0.0).astype(bf16)


def attend_kernel(place, *refs):
    hidden, vectors, key_marks, query_marks = refs[:4]
    blocks, (packed, att, att_t, probs, weight, sems) = refs[4:12], refs[12:]

    @pl.when(pl.program_id(0) == 0)
    def _():
        copies = block_copies(place, blocks, 0, weight, sems)
        start(copies)
        wait(copies)

    length = hidden.shape[0]
    for part in range(3):
        columns = slice(part * D, (part + 1) * D)
        block = dot(hidden[...], weight[:, columns])
        if part != 1:
            block = block + vectors[part // 2 : part // 2 + 1, :]
        block = block.astype(bf16)
        if part == 0:
            block = block * jnp.asarray(0.125, bf16)
        packed[:, columns] = block
    lanes = lax.broadcasted_iota(jnp.int32, (length, 128), 1)

    def pair(p, _):
        at = pl.multiple_of(p * 128, 128)
        q_t = packed[:, pl.ds(at, 128)].T
        k = packed[:, pl.ds(D + at, 128)]
        v_t = packed[:, pl.ds(2 * D + at, 128)].T
        scores = []
        for odd in range(2):
            keys = jnp.where((lanes >= 64) == bool(odd), k, key_marks[...])
            own = q_t[64 * odd : 64 * odd + 64]
            marks = query_marks[0]
            scores.append(dot(keys, jnp.concatenate([marks, own] if odd else [own, marks], 0)))
        outs = []
        for odd in range(2):
            weights = jnp.exp(scores[odd] - jnp.max(scores[odd], 0, keepdims=True))
            low = (weights * (1.0 / column_sum(weights))).astype(bf16)
            probs[p * 2 + odd] = low
            outs.append(dot(v_t[64 * odd : 64 * odd + 64], low))
        out = jnp.concatenate(outs, 0).astype(bf16)
        att_t[pl.ds(at, 128), :] = out
        att[:, pl.ds(at, 128)] = out.T
        return 0

    lax.fori_loop(0, HEADS // 2, pair, 0, unroll=True)


def attend(place, hidden, vectors, key_marks, query_marks, blocks):
    rows, length = query_marks.shape[0], query_marks.shape[2]
    tokens = rows * length
    return pl.pallas_call(
        functools.partial(attend_kernel, place),
        grid=(rows,),
        in_specs=[
            tile(D, length),
            fixed((12, D)),
            tile(128, length),
            pl.BlockSpec((1, 64, length), lambda i: (i, 0, 0)),
        ]
        + anywhere(8),
        scratch_shapes=[pltpu.VMEM((D, 3 * D), bf16), pltpu.SemaphoreType.DMA((32,))],
        out_specs=[
            tile(3 * D, length),
            tile(D, length),
            pl.BlockSpec((D, length), lambda i: (0, i)),
            pl.BlockSpec((HEADS, length, length), lambda i: (i, 0, 0)),
        ],
        out_shape=[
            Shape((tokens, 3 * D), bf16),
            Shape((tokens, D), bf16),
            Shape((D, tokens), bf16),
            Shape((rows * HEADS, length, length), bf16),
        ],
        compiler_params=params(),
        cost_estimate=cost(20),
        name="attend",
    )(hidden, vectors, key_marks, query_marks, *blocks)


def inner_kernel(place, *refs):
    att, hidden, vectors = refs[:3]
    blocks, (first_low, normed, inverse, activated, slope) = refs[3:11], refs[11:16]
    w_in, w_out, in_sems, out_sems = refs[16:]
    first_step = pl.program_id(0) == 0

    def row(i):
        return vectors[i : i + 1, :]

    def copies_in():
        return block_copies(place, blocks, 0, w_in, in_sems)

    @pl.when(first_step)
    def _():
        copies = block_copies(place, blocks, 1536, w_out, out_sems)
        start(copies)
        start(copies_in())
        wait(copies)

    n1, r1 = normalize(hidden[...].astype(f32) + dot(att[...], w_out[...]) + row(2))
    low = (n1 * row(3) + row(4)).astype(bf16)
    first_low[...] = low
    normed[...] = n1
    inverse[...] = jnp.broadcast_to(r1, inverse.shape)

    @pl.when(first_step)
    def _():
        wait(copies_in())

    for c in range(FF // D):
        columns = slice(c * D, c * D + D)
        act, back = smooth(dot(low, w_in[:, columns]) + row(5 + c))
        activated[:, columns] = act.astype(bf16)
        slope[:, columns] = back.astype(bf16)


def inner_forward(place, att, hidden, vectors, blocks):
    tokens = hidden.shape[0]
    return pl.pallas_call(
        functools.partial(inner_kernel, place),
        grid=(tokens // TILE,),
        in_specs=[tile(D)] * 2 + [fixed((12, D))] + anywhere(8),
        out_specs=[tile(D), tile(D), tile(128), tile(FF), tile(FF)],
        out_shape=[
            Shape((tokens, D), bf16),
            Shape((tokens, D), f32),
            Shape((tokens, 128), f32),
            Shape((tokens, FF), bf16),
            Shape((tokens, FF), bf16),
        ],
        scratch_shapes=[
            pltpu.VMEM((D, FF), bf16),
            pltpu.VMEM((D, D), bf16),
            pltpu.SemaphoreType.DMA((32,)),
            pltpu.SemaphoreType.DMA((32,)),
        ],
        compiler_params=params(),
        cost_estimate=cost(16),
        name="inner_forward",
    )(att, hidden, vectors, *blocks)


def outer_kernel(place, *refs):
    act, normed, cotangent, vectors, back_table = refs[:5]
    output, grad_second, sums, kept, sent, w_back, activated, grad_t, sems = refs[5:]
    step = pl.program_id(0)
    z, y, x, core = place()

    def row(i):
        return vectors[i : i + 1, :]

    @pl.when(step == 0)
    def _():
        copies = table_copies(back_table, w_back, sems)
        start(copies)
        wait(copies)

    here = pl.ds(pl.multiple_of(step * TILE, TILE), TILE)
    activated[here, :] = act[...]
    outward = normed[...] * row(3) + row(4) + dot(act[...], w_back[...]) + row(9)
    n2, r2 = normalize(outward)
    output[...] = (n2 * row(10) + row(11)).astype(bf16)
    cot = cotangent[...].astype(f32)
    g2 = normalize_back(cot * row(10), n2, r2)
    grad_second[...] = g2
    part = rows_of(8, column_sum(g2), column_sum(cot * n2), column_sum(cot))

    @pl.when(step == 0)
    def _():
        sums[...] = part

    @pl.when(step > 0)
    def _():
        sums[...] += part

    g2_t = g2.astype(bf16).T
    for n in range(4):
        at = ((n % 2) ^ core) * 2 + ((n // 2) ^ x)
        piece = g2_t[n * 192 : n * 192 + 192]
        grad_t[pl.ds(pl.multiple_of(at * 192, 192), 192), here] = piece

    @pl.when(step == pl.num_programs(0) - 1)
    def _():
        for k in range(4):
            columns = pl.ds(pl.multiple_of((z ^ k) * D, D), D)
            res = dot(grad_t[...], activated[:, columns]).astype(bf16)
            for other, out in enumerate((kept, sent)):
                for i in range(2):
                    at = (other * 2 + i) * 192
                    for half in range(2):
                        piece = res[at : at + 192, half * 384 : half * 384 + 384]
                        out[i + 2 * (half ^ y), k] = piece


def outer_forward(place, activated, normed, cotangent, vectors, back_table):
    tokens = normed.shape[0]
    return pl.pallas_call(
        functools.partial(outer_kernel, place),
        grid=(tokens // TILE,),
        in_specs=[tile(FF), tile(D), tile(D), fixed((12, D))] + anywhere(1),
        out_specs=[tile(D), tile(D), fixed((8, D))] + [fixed((4, 4, 192, 384))] * 2,
        out_shape=[
            Shape((tokens, D), bf16),
            Shape((tokens, D), f32),
            Shape((8, D), f32),
        ]
        + [Shape((4, 4, 192, 384), bf16)] * 2,
        scratch_shapes=[
            pltpu.VMEM((FF, D), bf16),
            pltpu.VMEM((tokens, FF), bf16),
            pltpu.VMEM((D, tokens), bf16),
            pltpu.SemaphoreType.DMA((32,)),
        ],
        compiler_params=params(),
        cost_estimate=cost(18),
        name="outer_forward",
    )(activated, normed, cotangent, vectors, back_table)


def backward_kernel(place, *refs):
    grad_second, slope, normed, inverse, first_low, att_t, vectors = refs[:7]
    blocks, back_table = refs[7:15], refs[15]
    grad_att, grad_branch, sums, sums_inner, kept, sent = refs[16:22]
    w_in, w_out, w_back, inner_low, first_t, grad_low, turned = refs[22:29]
    in_sems, out_sems, back_sems = refs[29:]
    step = pl.program_id(0)
    z, y, x, core = place()
    here = pl.ds(pl.multiple_of(step * TILE, TILE), TILE)

    def compute(first_step):
        if first_step:
            copies_back = table_copies(back_table, w_back, back_sems)
            copies_in = block_copies(place, blocks, 0, w_in, in_sems)
            copies_out = block_copies(place, blocks, 1536, w_out, out_sems)
            start(copies_back)
            start(copies_in)
            start(copies_out)
        g2 = grad_second[...]
        g2_low = g2.astype(bf16)
        grad_first = g2
        inner_sums = []
        for c in range(FF // D):
            columns = slice(c * D, c * D + D)
            if first_step:
                wait(copies_back[c * 8 : c * 8 + 8])
            gi = dot_t(g2_low, w_back[columns, :]) * slope[:, columns].astype(f32)
            inner_sums.append(column_sum(gi))
            gi = gi.astype(bf16)
            inner_low[here, columns] = gi
            if first_step and c == 0:
                wait(copies_in)
            grad_first = grad_first + dot_t(gi, w_in[:, columns])
        n1 = normed[...]
        g1 = normalize_back(grad_first * vectors[3:4, :], n1, inverse[:, :1])
        grad_branch[...] = g1
        g1_low = g1.astype(bf16)
        grad_low[here, :] = g1_low
        if first_step:
            wait(copies_out)
        grad_att[...] = dot_t(g1_low, w_out[...]).astype(bf16)
        part = rows_of(8, column_sum(g1), column_sum(grad_first * n1), column_sum(grad_first))
        part_inner = rows_of(8, *inner_sums)
        if first_step:
            sums[...] = part
            sums_inner[...] = part_inner
        else:
            sums[...] += part
            sums_inner[...] += part_inner
        low_t = first_low[...].T
        for w in range(8):
            at = ((w % 2) ^ y) * 4 + ((w // 2) ^ z)
            piece = low_t[w * 96 : w * 96 + 96]
            first_t[pl.ds(pl.multiple_of(at * 96, 96), 96), here] = piece
        turn_rows(place, att_t, turned, here)

    @pl.when(step == 0)
    def _():
        compute(True)

    @pl.when(step > 0)
    def _():
        compute(False)

    @pl.when(step == pl.num_programs(0) - 1)
    def _():
        for i in range(2):
            for other, out in enumerate((kept, sent)):
                at = ((x ^ i) * 2 + (core ^ other)) * D
                res = dot(first_t[...], inner_low[:, pl.ds(pl.multiple_of(at, D), D)])
                res = res.astype(bf16)
                for j in range(2):
                    for k in range(4):
                        at = (j * 4 + k) * 96
                        out[i + 2 * j, k, :, :D] = res[at : at + 48]
                        out[i + 2 * j, k, :, D : 2 * D] = res[at + 48 : at + 96]
        res = dot(turned[...], grad_low[...]).astype(bf16)
        for other, out in enumerate((kept, sent)):
            for j in range(2):
                for k in range(4):
                    at = (other * 8 + j * 4 + k) * 48
                    for half in range(2):
                        piece = res[at : at + 48, half * 384 : half * 384 + 384]
                        out[(half ^ x) + 2 * j, k, :, 2 * D :] = piece


def backward(place, grad_second, slope, normed, inverse, first_low, att_t, vectors, *weights):
    blocks, back_table = weights
    tokens = normed.shape[0]
    outs = [(4, 4, 48, 1920)] * 2
    return pl.pallas_call(
        functools.partial(backward_kernel, place),
        grid=(tokens // TILE,),
        in_specs=[tile(D), tile(FF), tile(D), tile(128), tile(D)]
        + [pl.BlockSpec((D, TILE), lambda i: (0, i)), fixed((12, D))]
        + anywhere(9),
        out_specs=[tile(D), tile(D)] + [fixed(s) for s in [(8, D)] * 2 + outs],
        out_shape=[Shape((tokens, D), bf16), Shape((tokens, D), f32)]
        + [Shape((8, D), f32)] * 2
        + [Shape(s, bf16) for s in outs],
        scratch_shapes=[
            pltpu.VMEM((D, FF), bf16),
            pltpu.VMEM((D, D), bf16),
            pltpu.VMEM((FF, D), bf16),
            pltpu.VMEM((tokens, FF), bf16),
            pltpu.VMEM((D, tokens), bf16),
            pltpu.VMEM((tokens, D), bf16),
            pltpu.VMEM((D, tokens), bf16),
        ]
        + [pltpu.SemaphoreType.DMA((32,))] * 3,
        compiler_params=params(),
        cost_estimate=cost(22),
        name="backward",
    )(grad_second, slope, normed, inverse, first_low, att_t, vectors, *blocks, back_table)


def turn_rows(place, source, turned, columns=slice(None)):
    z, y, _, core = place()
    for w in range(8):
        for half in range(2):
            at = (half ^ core) * 8 + ((w % 2) ^ y) * 4 + ((w // 2) ^ z)
            piece = (w * 2 + half) * 48
            rows = pl.ds(pl.multiple_of(at * 48, 48), 48)
            turned[rows, columns] = source[piece : piece + 48, :]


def attend_back_kernel(packed, grad_att, probs, grad_low, sums):
    length = packed.shape[0]
    lanes = lax.broadcasted_iota(jnp.int32, (length, 128), 1)
    zero = jnp.zeros((length, 128), bf16)
    blank = jnp.zeros((64, length), bf16)

    def pair(p, _):
        at = pl.multiple_of(p * 128, 128)
        q = packed[:, pl.ds(at, 128)]
        k_t = packed[:, pl.ds(D + at, 128)].T
        v = packed[:, pl.ds(2 * D + at, 128)]
        g = grad_att[:, pl.ds(at, 128)]
        g_t = g.T
        grad_probs = []
        for odd in range(2):
            own = g_t[64 * odd : 64 * odd + 64]
            grad_probs.append(dot(v, jnp.concatenate([blank, own] if odd else [own, blank], 0)))
        dk = dv = 0.0
        dq_t = []
        for odd in range(2):
            mine = (lanes >= 64) == bool(odd)
            low = probs[p * 2 + odd]
            wide = low.astype(f32)
            gp = grad_probs[odd]
            ds = (wide * (gp - column_sum(wide * gp))).astype(bf16)
            dv = dv + dot(low, jnp.where(mine, g, zero))
            dk = dk + dot(ds, jnp.where(mine, q, zero))
            dq_t.append(dot(k_t[64 * odd : 64 * odd + 64], ds))
        dq = jnp.concatenate(dq_t, 0).T * 0.125
        sums[0, :, pl.ds(at, 128)] = rows_of(8, column_sum(dq), column_sum(dv))
        grad_low[:, pl.ds(at, 128)] = dq.astype(bf16)
        grad_low[:, pl.ds(D + at, 128)] = dk.astype(bf16)
        grad_low[:, pl.ds(2 * D + at, 128)] = dv.astype(bf16)
        return 0

    lax.fori_loop(0, HEADS // 2, pair, 0, unroll=True)


def attend_back(row, packed, grad_att, probs, low=None):
    length = probs.shape[1]
    kernel, more, specs, alias = attend_back_kernel, (), [], {}
    if low is not None:
        more, specs, alias = (low,), [pl.BlockSpec(memory_space=pl.ANY)], {3: 0}

        def kernel(packed, grad_att, probs, low, grad_low, sums):
            attend_back_kernel(packed, grad_att, probs, grad_low, sums)

    return pl.pallas_call(
        kernel,
        grid=(1,),
        in_specs=[
            pl.BlockSpec((length, 3 * D), lambda i: (row, 0)),
            pl.BlockSpec((length, D), lambda i: (row, 0)),
            pl.BlockSpec((HEADS, length, length), lambda i: (row, 0, 0)),
        ]
        + specs,
        out_specs=[
            pl.BlockSpec((length, 3 * D), lambda i: (row, 0)),
            pl.BlockSpec((1, 8, D), lambda i: (0, 0, 0)),
        ],
        out_shape=[Shape(packed.shape, bf16), Shape((1, 8, D), f32)],
        input_output_aliases=alias,
        compiler_params=params(),
        cost_estimate=cost(12),
        name="attend_back",
    )(packed, grad_att, probs, *more)


def grad_qkv_kernel(place, hidden, low, *refs):
    sums_zero, sums_one, sums_first, sums_inner, sums_second = refs[:5]
    outs, turned, groups = refs[5:13], refs[13], refs[14]
    z, y, x, core = place()
    turn_rows(place, hidden[...].T, turned)
    rows = [sums_zero[0, i : i + 1, :] + sums_one[0, i : i + 1, :] for i in range(2)]
    rows += [sums_first[i : i + 1, :] for i in range(3)]
    rows += [sums_inner[i : i + 1, :] for i in range(4)]
    rows += [sums_second[i : i + 1, :] for i in range(3)]
    for group in range(72):
        column = group % 6 * 128
        groups[group] = rows[group // 6][:, column : column + 128]
    for group in range(72, 76):
        groups[group] = jnp.zeros((1, 128), f32)
    for i in range(2):
        columns = pl.ds(pl.multiple_of((x ^ i) * 1152, 128), 1152)
        res = dot(turned[...], low[:, columns]).astype(bf16)
        for other in range(2):
            for j in range(2):
                out = outs[other * 4 + i + 2 * j]
                for k in range(4):
                    at = (other * 8 + j * 4 + k) * 48
                    out[k, :, :1152] = res[at : at + 48]
                    device = ((z ^ k) * 2 + (y ^ j)) * 4 + (x ^ i) * 2 + (core ^ other)
                    group = (9 * device) // 4
                    part = jnp.concatenate([groups[group + q] for q in range(4)], 0)
                    out[k, :16, 1152:] = rows_of(16, part).astype(bf16)
                    out[k, 16:, 1152:] = jnp.zeros((32, 128), bf16)


def grad_qkv(place, hidden, low, *sums):
    return pl.pallas_call(
        functools.partial(grad_qkv_kernel, place),
        out_shape=[Shape((4, 48, 1280), bf16)] * 8,
        scratch_shapes=[pltpu.VMEM((D, hidden.shape[0]), bf16), pltpu.VMEM((80, 1, 128), f32)],
        compiler_params=params(),
        cost_estimate=cost(9),
        name="grad_qkv",
    )(hidden, low, *sums)


def cut_vectors(place, groups):
    z, y, x, core = place()
    at = (((z * 2 + y) * 4 + x * 2 + core) * 288) % 128
    return lax.dynamic_slice(groups.reshape(-1), (at,), (288,))


def hidden_kernel(place, *refs):
    low, grad_branch, blocks, out, weight, sems = *refs[:2], refs[2:10], *refs[10:]

    @pl.when(pl.program_id(0) == 0)
    def _():
        copies = block_copies(place, blocks, 0, weight, sems)
        start(copies)
        wait(copies)

    out[...] = grad_branch[...] + dot_t(low[...], weight[...])


def grad_of_hidden(place, low, grad_branch, blocks):
    tokens = low.shape[0]
    return pl.pallas_call(
        functools.partial(hidden_kernel, place),
        grid=(tokens // TILE,),
        in_specs=[tile(3 * D), tile(D)] + anywhere(8),
        out_specs=tile(D),
        out_shape=Shape((tokens, D), f32),
        scratch_shapes=[pltpu.VMEM((D, 3 * D), bf16), pltpu.SemaphoreType.DMA((32,))],
        compiler_params=params(),
        cost_estimate=cost(9),
        name="grad_hidden",
    )(low, grad_branch, *blocks)


def gather_plain(w_qkv, w_out, w_in, w_back, vectors):
    def whole(piece):
        return lax.all_gather(
            lax.all_gather(piece, "narrow", axis=1, tiled=True), "wide", axis=0, tiled=True
        )

    full = tuple(whole(piece) for piece in (w_qkv, w_out, w_in, w_back))
    return full + (lax.all_gather(vectors, ALL, axis=0, tiled=True).reshape(12, D),)


def tie(*values):
    return lax.optimization_barrier(values)


def unfold(table, order, shape):
    return table.reshape((2, 2, 2, 4) + table.shape[3:]).transpose(order).reshape(shape)


def scatter_whole(matrix):
    part = lax.psum_scatter(matrix, "wide", scatter_dimension=0, tiled=True)
    part = lax.psum_scatter(part, "narrow", scatter_dimension=1, tiled=True)
    return part.astype(f32)


def per_device(hidden, segment, w_qkv, w_out, w_in, w_back, vectors, cotangent):
    (qkv,) = pair_up([w_qkv], [send(w_qkv, core=1)], vectors)
    rest = [w_out, w_in, w_back]
    other_rest = [send(piece, core=1) for piece in rest]
    qkv, other_rest, segment = tie(qkv, other_rest, segment)
    key_marks, query_marks = segment_marks(segment)
    qkv_line = gather_z(qkv)
    out, inner, back = pair_up(rest, other_rest)
    mid = jnp.concatenate([inner, out], 1)
    qkv_line, mid, back, key_marks, query_marks = tie(
        jnp.stack(qkv_line), mid, back, key_marks, query_marks
    )

    qkv_blocks = gather_chips(qkv_line)
    mid_line = gather_z(mid)
    qkv_blocks, mid_line, back = tie(qkv_blocks, mid_line, back)

    back_table = lax.all_gather(back, ALL, axis=0, tiled=False)
    mid_blocks = gather_chips(jnp.stack(mid_line))
    qkv_blocks = gather_cores(qkv_blocks)
    all_vectors = place_vectors(qkv_blocks)
    attended = attend(position, hidden, all_vectors, key_marks, query_marks, qkv_blocks)
    attended, mid_blocks = tie(attended, mid_blocks)
    packed, att, att_t, probs = attended

    mid_blocks = gather_cores(mid_blocks)
    inner_outs = inner_forward(position, att, hidden, all_vectors, mid_blocks)
    inner_outs, back_table = tie(inner_outs, back_table)
    first_low, normed, inverse, activated, slope = inner_outs

    output, grad_second, sums_second, kept_back, sent_back = outer_forward(
        position, activated, normed, cotangent, all_vectors, back_table
    )

    received_back = send(sent_back, core=1)
    back_outs = backward(
        position,
        grad_second,
        slope,
        normed,
        inverse,
        first_low,
        att_t,
        all_vectors,
        mid_blocks,
        back_table,
    )
    back_outs, received_back = tie(back_outs, received_back)
    grad_att, grad_branch, sums_first, sums_inner, kept_mid, sent_mid = back_outs

    received_mid = send(sent_mid, core=1)
    parts_back = chip_parts(kept_back, received_back)
    parts_back, received_mid = tie(parts_back, received_mid)

    others_back = chip_sends(parts_back)
    parts_mid = chip_parts(kept_mid, received_mid)
    parts_mid, grad_att = tie(parts_mid, grad_att)
    plane_mid = [send(parts_mid[1], x=1), send(parts_mid[2], y=1)]
    packed_low, sums_zero = attend_back(0, packed, grad_att, probs)
    packed_low, sums_one = attend_back(1, packed, grad_att, probs, packed_low)
    packed_low, sums_one, others_back, corner_mid = tie(
        packed_low, sums_one, others_back, parts_mid[3]
    )

    near_back, far_back = line_halves(parts_back[0], others_back)
    near_back, far_back, corner_mid, packed_low = tie(near_back, far_back, corner_mid, packed_low)
    corner_mid = send(corner_mid, x=1, y=1)
    far_back = send(far_back, z=2)
    tables_qkv = grad_qkv(
        position, hidden, packed_low, sums_zero, sums_one, sums_first, sums_inner, sums_second
    )
    tables_qkv, far_back, plane_mid = tie(tables_qkv, far_back, plane_mid)
    kept_qkv, sent_qkv = tables_qkv[:4], tables_qkv[4:]

    received_qkv = [send(block, core=1) for block in sent_qkv]
    parts_qkv = chip_parts_of(kept_qkv, received_qkv)
    parts_qkv, grad_branch, near_back, corner_mid = tie(
        parts_qkv, grad_branch, near_back, corner_mid
    )
    others_qkv = chip_sends(parts_qkv)
    near_mid, far_mid = line_halves(parts_mid[0], plane_mid + [corner_mid])
    far_mid = send(far_mid, z=2)
    near_back = near_parts(near_back, far_back)
    next_back = send(near_back[1], z=1)
    near_back, grad_branch = tie(near_back, grad_branch)
    grad_hidden = grad_of_hidden(position, packed_low, grad_branch, qkv_blocks)
    grad_hidden, far_mid, next_back = tie(grad_hidden, far_mid, next_back)

    own_back = wide_sum(near_back[0], next_back).T
    near_mid = near_parts(near_mid, far_mid)
    next_mid = send(near_mid[1], z=1)
    others_qkv, near_mid = tie(others_qkv, near_mid)
    line_qkv = line_parts(parts_qkv[0], others_qkv)
    lines_qkv = line_sends(line_qkv)
    own_mid = wide_sum(near_mid[0], next_mid)
    own_in = jnp.concatenate([own_mid[:, :D], own_mid[:, D : 2 * D]], 0)
    own_out = swap_columns(own_mid[:, 2 * D :])
    own_in, own_out, own_back, lines_qkv = tie(own_in, own_out, own_back, lines_qkv)
    own_qkv = wide_sum(line_qkv[0], *lines_qkv)
    own_vectors = cut_vectors(position, own_qkv[:4, 1152:])
    own_qkv = swap_columns(own_qkv[:, :1152])
    return (output, grad_hidden, own_qkv, own_out, own_in, own_back, own_vectors)


def per_device_plain(hidden, segment, w_qkv, w_out, w_in, w_back, vectors, cotangent):
    key_marks, query_marks = segment_marks(segment)
    full_qkv, full_out, full_in, full_back, all_vectors = gather_plain(
        w_qkv, w_out, w_in, w_back, vectors
    )
    qkv_blocks = split_blocks(full_qkv, 48, 1152)
    mid_blocks = [
        jnp.concatenate(pair, 2)
        for pair in zip(split_blocks(full_in, 48, 1536), split_blocks(full_out, 48, 384))
    ]
    back_pieces = full_back.reshape(8, 2, 192, 2, 384).transpose(0, 3, 1, 2, 4)
    back_pieces = back_pieces.reshape(32, 192, 384)
    packed, att, att_t, probs = attend(
        origin, hidden, all_vectors, key_marks, query_marks, qkv_blocks
    )
    first_low, normed, inverse, activated, slope = inner_forward(
        origin, att, hidden, all_vectors, mid_blocks
    )
    output, grad_second, sums_second, *back_table = outer_forward(
        origin, activated, normed, cotangent, all_vectors, back_pieces
    )
    grad_att, grad_branch, sums_first, sums_inner, *tables = backward(
        origin,
        grad_second,
        slope,
        normed,
        inverse,
        first_low,
        att_t,
        all_vectors,
        mid_blocks,
        back_pieces,
    )
    mid_table = jnp.stack(tables)
    packed_low, sums_zero = attend_back(0, packed, grad_att, probs)
    packed_low, sums_one = attend_back(1, packed, grad_att, probs, packed_low)
    grad_hidden = grad_of_hidden(origin, packed_low, grad_branch, qkv_blocks)
    tables = grad_qkv(
        origin, hidden, packed_low, sums_zero, sums_one, sums_first, sums_inner, sums_second
    )
    grad_vectors = jnp.concatenate(
        [(sums_zero + sums_one)[0, :2], sums_first[:3], sums_inner[:4], sums_second[:3]], 0
    )
    qkv_table = jnp.stack(tables)
    qkv_table = qkv_table.reshape(2, 4, 4, 48, 1280)
    halves = jnp.stack([mid_table[..., :D], mid_table[..., D : 2 * D]], 4)
    own_qkv = scatter_whole(unfold(qkv_table[..., :1152], (3, 1, 0, 4, 2, 5), (D, 3 * D)))
    own_out = scatter_whole(unfold(mid_table[..., 2 * D :], (3, 1, 0, 4, 2, 5), (D, D)))
    own_in = scatter_whole(unfold(halves, (3, 1, 4, 5, 2, 0, 6), (D, FF)))
    back_t = unfold(jnp.stack(back_table), (2, 0, 4, 3, 1, 5), (D, FF))
    own_back = scatter_whole(back_t.T)
    own_vectors = lax.psum_scatter(
        grad_vectors.reshape(-1), ALL, scatter_dimension=0, tiled=True
    )
    return (output, grad_hidden, own_qkv, own_out, own_in, own_back, own_vectors)


def solution(mesh):
    trees = mesh.shape["wide"] == 8 and mesh.shape["narrow"] == 4
    return jax.shard_map(
        per_device if trees else per_device_plain,
        mesh=mesh,
        in_specs=(P(ALL, None),) * 2 + (P("wide", "narrow"),) * 4 + (P(ALL), P(ALL, None)),
        out_specs=(P(ALL, None),) * 2 + (P("wide", "narrow"),) * 4 + (P(ALL),),
        check_vma=False,
    )
```

```python
import functools

import jax
import jax.numpy as jnp
from jax import lax
from jax.experimental import pallas as pl
from jax.experimental.pallas import tpu as pltpu
from jax.sharding import PartitionSpec as P

D = 768
HEADS = 12
FF = 3072
TILE = 256
ALL = ("wide", "narrow")
CHIP_STEPS = ((0, 0), (1, 0), (0, 1), (1, 1))
bf16, f32 = jnp.bfloat16, jnp.float32
Shape = jax.ShapeDtypeStruct

epsilon = 1e-06


def cost(us):
    return pl.CostEstimate(flops=0 * us, bytes_accessed=0, transcendentals=0)


def params(mib=60):
    return pltpu.CompilerParams(vmem_limit_bytes=mib * 2**20)


def send(values, z=0, y=0, x=0, core=0):
    flip_wide, flip_narrow = 2 * z + y, 2 * x + core
    pairs = [
        (w * 4 + n, (w ^ flip_wide) * 4 + (n ^ flip_narrow)) for w in range(8) for n in range(4)
    ]
    return lax.ppermute(values, ALL, pairs)


def position():
    wide, narrow = lax.axis_index("wide"), lax.axis_index("narrow")
    return wide // 2, wide % 2, narrow // 2, narrow % 2


def origin():
    zero = jnp.int32(0)
    return zero, zero, zero, zero


def gather_z(values):
    return [values] + [send(values, z=k) for k in (1, 2, 3)]


def gather_chips(lines):
    return [lines] + [send(lines, x=i, y=j) for i, j in CHIP_STEPS[1:]]


def gather_cores(blocks):
    return blocks + [send(block, core=1) for block in blocks]


def pair_kernel(count, *refs):
    core = lax.rem(lax.axis_index("narrow"), 2)
    more, outs = refs[2 * count : -count], refs[-count:]
    for own, other, out in zip(refs[:count], refs[count : 2 * count], outs):
        rows, columns = own.shape[0] // 2, own.shape[1]
        half = pl.ds(pl.multiple_of(core * rows, rows), rows)

        @pl.when(core == 0)
        def _(own=own, other=other, out=out, half=half, columns=columns):
            out[:, :columns] = own[half, :]
            out[:, columns : 2 * columns] = other[half, :]

        @pl.when(core == 1)
        def _(own=own, other=other, out=out, half=half, columns=columns):
            out[:, :columns] = other[half, :]
            out[:, columns : 2 * columns] = own[half, :]

    for vector in more:
        rest, parts = vector[...], []
        for _ in range(3):
            parts.append(rest.astype(bf16).astype(f32))
            rest = rest - parts[-1]
        outs[0][:, 1152:] = rows_of(48, *parts).astype(bf16)


def pair_up(pieces, others, vectors=None):
    more = [0] * len(pieces)
    rows = ()
    if vectors is not None:
        rows = (jnp.pad(vectors, (0, 384 - vectors.shape[0])).reshape(3, 128),)
        more[0] = 128
    return pl.pallas_call(
        functools.partial(pair_kernel, len(pieces)),
        out_shape=[
            Shape((piece.shape[0] // 2, piece.shape[1] * 2 + extra), piece.dtype)
            for piece, extra in zip(pieces, more)
        ],
        cost_estimate=cost(2),
        name="pair_up",
    )(*pieces, *others, *rows)


def block_copies(place, blocks, left, out, sems):
    z, y, x, core = place()
    rows, width = blocks[0].shape[1], out.shape[1] // 2
    copies = []
    for other in range(2):
        for step, (i, j) in enumerate(CHIP_STEPS):
            for k in range(4):
                row = (((z ^ k) * 2 + (y ^ j)) * 2 + (core ^ other)) * rows
                copies.append(
                    pltpu.make_async_copy(
                        blocks[other * 4 + step].at[k, :, pl.ds(left, width)],
                        out.at[
                            pl.ds(pl.multiple_of(row, rows), rows),
                            pl.ds(pl.multiple_of((x ^ i) * width, width), width),
                        ],
                        sems.at[len(copies)],
                    )
                )
    return copies


def table_copies(table, out, sems):
    rows, columns = table.shape[1:]
    return [
        pltpu.make_async_copy(
            table.at[w * 4 + n],
            out.at[pl.ds((w * 2 + n % 2) * rows, rows), pl.ds(n // 2 * columns, columns)],
            sems.at[w * 4 + n],
        )
        for w in range(8)
        for n in range(4)
    ]


def start(copies):
    for copy in copies:
        copy.start()


def wait(copies):
    for copy in copies:
        copy.wait()


def anywhere(count):
    return [pl.BlockSpec(memory_space=pl.ANY)] * count


def split_blocks(matrix, rows, columns):
    parts = matrix.reshape(4, 2, 2, rows, 2, columns).transpose(2, 1, 4, 0, 3, 5)
    return [parts[other, j, i] for other in range(2) for i, j in CHIP_STEPS]


def place_kernel(*refs):
    z, y, x, core = position()
    out = refs[8]
    for other in range(2):
        for step, (i, j) in enumerate(CHIP_STEPS):
            for k in range(4):
                row = ((z ^ k) * 2 + (y ^ j)) * 4 + (x ^ i) * 2 + (core ^ other)
                parts = refs[other * 4 + step][k].astype(f32)
                out[row] = parts[:3] + parts[3:6] + parts[6:9]


def place_vectors(blocks):
    table = pl.pallas_call(
        place_kernel,
        grid=(1,),
        in_specs=[pl.BlockSpec((4, 16, 128), lambda i: (0, 0, 9))] * 8,
        out_specs=fixed((32, 3, 128)),
        out_shape=Shape((32, 3, 128), f32),
        cost_estimate=cost(1),
        name="place_vectors",
    )(*blocks)
    return table.reshape(32, 384)[:, :288].reshape(12, D)


def wide_sum(*terms):
    return functools.reduce(lambda a, b: a + b, [t.astype(f32) for t in terms])


def chip_parts(kept, received):
    return [wide_sum(kept[s], received[s]).astype(bf16) for s in range(4)]


def chip_kernel(*refs):
    for kept, received, out in zip(refs[:4], refs[4:8], refs[8:]):
        out[...] = wide_sum(kept[...], received[...]).astype(bf16)


def chip_parts_of(kept, received):
    rows, columns = kept[0].shape[1:]
    line = pl.BlockSpec((1, rows, columns), lambda k: (k, 0, 0))
    return pl.pallas_call(
        chip_kernel,
        grid=(4,),
        in_specs=[line] * 8,
        out_specs=[line] * 4,
        out_shape=[Shape((4, rows, columns), bf16)] * 4,
        compiler_params=params(32),
        cost_estimate=cost(3),
        name="chip_parts",
    )(*kept, *received)


def chip_sends(parts):
    return [send(parts[s], x=i, y=j) for s, (i, j) in enumerate(CHIP_STEPS) if s]


def line_kernel(far, *refs):
    terms, outs = refs[:4], refs[4:]
    for k in range(4):
        total = wide_sum(*[term[k] for term in terms]).astype(bf16)
        if far and k >= 2:
            outs[2][k - 2] = total
        else:
            outs[k][...] = total


def line_parts(own, others, far=False):
    piece = Shape(own.shape[1:], bf16)
    shapes = [piece] * 2 + [Shape((2,) + own.shape[1:], bf16)] if far else [piece] * 4
    return pl.pallas_call(
        functools.partial(line_kernel, far),
        out_shape=shapes,
        compiler_params=params(32),
        cost_estimate=cost(2),
        name="line_parts",
    )(own, *others)


def line_sends(line):
    return [send(line[k], z=k) for k in (1, 2, 3)]


def line_halves(own, others):
    *near, far = line_parts(own, others, True)
    return near, far


def near_parts(near, received):
    return [wide_sum(near[k], received[k]).astype(near[k].dtype) for k in range(2)]


def swap_columns(summed):
    core = lax.axis_index("narrow") % 2
    columns = summed.shape[1] // 2
    left, right = summed[:, :columns], summed[:, columns:]
    mine = jnp.where(core == 0, left, right)
    other = send(jnp.where(core == 0, right, left).astype(bf16), core=1).astype(f32)
    return jnp.concatenate(
        [jnp.where(core == 0, mine, other), jnp.where(core == 0, other, mine)], 0
    )


def dot(left_side, right_side):
    return jnp.dot(left_side, right_side, preferred_element_type=f32)


def dot_t(left_side, right_side):
    return lax.dot_general(
        left_side, right_side, (((1,), (1,)), ((), ())), preferred_element_type=f32
    )


def column_sum(values):
    return jnp.sum(values, 0, keepdims=True)


def normalize(values):
    center = values - jnp.mean(values, -1, keepdims=True)
    inverse = lax.rsqrt(jnp.mean(center * center, -1, keepdims=True) + epsilon)
    return center * inverse, inverse


def normalize_back(grad_norm, normed, inverse):
    return inverse * (
        grad_norm
        - jnp.mean(grad_norm, -1, keepdims=True)
        - normed * jnp.mean(grad_norm * normed, -1, keepdims=True)
    )


def smooth(values):
    density = jnp.exp(-0.5 * values * values) * 0.3989422804014327
    below = 0.5 + 0.5 * lax.erf(values * 0.7071067811865476)
    return values * below, below + values * density


def fixed(shape):
    return pl.BlockSpec(shape, lambda i: (0,) * len(shape))


def tile(columns, rows=TILE):
    return pl.BlockSpec((rows, columns), lambda i: (i, 0))


def rows_of(count, *parts):
    missing = count - sum(part.shape[0] for part in parts)
    return jnp.concatenate(list(parts) + [jnp.zeros((missing, parts[0].shape[1]), f32)], 0)


def segment_marks(segment):
    kinds = lax.broadcasted_iota(jnp.int32, (1, 64), 1)
    mark = (segment.reshape(-1, 1) == kinds).astype(bf16)
    tall = lax.broadcasted_iota(jnp.int32, (1, 64, 1), 1)
    away = (segment[:, None, :] != tall) & (tall < 4)
    return jnp.concatenate([mark, mark], 1), jnp.where(away, -(2.0**30), 0.0).astype(bf16)


def attend_kernel(place, *refs):
    hidden, vectors, key_marks, query_marks = refs[:4]
    blocks, (packed, att, att_t, probs, weight, sems) = refs[4:12], refs[12:]

    @pl.when(pl.program_id(0) == 0)
    def _():
        copies = block_copies(place, blocks, 0, weight, sems)
        start(copies)
        wait(copies)

    length = hidden.shape[0]
    for part in range(3):
        columns = slice(part * D, (part + 1) * D)
        block = dot(hidden[...], weight[:, columns])
        if part != 1:
            block = block + vectors[part // 2 : part // 2 + 1, :]
        block = block.astype(bf16)
        if part == 0:
            block = block * jnp.asarray(0.125, bf16)
        packed[:, columns] = block
    lanes = lax.broadcasted_iota(jnp.int32, (length, 128), 1)

    def pair(p, _):
        at = pl.multiple_of(p * 128, 128)
        q_t = packed[:, pl.ds(at, 128)].T
        k = packed[:, pl.ds(D + at, 128)]
        v_t = packed[:, pl.ds(2 * D + at, 128)].T
        scores = []
        for odd in range(2):
            keys = jnp.where((lanes >= 64) == bool(odd), k, key_marks[...])
            own = q_t[64 * odd : 64 * odd + 64]
            marks = query_marks[0]
            scores.append(dot(keys, jnp.concatenate([marks, own] if odd else [own, marks], 0)))
        outs = []
        for odd in range(2):
            weights = jnp.exp(scores[odd] - jnp.max(scores[odd], 0, keepdims=True))
            low = (weights * (1.0 / column_sum(weights))).astype(bf16)
            probs[p * 2 + odd] = low
            outs.append(dot(v_t[64 * odd : 64 * odd + 64], low))
        out = jnp.concatenate(outs, 0).astype(bf16)
        att_t[pl.ds(at, 128), :] = out
        att[:, pl.ds(at, 128)] = out.T
        return 0

    lax.fori_loop(0, HEADS // 2, pair, 0, unroll=True)


def attend(place, hidden, vectors, key_marks, query_marks, blocks):
    rows, length = query_marks.shape[0], query_marks.shape[2]
    tokens = rows * length
    return pl.pallas_call(
        functools.partial(attend_kernel, place),
        grid=(rows,),
        in_specs=[
            tile(D, length),
            fixed((12, D)),
            tile(128, length),
            pl.BlockSpec((1, 64, length), lambda i: (i, 0, 0)),
        ]
        + anywhere(8),
        scratch_shapes=[pltpu.VMEM((D, 3 * D), bf16), pltpu.SemaphoreType.DMA((32,))],
        out_specs=[
            tile(3 * D, length),
            tile(D, length),
            pl.BlockSpec((D, length), lambda i: (0, i)),
            pl.BlockSpec((HEADS, length, length), lambda i: (i, 0, 0)),
        ],
        out_shape=[
            Shape((tokens, 3 * D), bf16),
            Shape((tokens, D), bf16),
            Shape((D, tokens), bf16),
            Shape((rows * HEADS, length, length), bf16),
        ],
        compiler_params=params(60),
        cost_estimate=cost(20),
        name="attend",
    )(hidden, vectors, key_marks, query_marks, *blocks)


def inner_kernel(place, *refs):
    att, hidden, vectors = refs[:3]
    blocks, (first_low, normed, inverse, activated, slope) = refs[3:11], refs[11:16]
    w_in, w_out, in_sems, out_sems = refs[16:]
    first_step = pl.program_id(0) == 0

    def row(i):
        return vectors[i : i + 1, :]

    def copies_in():
        return block_copies(place, blocks, 0, w_in, in_sems)

    @pl.when(first_step)
    def _():
        copies = block_copies(place, blocks, 1536, w_out, out_sems)
        start(copies)
        start(copies_in())
        wait(copies)

    n1, r1 = normalize(hidden[...].astype(f32) + dot(att[...], w_out[...]) + row(2))
    low = (n1 * row(3) + row(4)).astype(bf16)
    first_low[...] = low
    normed[...] = n1
    inverse[...] = jnp.broadcast_to(r1, inverse.shape)

    @pl.when(first_step)
    def _():
        wait(copies_in())

    for c in range(FF // D):
        columns = slice(c * D, c * D + D)
        act, back = smooth(dot(low, w_in[:, columns]) + row(5 + c))
        activated[:, columns] = act.astype(bf16)
        slope[:, columns] = back.astype(bf16)


def inner_forward(place, att, hidden, vectors, blocks):
    tokens = hidden.shape[0]
    return pl.pallas_call(
        functools.partial(inner_kernel, place),
        grid=(tokens // TILE,),
        in_specs=[tile(D)] * 2 + [fixed((12, D))] + anywhere(8),
        out_specs=[tile(D), tile(D), tile(128), tile(FF), tile(FF)],
        out_shape=[
            Shape((tokens, D), bf16),
            Shape((tokens, D), f32),
            Shape((tokens, 128), f32),
            Shape((tokens, FF), bf16),
            Shape((tokens, FF), bf16),
        ],
        scratch_shapes=[
            pltpu.VMEM((D, FF), bf16),
            pltpu.VMEM((D, D), bf16),
            pltpu.SemaphoreType.DMA((32,)),
            pltpu.SemaphoreType.DMA((32,)),
        ],
        compiler_params=params(60),
        cost_estimate=cost(16),
        name="inner_forward",
    )(att, hidden, vectors, *blocks)


def outer_kernel(place, *refs):
    act, normed, cotangent, vectors, back_table = refs[:5]
    output, grad_second, sums = refs[5:8]
    outs, (w_back, activated, grad_t, sems) = refs[8:16], refs[16:]
    step = pl.program_id(0)
    z, y, x, core = place()

    def row(i):
        return vectors[i : i + 1, :]

    @pl.when(step == 0)
    def _():
        copies = table_copies(back_table, w_back, sems)
        start(copies)
        wait(copies)

    here = pl.ds(pl.multiple_of(step * TILE, TILE), TILE)
    activated[here, :] = act[...]
    outward = normed[...] * row(3) + row(4) + dot(act[...], w_back[...]) + row(9)
    n2, r2 = normalize(outward)
    output[...] = (n2 * row(10) + row(11)).astype(bf16)
    cot = cotangent[...].astype(f32)
    g2 = normalize_back(cot * row(10), n2, r2)
    grad_second[...] = g2
    part = rows_of(8, column_sum(g2), column_sum(cot * n2), column_sum(cot))

    @pl.when(step == 0)
    def _():
        sums[...] = part

    @pl.when(step > 0)
    def _():
        sums[...] += part

    g2_t = g2.astype(bf16).T
    for n in range(4):
        at = ((n % 2) ^ core) * 2 + ((n // 2) ^ x)
        piece = g2_t[n * 192 : n * 192 + 192]
        grad_t[pl.ds(pl.multiple_of(at * 192, 192), 192), here] = piece

    @pl.when(step == pl.num_programs(0) - 1)
    def _():
        for k in range(4):
            columns = pl.ds(pl.multiple_of((z ^ k) * D, D), D)
            res = dot(grad_t[...], activated[:, columns]).astype(bf16)
            for other in range(2):
                for i in range(2):
                    at = (other * 2 + i) * 192
                    pieces = [res[at : at + 192, half * 384 : half * 384 + 384] for half in range(2)]
                    for bit in range(2):

                        @pl.when(y == bit)
                        def _(other=other, i=i, k=k, pieces=pieces, bit=bit):
                            outs[other * 4 + i][k] = pieces[bit]
                            outs[other * 4 + i + 2][k] = pieces[1 - bit]


def outer_forward(place, activated, normed, cotangent, vectors, back_table):
    tokens = normed.shape[0]
    return pl.pallas_call(
        functools.partial(outer_kernel, place),
        grid=(tokens // TILE,),
        in_specs=[tile(FF), tile(D), tile(D), fixed((12, D))] + anywhere(1),
        out_specs=[tile(D), tile(D), fixed((8, D))] + [fixed((4, 192, 384))] * 8,
        out_shape=[
            Shape((tokens, D), bf16),
            Shape((tokens, D), f32),
            Shape((8, D), f32),
        ]
        + [Shape((4, 192, 384), bf16)] * 8,
        scratch_shapes=[
            pltpu.VMEM((FF, D), bf16),
            pltpu.VMEM((tokens, FF), bf16),
            pltpu.VMEM((D, tokens), bf16),
            pltpu.SemaphoreType.DMA((32,)),
        ],
        compiler_params=params(60),
        cost_estimate=cost(18),
        name="outer_forward",
    )(activated, normed, cotangent, vectors, back_table)


def backward_kernel(place, *refs):
    grad_second, slope, normed, inverse, first_low, att_t, vectors = refs[:7]
    blocks, back_table = refs[7:15], refs[15]
    grad_att, grad_branch, sums, sums_inner, kept, sent = refs[16:22]
    w_in, w_out, w_back, inner_low, first_t, grad_low, turned = refs[22:29]
    in_sems, out_sems, back_sems = refs[29:]
    step = pl.program_id(0)
    z, y, x, core = place()
    here = pl.ds(pl.multiple_of(step * TILE, TILE), TILE)

    def compute(first_step):
        if first_step:
            copies_back = table_copies(back_table, w_back, back_sems)
            copies_in = block_copies(place, blocks, 0, w_in, in_sems)
            copies_out = block_copies(place, blocks, 1536, w_out, out_sems)
            start(copies_back)
            start(copies_in)
            start(copies_out)
        g2 = grad_second[...]
        g2_low = g2.astype(bf16)
        grad_first = g2
        inner_sums = []
        for c in range(FF // D):
            columns = slice(c * D, c * D + D)
            if first_step:
                wait(copies_back[c * 8 : c * 8 + 8])
            gi = dot_t(g2_low, w_back[columns, :]) * slope[:, columns].astype(f32)
            inner_sums.append(column_sum(gi))
            gi = gi.astype(bf16)
            inner_low[here, columns] = gi
            if first_step and c == 0:
                wait(copies_in)
            grad_first = grad_first + dot_t(gi, w_in[:, columns])
        n1 = normed[...]
        g1 = normalize_back(grad_first * vectors[3:4, :], n1, inverse[:, :1])
        grad_branch[...] = g1
        g1_low = g1.astype(bf16)
        grad_low[here, :] = g1_low
        if first_step:
            wait(copies_out)
        grad_att[...] = dot_t(g1_low, w_out[...]).astype(bf16)
        part = rows_of(8, column_sum(g1), column_sum(grad_first * n1), column_sum(grad_first))
        part_inner = rows_of(8, *inner_sums)
        if first_step:
            sums[...] = part
            sums_inner[...] = part_inner
        else:
            sums[...] += part
            sums_inner[...] += part_inner
        low_t = first_low[...].T
        for w in range(8):
            at = ((w % 2) ^ y) * 4 + ((w // 2) ^ z)
            piece = low_t[w * 96 : w * 96 + 96]
            first_t[pl.ds(pl.multiple_of(at * 96, 96), 96), here] = piece
        turn_rows(place, att_t, turned, here)

    @pl.when(step == 0)
    def _():
        compute(True)

    @pl.when(step > 0)
    def _():
        compute(False)

    @pl.when(step == pl.num_programs(0) - 1)
    def _():
        for i in range(2):
            for other, out in enumerate((kept, sent)):
                at = ((x ^ i) * 2 + (core ^ other)) * D
                res = dot(first_t[...], inner_low[:, pl.ds(pl.multiple_of(at, D), D)])
                res = res.astype(bf16)
                for j in range(2):
                    for k in range(4):
                        at = (j * 4 + k) * 96
                        out[i + 2 * j, k, :, :D] = res[at : at + 48]
                        out[i + 2 * j, k, :, D : 2 * D] = res[at + 48 : at + 96]
        res = dot(turned[...], grad_low[...]).astype(bf16)
        for other, out in enumerate((kept, sent)):
            for j in range(2):
                for k in range(4):
                    at = (other * 8 + j * 4 + k) * 48
                    for half in range(2):
                        piece = res[at : at + 48, half * 384 : half * 384 + 384]
                        out[(half ^ x) + 2 * j, k, :, 2 * D :] = piece


def backward(place, grad_second, slope, normed, inverse, first_low, att_t, vectors, *weights):
    blocks, back_table = weights
    tokens = normed.shape[0]
    outs = [(4, 4, 48, 1920)] * 2
    return pl.pallas_call(
        functools.partial(backward_kernel, place),
        grid=(tokens // TILE,),
        in_specs=[tile(D), tile(FF), tile(D), tile(128), tile(D)]
        + [pl.BlockSpec((D, TILE), lambda i: (0, i)), fixed((12, D))]
        + anywhere(9),
        out_specs=[tile(D), tile(D)] + [fixed(s) for s in [(8, D)] * 2 + outs],
        out_shape=[Shape((tokens, D), bf16), Shape((tokens, D), f32)]
        + [Shape((8, D), f32)] * 2
        + [Shape(s, bf16) for s in outs],
        scratch_shapes=[
            pltpu.VMEM((D, FF), bf16),
            pltpu.VMEM((D, D), bf16),
            pltpu.VMEM((FF, D), bf16),
            pltpu.VMEM((tokens, FF), bf16),
            pltpu.VMEM((D, tokens), bf16),
            pltpu.VMEM((tokens, D), bf16),
            pltpu.VMEM((D, tokens), bf16),
        ]
        + [pltpu.SemaphoreType.DMA((32,))] * 3,
        compiler_params=params(32),
        cost_estimate=cost(22),
        name="backward",
    )(grad_second, slope, normed, inverse, first_low, att_t, vectors, *blocks, back_table)


def turn_rows(place, source, turned, columns=slice(None)):
    z, y, _, core = place()
    for w in range(8):
        for half in range(2):
            at = (half ^ core) * 8 + ((w % 2) ^ y) * 4 + ((w // 2) ^ z)
            piece = (w * 2 + half) * 48
            rows = pl.ds(pl.multiple_of(at * 48, 48), 48)
            turned[rows, columns] = source[piece : piece + 48, :]


def attend_back_kernel(packed, grad_att, probs, grad_low, sums):
    length = packed.shape[0]
    lanes = lax.broadcasted_iota(jnp.int32, (length, 128), 1)
    zero = jnp.zeros((length, 128), bf16)
    blank = jnp.zeros((64, length), bf16)

    def pair(p, _):
        at = pl.multiple_of(p * 128, 128)
        q = packed[:, pl.ds(at, 128)]
        k_t = packed[:, pl.ds(D + at, 128)].T
        v = packed[:, pl.ds(2 * D + at, 128)]
        g = grad_att[:, pl.ds(at, 128)]
        g_t = g.T
        grad_probs = []
        for odd in range(2):
            own = g_t[64 * odd : 64 * odd + 64]
            grad_probs.append(dot(v, jnp.concatenate([blank, own] if odd else [own, blank], 0)))
        dk = dv = 0.0
        dq_t = []
        for odd in range(2):
            mine = (lanes >= 64) == bool(odd)
            low = probs[p * 2 + odd]
            wide = low.astype(f32)
            gp = grad_probs[odd]
            ds = (wide * (gp - column_sum(wide * gp))).astype(bf16)
            dv = dv + dot(low, jnp.where(mine, g, zero))
            dk = dk + dot(ds, jnp.where(mine, q, zero))
            dq_t.append(dot(k_t[64 * odd : 64 * odd + 64], ds))
        dq = jnp.concatenate(dq_t, 0).T * 0.125
        sums[0, :, pl.ds(at, 128)] = rows_of(8, column_sum(dq), column_sum(dv))
        grad_low[:, pl.ds(at, 128)] = dq.astype(bf16)
        grad_low[:, pl.ds(D + at, 128)] = dk.astype(bf16)
        grad_low[:, pl.ds(2 * D + at, 128)] = dv.astype(bf16)
        return 0

    lax.fori_loop(0, HEADS // 2, pair, 0, unroll=True)


def attend_back(row, packed, grad_att, probs, low=None):
    length = probs.shape[1]
    kernel, more, specs, alias = attend_back_kernel, (), [], {}
    if low is not None:
        more, specs, alias = (low,), [pl.BlockSpec(memory_space=pl.ANY)], {3: 0}

        def kernel(packed, grad_att, probs, low, grad_low, sums):
            attend_back_kernel(packed, grad_att, probs, grad_low, sums)

    return pl.pallas_call(
        kernel,
        grid=(1,),
        in_specs=[
            pl.BlockSpec((length, 3 * D), lambda i: (row, 0)),
            pl.BlockSpec((length, D), lambda i: (row, 0)),
            pl.BlockSpec((HEADS, length, length), lambda i: (row, 0, 0)),
        ]
        + specs,
        out_specs=[
            pl.BlockSpec((length, 3 * D), lambda i: (row, 0)),
            pl.BlockSpec((1, 8, D), lambda i: (0, 0, 0)),
        ],
        out_shape=[Shape(packed.shape, bf16), Shape((1, 8, D), f32)],
        input_output_aliases=alias,
        compiler_params=params(32),
        cost_estimate=cost(12),
        name="attend_back",
    )(packed, grad_att, probs, *more)


def grad_qkv_kernel(place, hidden, low, *refs):
    sums_zero, sums_one, sums_first, sums_inner, sums_second = refs[:5]
    outs, turned, groups = refs[5:13], refs[13], refs[14]
    z, y, x, core = place()
    turn_rows(place, hidden[...].T, turned)
    rows = [sums_zero[0, i : i + 1, :] + sums_one[0, i : i + 1, :] for i in range(2)]
    rows += [sums_first[i : i + 1, :] for i in range(3)]
    rows += [sums_inner[i : i + 1, :] for i in range(4)]
    rows += [sums_second[i : i + 1, :] for i in range(3)]
    for group in range(72):
        column = group % 6 * 128
        groups[group] = rows[group // 6][:, column : column + 128]
    for group in range(72, 76):
        groups[group] = jnp.zeros((1, 128), f32)
    for i in range(2):
        columns = pl.ds(pl.multiple_of((x ^ i) * 1152, 128), 1152)
        res = dot(turned[...], low[:, columns]).astype(bf16)
        for other in range(2):
            for j in range(2):
                out = outs[other * 4 + i + 2 * j]
                for k in range(4):
                    at = (other * 8 + j * 4 + k) * 48
                    out[k, :, :1152] = res[at : at + 48]
                    device = ((z ^ k) * 2 + (y ^ j)) * 4 + (x ^ i) * 2 + (core ^ other)
                    group = (9 * device) // 4
                    part = jnp.concatenate([groups[group + q] for q in range(4)], 0)
                    out[k, :16, 1152:] = rows_of(16, part).astype(bf16)
                    out[k, 16:, 1152:] = jnp.zeros((32, 128), bf16)


def grad_qkv(place, hidden, low, *sums):
    return pl.pallas_call(
        functools.partial(grad_qkv_kernel, place),
        out_shape=[Shape((4, 48, 1280), bf16)] * 8,
        scratch_shapes=[pltpu.VMEM((D, hidden.shape[0]), bf16), pltpu.VMEM((80, 1, 128), f32)],
        compiler_params=params(32),
        cost_estimate=cost(9),
        name="grad_qkv",
    )(hidden, low, *sums)


def cut_vectors(place, groups):
    z, y, x, core = place()
    at = (((z * 2 + y) * 4 + x * 2 + core) * 288) % 128
    return lax.dynamic_slice(groups.reshape(-1), (at,), (288,))


def hidden_kernel(place, *refs):
    low, grad_branch, blocks, out, weight, sems = *refs[:2], refs[2:10], *refs[10:]

    @pl.when(pl.program_id(0) == 0)
    def _():
        copies = block_copies(place, blocks, 0, weight, sems)
        start(copies)
        wait(copies)

    out[...] = grad_branch[...] + dot_t(low[...], weight[...])


def grad_of_hidden(place, low, grad_branch, blocks):
    tokens = low.shape[0]
    return pl.pallas_call(
        functools.partial(hidden_kernel, place),
        grid=(tokens // TILE,),
        in_specs=[tile(3 * D), tile(D)] + anywhere(8),
        out_specs=tile(D),
        out_shape=Shape((tokens, D), f32),
        scratch_shapes=[pltpu.VMEM((D, 3 * D), bf16), pltpu.SemaphoreType.DMA((32,))],
        compiler_params=params(32),
        cost_estimate=cost(9),
        name="grad_hidden",
    )(low, grad_branch, *blocks)


def gather_plain(w_qkv, w_out, w_in, w_back, vectors):
    def whole(piece):
        return lax.all_gather(
            lax.all_gather(piece, "narrow", axis=1, tiled=True), "wide", axis=0, tiled=True
        )

    full = tuple(whole(piece) for piece in (w_qkv, w_out, w_in, w_back))
    return full + (lax.all_gather(vectors, ALL, axis=0, tiled=True).reshape(12, D),)


def tie(*values):
    return lax.optimization_barrier(values)


def unfold(table, order, shape):
    return table.reshape((2, 2, 2, 4) + table.shape[3:]).transpose(order).reshape(shape)


def scatter_whole(matrix):
    part = lax.psum_scatter(matrix, "wide", scatter_dimension=0, tiled=True)
    part = lax.psum_scatter(part, "narrow", scatter_dimension=1, tiled=True)
    return part.astype(f32)


def per_device(hidden, segment, w_qkv, w_out, w_in, w_back, vectors, cotangent):
    (qkv,) = pair_up([w_qkv], [send(w_qkv, core=1)], vectors)
    rest = [w_out, w_in, w_back]
    other_rest = [send(piece, core=1) for piece in rest]
    qkv, other_rest, segment = tie(qkv, other_rest, segment)
    key_marks, query_marks = segment_marks(segment)
    qkv_line = gather_z(qkv)
    out, inner, back = pair_up(rest, other_rest)
    mid = jnp.concatenate([inner, out], 1)
    qkv_line, mid, back, key_marks, query_marks = tie(
        jnp.stack(qkv_line), mid, back, key_marks, query_marks
    )

    qkv_blocks = gather_chips(qkv_line)
    mid_line = gather_z(mid)
    qkv_blocks, mid_line, back = tie(qkv_blocks, mid_line, back)

    back_table = lax.all_gather(back, ALL, axis=0, tiled=False)
    mid_blocks = gather_chips(jnp.stack(mid_line))
    qkv_blocks = gather_cores(qkv_blocks)
    all_vectors = place_vectors(qkv_blocks)
    attended = attend(position, hidden, all_vectors, key_marks, query_marks, qkv_blocks)
    attended, mid_blocks = tie(attended, mid_blocks)
    packed, att, att_t, probs = attended

    mid_blocks = gather_cores(mid_blocks)
    inner_outs = inner_forward(position, att, hidden, all_vectors, mid_blocks)
    inner_outs, back_table = tie(inner_outs, back_table)
    first_low, normed, inverse, activated, slope = inner_outs

    output, grad_second, sums_second, *tables_back = outer_forward(
        position, activated, normed, cotangent, all_vectors, back_table
    )

    received_back = [send(block, core=1) for block in tables_back[4:]]
    parts_back = chip_parts(tables_back[:4], received_back)
    parts_back, grad_second = tie(parts_back, grad_second)
    others_back = chip_sends(parts_back)
    back_outs = backward(
        position,
        grad_second,
        slope,
        normed,
        inverse,
        first_low,
        att_t,
        all_vectors,
        mid_blocks,
        back_table,
    )
    back_outs, others_back = tie(back_outs, others_back)
    grad_att, grad_branch, sums_first, sums_inner, kept_mid, sent_mid = back_outs

    received_mid = send(sent_mid, core=1)
    near_back, far_back = line_halves(parts_back[0], others_back)
    parts_mid = chip_parts(kept_mid, received_mid)
    parts_mid, grad_att, near_back, far_back = tie(parts_mid, grad_att, near_back, far_back)

    plane_mid = [send(parts_mid[1], x=1), send(parts_mid[2], y=1)]
    corner_mid = send(parts_mid[3], x=1, y=1)
    far_back = send(far_back, z=2)
    packed_low, sums_zero = attend_back(0, packed, grad_att, probs)
    packed_low, sums_one = attend_back(1, packed, grad_att, probs, packed_low)
    tables_qkv = grad_qkv(
        position, hidden, packed_low, sums_zero, sums_one, sums_first, sums_inner, sums_second
    )
    tables_qkv, far_back, plane_mid = tie(tables_qkv, far_back, plane_mid)
    kept_qkv, sent_qkv = tables_qkv[:4], tables_qkv[4:]

    received_qkv = [send(block, core=1) for block in sent_qkv]
    parts_qkv = chip_parts_of(kept_qkv, received_qkv)
    parts_qkv, grad_branch, near_back, corner_mid = tie(
        parts_qkv, grad_branch, near_back, corner_mid
    )
    others_qkv = chip_sends(parts_qkv)
    near_mid, far_mid = line_halves(parts_mid[0], plane_mid + [corner_mid])
    far_mid = send(far_mid, z=2)
    near_back = near_parts(near_back, far_back)
    next_back = send(near_back[1], z=1)
    near_back, grad_branch = tie(near_back, grad_branch)
    grad_hidden = grad_of_hidden(position, packed_low, grad_branch, qkv_blocks)
    grad_hidden, far_mid, next_back = tie(grad_hidden, far_mid, next_back)

    own_back = wide_sum(near_back[0], next_back).T
    near_mid = near_parts(near_mid, far_mid)
    next_mid = send(near_mid[1], z=1)
    others_qkv, near_mid = tie(others_qkv, near_mid)
    line_qkv = line_parts(parts_qkv[0], others_qkv)
    lines_qkv = line_sends(line_qkv)
    own_mid = wide_sum(near_mid[0], next_mid)
    own_in = jnp.concatenate([own_mid[:, :D], own_mid[:, D : 2 * D]], 0)
    own_out = swap_columns(own_mid[:, 2 * D :])
    own_in, own_out, own_back, lines_qkv = tie(own_in, own_out, own_back, lines_qkv)
    own_qkv = wide_sum(line_qkv[0], *lines_qkv)
    own_vectors = cut_vectors(position, own_qkv[:4, 1152:])
    own_qkv = swap_columns(own_qkv[:, :1152])
    return (output, grad_hidden, own_qkv, own_out, own_in, own_back, own_vectors)


def per_device_plain(hidden, segment, w_qkv, w_out, w_in, w_back, vectors, cotangent):
    key_marks, query_marks = segment_marks(segment)
    full_qkv, full_out, full_in, full_back, all_vectors = gather_plain(
        w_qkv, w_out, w_in, w_back, vectors
    )
    qkv_blocks = split_blocks(full_qkv, 48, 1152)
    mid_blocks = [
        jnp.concatenate(pair, 2)
        for pair in zip(split_blocks(full_in, 48, 1536), split_blocks(full_out, 48, 384))
    ]
    back_pieces = full_back.reshape(8, 2, 192, 2, 384).transpose(0, 3, 1, 2, 4)
    back_pieces = back_pieces.reshape(32, 192, 384)
    packed, att, att_t, probs = attend(
        origin, hidden, all_vectors, key_marks, query_marks, qkv_blocks
    )
    first_low, normed, inverse, activated, slope = inner_forward(
        origin, att, hidden, all_vectors, mid_blocks
    )
    output, grad_second, sums_second, *back_table = outer_forward(
        origin, activated, normed, cotangent, all_vectors, back_pieces
    )
    grad_att, grad_branch, sums_first, sums_inner, *tables = backward(
        origin,
        grad_second,
        slope,
        normed,
        inverse,
        first_low,
        att_t,
        all_vectors,
        mid_blocks,
        back_pieces,
    )
    mid_table = jnp.stack(tables)
    packed_low, sums_zero = attend_back(0, packed, grad_att, probs)
    packed_low, sums_one = attend_back(1, packed, grad_att, probs, packed_low)
    grad_hidden = grad_of_hidden(origin, packed_low, grad_branch, qkv_blocks)
    tables = grad_qkv(
        origin, hidden, packed_low, sums_zero, sums_one, sums_first, sums_inner, sums_second
    )
    grad_vectors = jnp.concatenate(
        [(sums_zero + sums_one)[0, :2], sums_first[:3], sums_inner[:4], sums_second[:3]], 0
    )
    qkv_table = jnp.stack(tables)
    qkv_table = qkv_table.reshape(2, 4, 4, 48, 1280)
    halves = jnp.stack([mid_table[..., :D], mid_table[..., D : 2 * D]], 4)
    own_qkv = scatter_whole(unfold(qkv_table[..., :1152], (3, 1, 0, 4, 2, 5), (D, 3 * D)))
    own_out = scatter_whole(unfold(mid_table[..., 2 * D :], (3, 1, 0, 4, 2, 5), (D, D)))
    own_in = scatter_whole(unfold(halves, (3, 1, 4, 5, 2, 0, 6), (D, FF)))
    back_table = jnp.stack(back_table).reshape(2, 4, 4, 192, 384)
    back_t = unfold(back_table, (2, 0, 4, 3, 1, 5), (D, FF))
    own_back = scatter_whole(back_t.T)
    own_vectors = lax.psum_scatter(
        grad_vectors.reshape(-1), ALL, scatter_dimension=0, tiled=True
    )
    return (output, grad_hidden, own_qkv, own_out, own_in, own_back, own_vectors)


def solution(mesh):
    trees = mesh.shape["wide"] == 8 and mesh.shape["narrow"] == 4
    return jax.shard_map(
        per_device if trees else per_device_plain,
        mesh=mesh,
        in_specs=(P(ALL, None),) * 2 + (P("wide", "narrow"),) * 4 + (P(ALL), P(ALL, None)),
        out_specs=(P(ALL, None),) * 2 + (P("wide", "narrow"),) * 4 + (P(ALL),),
        check_vma=False,
    )
```

```python
import functools

import jax
import jax.numpy as jnp
from jax import lax
from jax.experimental import pallas as pl
from jax.experimental.pallas import tpu as pltpu
from jax.sharding import PartitionSpec as P

D = 768
HEADS = 12
FF = 3072
TILE = 256
ALL = ("wide", "narrow")
CHIP_STEPS = ((0, 0), (1, 0), (0, 1), (1, 1))
bf16, f32 = jnp.bfloat16, jnp.float32
Shape = jax.ShapeDtypeStruct

epsilon = 1e-06


def cost(us):
    return pl.CostEstimate(flops=0 * us, bytes_accessed=0, transcendentals=0)


def params(mib=60):
    return pltpu.CompilerParams(vmem_limit_bytes=mib * 2**20)


def send(values, z=0, y=0, x=0, core=0):
    flip_wide, flip_narrow = 2 * z + y, 2 * x + core
    pairs = [
        (w * 4 + n, (w ^ flip_wide) * 4 + (n ^ flip_narrow)) for w in range(8) for n in range(4)
    ]
    return lax.ppermute(values, ALL, pairs)


def position():
    wide, narrow = lax.axis_index("wide"), lax.axis_index("narrow")
    return wide // 2, wide % 2, narrow // 2, narrow % 2


def origin():
    zero = jnp.int32(0)
    return zero, zero, zero, zero


def gather_z(values):
    return [values] + [send(values, z=k) for k in (1, 2, 3)]


def gather_chips(lines):
    return [lines] + [send(lines, x=i, y=j) for i, j in CHIP_STEPS[1:]]


def gather_cores(blocks):
    return blocks + [send(block, core=1) for block in blocks]


def pair_kernel(count, *refs):
    core = lax.rem(lax.axis_index("narrow"), 2)
    more, outs = refs[2 * count : -count], refs[-count:]
    for own, other, out in zip(refs[:count], refs[count : 2 * count], outs):
        rows, columns = own.shape[0] // 2, own.shape[1]
        half = pl.ds(pl.multiple_of(core * rows, rows), rows)

        @pl.when(core == 0)
        def _(own=own, other=other, out=out, half=half, columns=columns):
            out[:, :columns] = own[half, :]
            out[:, columns : 2 * columns] = other[half, :]

        @pl.when(core == 1)
        def _(own=own, other=other, out=out, half=half, columns=columns):
            out[:, :columns] = other[half, :]
            out[:, columns : 2 * columns] = own[half, :]

    for vector in more:
        rest, parts = vector[...], []
        for _ in range(3):
            parts.append(rest.astype(bf16).astype(f32))
            rest = rest - parts[-1]
        outs[0][:, 1152:] = rows_of(48, *parts).astype(bf16)


def pair_up(pieces, others, vectors=None):
    more = [0] * len(pieces)
    rows = ()
    if vectors is not None:
        rows = (jnp.pad(vectors, (0, 384 - vectors.shape[0])).reshape(3, 128),)
        more[0] = 128
    return pl.pallas_call(
        functools.partial(pair_kernel, len(pieces)),
        out_shape=[
            Shape((piece.shape[0] // 2, piece.shape[1] * 2 + extra), piece.dtype)
            for piece, extra in zip(pieces, more)
        ],
        cost_estimate=cost(2),
        name="pair_up",
    )(*pieces, *others, *rows)


def block_copies(place, blocks, left, out, sems):
    z, y, x, core = place()
    rows, width = blocks[0].shape[1], out.shape[1] // 2
    copies = []
    for other in range(2):
        for step, (i, j) in enumerate(CHIP_STEPS):
            for k in range(4):
                row = (((z ^ k) * 2 + (y ^ j)) * 2 + (core ^ other)) * rows
                copies.append(
                    pltpu.make_async_copy(
                        blocks[other * 4 + step].at[k, :, pl.ds(left, width)],
                        out.at[
                            pl.ds(pl.multiple_of(row, rows), rows),
                            pl.ds(pl.multiple_of((x ^ i) * width, width), width),
                        ],
                        sems.at[len(copies)],
                    )
                )
    return copies


def table_copies(table, out, sems):
    rows, columns = table.shape[1:]
    return [
        pltpu.make_async_copy(
            table.at[w * 4 + n],
            out.at[pl.ds((w * 2 + n % 2) * rows, rows), pl.ds(n // 2 * columns, columns)],
            sems.at[w * 4 + n],
        )
        for w in range(8)
        for n in range(4)
    ]


def start(copies):
    for copy in copies:
        copy.start()


def wait(copies):
    for copy in copies:
        copy.wait()


def anywhere(count):
    return [pl.BlockSpec(memory_space=pl.ANY)] * count


def split_blocks(matrix, rows, columns):
    parts = matrix.reshape(4, 2, 2, rows, 2, columns).transpose(2, 1, 4, 0, 3, 5)
    return [parts[other, j, i] for other in range(2) for i, j in CHIP_STEPS]


def place_kernel(*refs):
    z, y, x, core = position()
    out = refs[8]
    for other in range(2):
        for step, (i, j) in enumerate(CHIP_STEPS):
            for k in range(4):
                row = ((z ^ k) * 2 + (y ^ j)) * 4 + (x ^ i) * 2 + (core ^ other)
                parts = refs[other * 4 + step][k].astype(f32)
                out[row] = parts[:3] + parts[3:6] + parts[6:9]


def place_vectors(blocks):
    table = pl.pallas_call(
        place_kernel,
        grid=(1,),
        in_specs=[pl.BlockSpec((4, 16, 128), lambda i: (0, 0, 9))] * 8,
        out_specs=fixed((32, 3, 128)),
        out_shape=Shape((32, 3, 128), f32),
        cost_estimate=cost(1),
        name="place_vectors",
    )(*blocks)
    return table.reshape(32, 384)[:, :288].reshape(12, D)


def wide_sum(*terms):
    return functools.reduce(lambda a, b: a + b, [t.astype(f32) for t in terms])


def chip_parts(kept, received):
    return [wide_sum(kept[s], received[s]).astype(bf16) for s in range(4)]


def chip_kernel(*refs):
    for kept, received, out in zip(refs[:4], refs[4:8], refs[8:]):
        out[...] = wide_sum(kept[...], received[...]).astype(bf16)


def chip_parts_of(kept, received):
    rows, columns = kept[0].shape[1:]
    line = pl.BlockSpec((1, rows, columns), lambda k: (k, 0, 0))
    return pl.pallas_call(
        chip_kernel,
        grid=(4,),
        in_specs=[line] * 8,
        out_specs=[line] * 4,
        out_shape=[Shape((4, rows, columns), bf16)] * 4,
        compiler_params=params(32),
        cost_estimate=cost(3),
        name="chip_parts",
    )(*kept, *received)


def chip_sends(parts):
    return [send(parts[s], x=i, y=j) for s, (i, j) in enumerate(CHIP_STEPS) if s]


def line_kernel(far, *refs):
    terms, outs = refs[:4], refs[4:]
    for k in range(4):
        total = wide_sum(*[term[k] for term in terms]).astype(bf16)
        if far and k >= 2:
            outs[2][k - 2] = total
        else:
            outs[k][...] = total


def line_parts(own, others, far=False):
    piece = Shape(own.shape[1:], bf16)
    shapes = [piece] * 2 + [Shape((2,) + own.shape[1:], bf16)] if far else [piece] * 4
    return pl.pallas_call(
        functools.partial(line_kernel, far),
        out_shape=shapes,
        compiler_params=params(32),
        cost_estimate=cost(2),
        name="line_parts",
    )(own, *others)


def line_sends(line):
    return [send(line[k], z=k) for k in (1, 2, 3)]


def line_halves(own, others):
    *near, far = line_parts(own, others, True)
    return near, far


def near_parts(near, received):
    return [wide_sum(near[k], received[k]).astype(near[k].dtype) for k in range(2)]


def swap_columns(summed):
    core = lax.axis_index("narrow") % 2
    columns = summed.shape[1] // 2
    left, right = summed[:, :columns], summed[:, columns:]
    mine = jnp.where(core == 0, left, right)
    other = send(jnp.where(core == 0, right, left).astype(bf16), core=1).astype(f32)
    return jnp.concatenate(
        [jnp.where(core == 0, mine, other), jnp.where(core == 0, other, mine)], 0
    )


def dot(left_side, right_side):
    return jnp.dot(left_side, right_side, preferred_element_type=f32)


def dot_t(left_side, right_side):
    return lax.dot_general(
        left_side, right_side, (((1,), (1,)), ((), ())), preferred_element_type=f32
    )


def column_sum(values):
    return jnp.sum(values, 0, keepdims=True)


def normalize(values):
    center = values - jnp.mean(values, -1, keepdims=True)
    inverse = lax.rsqrt(jnp.mean(center * center, -1, keepdims=True) + epsilon)
    return center * inverse, inverse


def normalize_back(grad_norm, normed, inverse):
    return inverse * (
        grad_norm
        - jnp.mean(grad_norm, -1, keepdims=True)
        - normed * jnp.mean(grad_norm * normed, -1, keepdims=True)
    )


def smooth(values):
    density = jnp.exp(-0.5 * values * values) * 0.3989422804014327
    below = 0.5 + 0.5 * lax.erf(values * 0.7071067811865476)
    return values * below, below + values * density


def fixed(shape):
    return pl.BlockSpec(shape, lambda i: (0,) * len(shape))


def tile(columns, rows=TILE):
    return pl.BlockSpec((rows, columns), lambda i: (i, 0))


def rows_of(count, *parts):
    missing = count - sum(part.shape[0] for part in parts)
    return jnp.concatenate(list(parts) + [jnp.zeros((missing, parts[0].shape[1]), f32)], 0)


def segment_marks(segment):
    kinds = lax.broadcasted_iota(jnp.int32, (1, 64), 1)
    mark = (segment.reshape(-1, 1) == kinds).astype(bf16)
    tall = lax.broadcasted_iota(jnp.int32, (1, 64, 1), 1)
    away = (segment[:, None, :] != tall) & (tall < 4)
    return jnp.concatenate([mark, mark], 1), jnp.where(away, -(2.0**30), 0.0).astype(bf16)


def attend_kernel(place, *refs):
    hidden, vectors, key_marks, query_marks = refs[:4]
    blocks, (packed, att, att_t, probs, weight, sems) = refs[4:12], refs[12:]

    @pl.when(pl.program_id(0) == 0)
    def _():
        copies = block_copies(place, blocks, 0, weight, sems)
        start(copies)
        wait(copies)

    length = hidden.shape[0]
    for part in range(3):
        columns = slice(part * D, (part + 1) * D)
        block = dot(hidden[...], weight[:, columns])
        if part != 1:
            block = block + vectors[part // 2 : part // 2 + 1, :]
        block = block.astype(bf16)
        if part == 0:
            block = block * jnp.asarray(0.125, bf16)
        packed[:, columns] = block
    lanes = lax.broadcasted_iota(jnp.int32, (length, 128), 1)

    def pair(p, _):
        at = pl.multiple_of(p * 128, 128)
        q_t = packed[:, pl.ds(at, 128)].T
        k = packed[:, pl.ds(D + at, 128)]
        v_t = packed[:, pl.ds(2 * D + at, 128)].T
        scores = []
        for odd in range(2):
            keys = jnp.where((lanes >= 64) == bool(odd), k, key_marks[...])
            own = q_t[64 * odd : 64 * odd + 64]
            marks = query_marks[0]
            scores.append(dot(keys, jnp.concatenate([marks, own] if odd else [own, marks], 0)))
        outs = []
        for odd in range(2):
            weights = jnp.exp(scores[odd] - jnp.max(scores[odd], 0, keepdims=True))
            low = (weights * (1.0 / column_sum(weights))).astype(bf16)
            probs[p * 2 + odd] = low
            outs.append(dot(v_t[64 * odd : 64 * odd + 64], low))
        out = jnp.concatenate(outs, 0).astype(bf16)
        att_t[pl.ds(at, 128), :] = out
        att[:, pl.ds(at, 128)] = out.T
        return 0

    lax.fori_loop(0, HEADS // 2, pair, 0, unroll=True)


def attend(place, hidden, vectors, key_marks, query_marks, blocks):
    rows, length = query_marks.shape[0], query_marks.shape[2]
    tokens = rows * length
    return pl.pallas_call(
        functools.partial(attend_kernel, place),
        grid=(rows,),
        in_specs=[
            tile(D, length),
            fixed((12, D)),
            tile(128, length),
            pl.BlockSpec((1, 64, length), lambda i: (i, 0, 0)),
        ]
        + anywhere(8),
        scratch_shapes=[pltpu.VMEM((D, 3 * D), bf16), pltpu.SemaphoreType.DMA((32,))],
        out_specs=[
            tile(3 * D, length),
            tile(D, length),
            pl.BlockSpec((D, length), lambda i: (0, i)),
            pl.BlockSpec((HEADS, length, length), lambda i: (i, 0, 0)),
        ],
        out_shape=[
            Shape((tokens, 3 * D), bf16),
            Shape((tokens, D), bf16),
            Shape((D, tokens), bf16),
            Shape((rows * HEADS, length, length), bf16),
        ],
        compiler_params=params(60),
        cost_estimate=cost(20),
        name="attend",
    )(hidden, vectors, key_marks, query_marks, *blocks)


def inner_kernel(place, *refs):
    att, hidden, vectors = refs[:3]
    blocks, (first_low, normed, inverse, activated, slope) = refs[3:11], refs[11:16]
    w_in, w_out, in_sems, out_sems = refs[16:]
    first_step = pl.program_id(0) == 0

    def row(i):
        return vectors[i : i + 1, :]

    def copies_in():
        return block_copies(place, blocks, 0, w_in, in_sems)

    @pl.when(first_step)
    def _():
        copies = block_copies(place, blocks, 1536, w_out, out_sems)
        start(copies)
        start(copies_in())
        wait(copies)

    n1, r1 = normalize(hidden[...].astype(f32) + dot(att[...], w_out[...]) + row(2))
    low = (n1 * row(3) + row(4)).astype(bf16)
    first_low[...] = low
    normed[...] = n1.astype(bf16)
    inverse[...] = jnp.broadcast_to(r1, inverse.shape)

    @pl.when(first_step)
    def _():
        wait(copies_in())

    for c in range(FF // D):
        columns = slice(c * D, c * D + D)
        act, back = smooth(dot(low, w_in[:, columns]) + row(5 + c))
        activated[:, columns] = act.astype(bf16)
        slope[:, columns] = back.astype(bf16)


def inner_forward(place, att, hidden, vectors, blocks):
    tokens = hidden.shape[0]
    return pl.pallas_call(
        functools.partial(inner_kernel, place),
        grid=(tokens // TILE,),
        in_specs=[tile(D)] * 2 + [fixed((12, D))] + anywhere(8),
        out_specs=[tile(D), tile(D), tile(128), tile(FF), tile(FF)],
        out_shape=[
            Shape((tokens, D), bf16),
            Shape((tokens, D), bf16),
            Shape((tokens, 128), f32),
            Shape((tokens, FF), bf16),
            Shape((tokens, FF), bf16),
        ],
        scratch_shapes=[
            pltpu.VMEM((D, FF), bf16),
            pltpu.VMEM((D, D), bf16),
            pltpu.SemaphoreType.DMA((32,)),
            pltpu.SemaphoreType.DMA((32,)),
        ],
        compiler_params=params(60),
        cost_estimate=cost(16),
        name="inner_forward",
    )(att, hidden, vectors, *blocks)


def outer_kernel(place, *refs):
    act, normed, cotangent, vectors, back_table = refs[:5]
    output, grad_second, sums = refs[5:8]
    outs, (w_back, activated, grad_t, sems) = refs[8:16], refs[16:]
    step = pl.program_id(0)
    z, y, x, core = place()

    def row(i):
        return vectors[i : i + 1, :]

    @pl.when(step == 0)
    def _():
        copies = table_copies(back_table, w_back, sems)
        start(copies)
        wait(copies)

    here = pl.ds(pl.multiple_of(step * TILE, TILE), TILE)
    activated[here, :] = act[...]
    outward = normed[...].astype(f32) * row(3) + row(4) + dot(act[...], w_back[...]) + row(9)
    n2, r2 = normalize(outward)
    output[...] = (n2 * row(10) + row(11)).astype(bf16)
    cot = cotangent[...].astype(f32)
    g2 = normalize_back(cot * row(10), n2, r2)
    grad_second[...] = g2.astype(bf16)
    part = rows_of(8, column_sum(g2), column_sum(cot * n2), column_sum(cot))

    @pl.when(step == 0)
    def _():
        sums[...] = part

    @pl.when(step > 0)
    def _():
        sums[...] += part

    g2_t = g2.astype(bf16).T
    for n in range(4):
        at = ((n % 2) ^ core) * 2 + ((n // 2) ^ x)
        piece = g2_t[n * 192 : n * 192 + 192]
        grad_t[pl.ds(pl.multiple_of(at * 192, 192), 192), here] = piece

    @pl.when(step == pl.num_programs(0) - 1)
    def _():
        for k in range(4):
            columns = pl.ds(pl.multiple_of((z ^ k) * D, D), D)
            res = dot(grad_t[...], activated[:, columns]).astype(bf16)
            for other in range(2):
                for i in range(2):
                    at = (other * 2 + i) * 192
                    pieces = [res[at : at + 192, half * 384 : half * 384 + 384] for half in range(2)]
                    for bit in range(2):

                        @pl.when(y == bit)
                        def _(other=other, i=i, k=k, pieces=pieces, bit=bit):
                            outs[other * 4 + i][k] = pieces[bit]
                            outs[other * 4 + i + 2][k] = pieces[1 - bit]


def outer_forward(place, activated, normed, cotangent, vectors, back_table):
    tokens = normed.shape[0]
    return pl.pallas_call(
        functools.partial(outer_kernel, place),
        grid=(tokens // TILE,),
        in_specs=[tile(FF), tile(D), tile(D), fixed((12, D))] + anywhere(1),
        out_specs=[tile(D), tile(D), fixed((8, D))] + [fixed((4, 192, 384))] * 8,
        out_shape=[
            Shape((tokens, D), bf16),
            Shape((tokens, D), bf16),
            Shape((8, D), f32),
        ]
        + [Shape((4, 192, 384), bf16)] * 8,
        scratch_shapes=[
            pltpu.VMEM((FF, D), bf16),
            pltpu.VMEM((tokens, FF), bf16),
            pltpu.VMEM((D, tokens), bf16),
            pltpu.SemaphoreType.DMA((32,)),
        ],
        compiler_params=params(40),
        cost_estimate=cost(18),
        name="outer_forward",
    )(activated, normed, cotangent, vectors, back_table)


def backward_kernel(place, *refs):
    grad_second, slope, normed, inverse, first_low, att_t, vectors = refs[:7]
    blocks, back_table = refs[7:15], refs[15]
    grad_att, grad_branch, sums, sums_inner = refs[16:20]
    outs = refs[20:28]
    w_in, w_out, w_back, inner_low, first_t, grad_low, turned = refs[28:35]
    in_sems, out_sems, back_sems = refs[35:]
    step = pl.program_id(0)
    z, y, x, core = place()
    here = pl.ds(pl.multiple_of(step * TILE, TILE), TILE)

    def compute(first_step):
        if first_step:
            copies_back = table_copies(back_table, w_back, back_sems)
            copies_in = block_copies(place, blocks, 0, w_in, in_sems)
            copies_out = block_copies(place, blocks, 1536, w_out, out_sems)
            start(copies_back)
            start(copies_in)
            start(copies_out)
        g2_low = grad_second[...]
        grad_first = g2_low.astype(f32)
        inner_sums = []
        for c in range(FF // D):
            columns = slice(c * D, c * D + D)
            if first_step:
                wait(copies_back[c * 8 : c * 8 + 8])
            gi = dot_t(g2_low, w_back[columns, :]) * slope[:, columns].astype(f32)
            inner_sums.append(column_sum(gi))
            gi = gi.astype(bf16)
            inner_low[here, columns] = gi
            if first_step and c == 0:
                wait(copies_in)
            grad_first = grad_first + dot_t(gi, w_in[:, columns])
        n1 = normed[...].astype(f32)
        g1 = normalize_back(grad_first * vectors[3:4, :], n1, inverse[:, :1])
        g1_low = g1.astype(bf16)
        grad_branch[...] = g1_low
        grad_low[here, :] = g1_low
        if first_step:
            wait(copies_out)
        grad_att[...] = dot_t(g1_low, w_out[...]).astype(bf16)
        part = rows_of(8, column_sum(g1), column_sum(grad_first * n1), column_sum(grad_first))
        part_inner = rows_of(8, *inner_sums)
        if first_step:
            sums[...] = part
            sums_inner[...] = part_inner
        else:
            sums[...] += part
            sums_inner[...] += part_inner
        low_t = first_low[...].T
        for w in range(8):
            at = ((w % 2) ^ y) * 4 + ((w // 2) ^ z)
            piece = low_t[w * 96 : w * 96 + 96]
            first_t[pl.ds(pl.multiple_of(at * 96, 96), 96), here] = piece
        turn_rows(place, att_t, turned, here)

    @pl.when(step == 0)
    def _():
        compute(True)

    @pl.when(step > 0)
    def _():
        compute(False)

    @pl.when(step == pl.num_programs(0) - 1)
    def _():
        for i in range(2):
            for other in range(2):
                at = ((x ^ i) * 2 + (core ^ other)) * D
                res = dot(first_t[...], inner_low[:, pl.ds(pl.multiple_of(at, D), D)])
                res = res.astype(bf16)
                for j in range(2):
                    for k in range(4):
                        at = (j * 4 + k) * 96
                        outs[other * 4 + i + 2 * j][k, :, :D] = res[at : at + 48]
                        outs[other * 4 + i + 2 * j][k, :, D : 2 * D] = res[at + 48 : at + 96]
        res = dot(turned[...], grad_low[...]).astype(bf16)
        for bit in range(2):

            @pl.when(x == bit)
            def _(bit=bit):
                for other in range(2):
                    for j in range(2):
                        for k in range(4):
                            at = (other * 8 + j * 4 + k) * 48
                            for half in range(2):
                                piece = res[at : at + 48, half * 384 : half * 384 + 384]
                                outs[other * 4 + (half ^ bit) + 2 * j][k, :, 2 * D :] = piece


def backward(place, grad_second, slope, normed, inverse, first_low, att_t, vectors, *weights):
    blocks, back_table = weights
    tokens = normed.shape[0]
    outs = [(4, 48, 1920)] * 8
    return pl.pallas_call(
        functools.partial(backward_kernel, place),
        grid=(tokens // TILE,),
        in_specs=[tile(D), tile(FF), tile(D), tile(128), tile(D)]
        + [pl.BlockSpec((D, TILE), lambda i: (0, i)), fixed((12, D))]
        + anywhere(9),
        out_specs=[tile(D), tile(D)] + [fixed(s) for s in [(8, D)] * 2 + outs],
        out_shape=[Shape((tokens, D), bf16), Shape((tokens, D), bf16)]
        + [Shape((8, D), f32)] * 2
        + [Shape(s, bf16) for s in outs],
        scratch_shapes=[
            pltpu.VMEM((D, FF), bf16),
            pltpu.VMEM((D, D), bf16),
            pltpu.VMEM((FF, D), bf16),
            pltpu.VMEM((tokens, FF), bf16),
            pltpu.VMEM((D, tokens), bf16),
            pltpu.VMEM((tokens, D), bf16),
            pltpu.VMEM((D, tokens), bf16),
        ]
        + [pltpu.SemaphoreType.DMA((32,))] * 3,
        compiler_params=params(32),
        cost_estimate=cost(22),
        name="backward",
    )(grad_second, slope, normed, inverse, first_low, att_t, vectors, *blocks, back_table)


def turn_rows(place, source, turned, columns=slice(None)):
    z, y, _, core = place()
    for w in range(8):
        for half in range(2):
            at = (half ^ core) * 8 + ((w % 2) ^ y) * 4 + ((w // 2) ^ z)
            piece = (w * 2 + half) * 48
            rows = pl.ds(pl.multiple_of(at * 48, 48), 48)
            turned[rows, columns] = source[piece : piece + 48, :]


def attend_back_kernel(packed, grad_att, probs, grad_low, sums):
    length = packed.shape[0]
    lanes = lax.broadcasted_iota(jnp.int32, (length, 128), 1)
    zero = jnp.zeros((length, 128), bf16)
    blank = jnp.zeros((64, length), bf16)

    def pair(p, _):
        at = pl.multiple_of(p * 128, 128)
        q = packed[:, pl.ds(at, 128)]
        k_t = packed[:, pl.ds(D + at, 128)].T
        v = packed[:, pl.ds(2 * D + at, 128)]
        g = grad_att[:, pl.ds(at, 128)]
        g_t = g.T
        grad_probs = []
        for odd in range(2):
            own = g_t[64 * odd : 64 * odd + 64]
            grad_probs.append(dot(v, jnp.concatenate([blank, own] if odd else [own, blank], 0)))
        dk = dv = 0.0
        dq_t = []
        for odd in range(2):
            mine = (lanes >= 64) == bool(odd)
            low = probs[p * 2 + odd]
            wide = low.astype(f32)
            gp = grad_probs[odd]
            ds = (wide * (gp - column_sum(wide * gp))).astype(bf16)
            dv = dv + dot(low, jnp.where(mine, g, zero))
            dk = dk + dot(ds, jnp.where(mine, q, zero))
            dq_t.append(dot(k_t[64 * odd : 64 * odd + 64], ds))
        dq = jnp.concatenate(dq_t, 0).T * 0.125
        sums[0, :, pl.ds(at, 128)] = rows_of(8, column_sum(dq), column_sum(dv))
        grad_low[:, pl.ds(at, 128)] = dq.astype(bf16)
        grad_low[:, pl.ds(D + at, 128)] = dk.astype(bf16)
        grad_low[:, pl.ds(2 * D + at, 128)] = dv.astype(bf16)
        return 0

    lax.fori_loop(0, HEADS // 2, pair, 0, unroll=True)


def attend_back(row, packed, grad_att, probs, low=None):
    length = probs.shape[1]
    kernel, more, specs, alias = attend_back_kernel, (), [], {}
    if low is not None:
        more, specs, alias = (low,), [pl.BlockSpec(memory_space=pl.ANY)], {3: 0}

        def kernel(packed, grad_att, probs, low, grad_low, sums):
            attend_back_kernel(packed, grad_att, probs, grad_low, sums)

    return pl.pallas_call(
        kernel,
        grid=(1,),
        in_specs=[
            pl.BlockSpec((length, 3 * D), lambda i: (row, 0)),
            pl.BlockSpec((length, D), lambda i: (row, 0)),
            pl.BlockSpec((HEADS, length, length), lambda i: (row, 0, 0)),
        ]
        + specs,
        out_specs=[
            pl.BlockSpec((length, 3 * D), lambda i: (row, 0)),
            pl.BlockSpec((1, 8, D), lambda i: (0, 0, 0)),
        ],
        out_shape=[Shape(packed.shape, bf16), Shape((1, 8, D), f32)],
        input_output_aliases=alias,
        compiler_params=params(32),
        cost_estimate=cost(12),
        name="attend_back",
    )(packed, grad_att, probs, *more)


def grad_qkv_kernel(place, hidden, low, *refs):
    sums_zero, sums_one, sums_first, sums_inner, sums_second = refs[:5]
    outs, turned, groups = refs[5:13], refs[13], refs[14]
    z, y, x, core = place()
    turn_rows(place, hidden[...].T, turned)
    rows = [sums_zero[0, i : i + 1, :] + sums_one[0, i : i + 1, :] for i in range(2)]
    rows += [sums_first[i : i + 1, :] for i in range(3)]
    rows += [sums_inner[i : i + 1, :] for i in range(4)]
    rows += [sums_second[i : i + 1, :] for i in range(3)]
    for group in range(72):
        column = group % 6 * 128
        groups[group] = rows[group // 6][:, column : column + 128]
    for group in range(72, 76):
        groups[group] = jnp.zeros((1, 128), f32)
    for i in range(2):
        columns = pl.ds(pl.multiple_of((x ^ i) * 1152, 128), 1152)
        res = dot(turned[...], low[:, columns]).astype(bf16)
        for other in range(2):
            for j in range(2):
                out = outs[other * 4 + i + 2 * j]
                for k in range(4):
                    at = (other * 8 + j * 4 + k) * 48
                    out[k, :, :1152] = res[at : at + 48]
                    device = ((z ^ k) * 2 + (y ^ j)) * 4 + (x ^ i) * 2 + (core ^ other)
                    group = (9 * device) // 4
                    part = jnp.concatenate([groups[group + q] for q in range(4)], 0)
                    out[k, :16, 1152:] = rows_of(16, part).astype(bf16)
                    out[k, 16:, 1152:] = jnp.zeros((32, 128), bf16)


def grad_qkv(place, hidden, low, *sums):
    return pl.pallas_call(
        functools.partial(grad_qkv_kernel, place),
        out_shape=[Shape((4, 48, 1280), bf16)] * 8,
        scratch_shapes=[pltpu.VMEM((D, hidden.shape[0]), bf16), pltpu.VMEM((80, 1, 128), f32)],
        compiler_params=params(32),
        cost_estimate=cost(9),
        name="grad_qkv",
    )(hidden, low, *sums)


def cut_vectors(place, groups):
    z, y, x, core = place()
    at = (((z * 2 + y) * 4 + x * 2 + core) * 288) % 128
    return lax.dynamic_slice(groups.reshape(-1), (at,), (288,))


def hidden_kernel(place, *refs):
    low, grad_branch, blocks, out, weight, sems = *refs[:2], refs[2:10], *refs[10:]

    @pl.when(pl.program_id(0) == 0)
    def _():
        copies = block_copies(place, blocks, 0, weight, sems)
        start(copies)
        wait(copies)

    out[...] = grad_branch[...].astype(f32) + dot_t(low[...], weight[...])


def grad_of_hidden(place, low, grad_branch, blocks):
    tokens = low.shape[0]
    return pl.pallas_call(
        functools.partial(hidden_kernel, place),
        grid=(tokens // TILE,),
        in_specs=[tile(3 * D), tile(D)] + anywhere(8),
        out_specs=tile(D),
        out_shape=Shape((tokens, D), f32),
        scratch_shapes=[pltpu.VMEM((D, 3 * D), bf16), pltpu.SemaphoreType.DMA((32,))],
        compiler_params=params(60),
        cost_estimate=cost(9),
        name="grad_hidden",
    )(low, grad_branch, *blocks)


def gather_plain(w_qkv, w_out, w_in, w_back, vectors):
    def whole(piece):
        return lax.all_gather(
            lax.all_gather(piece, "narrow", axis=1, tiled=True), "wide", axis=0, tiled=True
        )

    full = tuple(whole(piece) for piece in (w_qkv, w_out, w_in, w_back))
    return full + (lax.all_gather(vectors, ALL, axis=0, tiled=True).reshape(12, D),)


def tie(*values):
    return lax.optimization_barrier(values)


def unfold(table, order, shape):
    return table.reshape((2, 2, 2, 4) + table.shape[3:]).transpose(order).reshape(shape)


def scatter_whole(matrix):
    part = lax.psum_scatter(matrix, "wide", scatter_dimension=0, tiled=True)
    part = lax.psum_scatter(part, "narrow", scatter_dimension=1, tiled=True)
    return part.astype(f32)


def per_device(hidden, segment, w_qkv, w_out, w_in, w_back, vectors, cotangent):
    (qkv,) = pair_up([w_qkv], [send(w_qkv, core=1)], vectors)
    rest = [w_out, w_in, w_back]
    other_rest = [send(piece, core=1) for piece in rest]
    qkv, other_rest, segment = tie(qkv, other_rest, segment)
    key_marks, query_marks = segment_marks(segment)
    qkv_line = gather_z(qkv)
    out, inner, back = pair_up(rest, other_rest)
    mid = jnp.concatenate([inner, out], 1)
    qkv_line, mid, back, key_marks, query_marks = tie(
        jnp.stack(qkv_line), mid, back, key_marks, query_marks
    )

    qkv_blocks = gather_chips(qkv_line)
    mid_line = gather_z(mid)
    qkv_blocks, mid_line, back = tie(qkv_blocks, mid_line, back)

    back_table = lax.all_gather(back, ALL, axis=0, tiled=False)
    mid_blocks = gather_chips(jnp.stack(mid_line))
    qkv_blocks = gather_cores(qkv_blocks)
    all_vectors = place_vectors(qkv_blocks)
    attended = attend(position, hidden, all_vectors, key_marks, query_marks, qkv_blocks)
    attended, mid_blocks = tie(attended, mid_blocks)
    packed, att, att_t, probs = attended

    mid_blocks = gather_cores(mid_blocks)
    inner_outs = inner_forward(position, att, hidden, all_vectors, mid_blocks)
    inner_outs, back_table = tie(inner_outs, back_table)
    first_low, normed, inverse, activated, slope = inner_outs

    output, grad_second, sums_second, *tables_back = outer_forward(
        position, activated, normed, cotangent, all_vectors, back_table
    )

    received_back = [send(block, core=1) for block in tables_back[4:]]
    parts_back = chip_parts(tables_back[:4], received_back)
    parts_back, grad_second = tie(parts_back, grad_second)
    others_back = chip_sends(parts_back)
    back_outs = backward(
        position,
        grad_second,
        slope,
        normed,
        inverse,
        first_low,
        att_t,
        all_vectors,
        mid_blocks,
        back_table,
    )
    back_outs, others_back = tie(back_outs, others_back)
    grad_att, grad_branch, sums_first, sums_inner, *tables_mid = back_outs

    received_mid = [send(block, core=1) for block in tables_mid[4:]]
    near_back, far_back = line_halves(parts_back[0], others_back)
    parts_mid = chip_parts(tables_mid[:4], received_mid)
    parts_mid, grad_att, near_back, far_back = tie(parts_mid, grad_att, near_back, far_back)

    plane_mid = [send(parts_mid[1], x=1), send(parts_mid[2], y=1)]
    corner_mid = send(parts_mid[3], x=1, y=1)
    far_back = send(far_back, z=2)
    packed_low, sums_zero = attend_back(0, packed, grad_att, probs)
    packed_low, sums_one = attend_back(1, packed, grad_att, probs, packed_low)
    tables_qkv = grad_qkv(
        position, hidden, packed_low, sums_zero, sums_one, sums_first, sums_inner, sums_second
    )
    tables_qkv, far_back, plane_mid = tie(tables_qkv, far_back, plane_mid)
    kept_qkv, sent_qkv = tables_qkv[:4], tables_qkv[4:]

    received_qkv = [send(block, core=1) for block in sent_qkv]
    parts_qkv = chip_parts_of(kept_qkv, received_qkv)
    parts_qkv, grad_branch, near_back, corner_mid = tie(
        parts_qkv, grad_branch, near_back, corner_mid
    )
    others_qkv = chip_sends(parts_qkv)
    near_mid, far_mid = line_halves(parts_mid[0], plane_mid + [corner_mid])
    far_mid = send(far_mid, z=2)
    near_back = near_parts(near_back, far_back)
    next_back = send(near_back[1], z=1)
    near_back, grad_branch = tie(near_back, grad_branch)
    grad_hidden = grad_of_hidden(position, packed_low, grad_branch, qkv_blocks)
    grad_hidden, far_mid, next_back = tie(grad_hidden, far_mid, next_back)

    own_back = wide_sum(near_back[0], next_back).T
    near_mid = near_parts(near_mid, far_mid)
    next_mid = send(near_mid[1], z=1)
    others_qkv, near_mid = tie(others_qkv, near_mid)
    line_qkv = line_parts(parts_qkv[0], others_qkv)
    lines_qkv = line_sends(line_qkv)
    own_mid = wide_sum(near_mid[0], next_mid)
    own_in = jnp.concatenate([own_mid[:, :D], own_mid[:, D : 2 * D]], 0)
    own_out = swap_columns(own_mid[:, 2 * D :])
    own_in, own_out, own_back, lines_qkv = tie(own_in, own_out, own_back, lines_qkv)
    own_qkv = wide_sum(line_qkv[0], *lines_qkv)
    own_vectors = cut_vectors(position, own_qkv[:4, 1152:])
    own_qkv = swap_columns(own_qkv[:, :1152])
    return (output, grad_hidden, own_qkv, own_out, own_in, own_back, own_vectors)


def per_device_plain(hidden, segment, w_qkv, w_out, w_in, w_back, vectors, cotangent):
    key_marks, query_marks = segment_marks(segment)
    full_qkv, full_out, full_in, full_back, all_vectors = gather_plain(
        w_qkv, w_out, w_in, w_back, vectors
    )
    qkv_blocks = split_blocks(full_qkv, 48, 1152)
    mid_blocks = [
        jnp.concatenate(pair, 2)
        for pair in zip(split_blocks(full_in, 48, 1536), split_blocks(full_out, 48, 384))
    ]
    back_pieces = full_back.reshape(8, 2, 192, 2, 384).transpose(0, 3, 1, 2, 4)
    back_pieces = back_pieces.reshape(32, 192, 384)
    packed, att, att_t, probs = attend(
        origin, hidden, all_vectors, key_marks, query_marks, qkv_blocks
    )
    first_low, normed, inverse, activated, slope = inner_forward(
        origin, att, hidden, all_vectors, mid_blocks
    )
    output, grad_second, sums_second, *back_table = outer_forward(
        origin, activated, normed, cotangent, all_vectors, back_pieces
    )
    grad_att, grad_branch, sums_first, sums_inner, *tables = backward(
        origin,
        grad_second,
        slope,
        normed,
        inverse,
        first_low,
        att_t,
        all_vectors,
        mid_blocks,
        back_pieces,
    )
    mid_table = jnp.stack(tables).reshape(2, 4, 4, 48, 1920)
    packed_low, sums_zero = attend_back(0, packed, grad_att, probs)
    packed_low, sums_one = attend_back(1, packed, grad_att, probs, packed_low)
    grad_hidden = grad_of_hidden(origin, packed_low, grad_branch, qkv_blocks)
    tables = grad_qkv(
        origin, hidden, packed_low, sums_zero, sums_one, sums_first, sums_inner, sums_second
    )
    grad_vectors = jnp.concatenate(
        [(sums_zero + sums_one)[0, :2], sums_first[:3], sums_inner[:4], sums_second[:3]], 0
    )
    qkv_table = jnp.stack(tables)
    qkv_table = qkv_table.reshape(2, 4, 4, 48, 1280)
    halves = jnp.stack([mid_table[..., :D], mid_table[..., D : 2 * D]], 4)
    own_qkv = scatter_whole(unfold(qkv_table[..., :1152], (3, 1, 0, 4, 2, 5), (D, 3 * D)))
    own_out = scatter_whole(unfold(mid_table[..., 2 * D :], (3, 1, 0, 4, 2, 5), (D, D)))
    own_in = scatter_whole(unfold(halves, (3, 1, 4, 5, 2, 0, 6), (D, FF)))
    back_table = jnp.stack(back_table).reshape(2, 4, 4, 192, 384)
    back_t = unfold(back_table, (2, 0, 4, 3, 1, 5), (D, FF))
    own_back = scatter_whole(back_t.T)
    own_vectors = lax.psum_scatter(
        grad_vectors.reshape(-1), ALL, scatter_dimension=0, tiled=True
    )
    return (output, grad_hidden, own_qkv, own_out, own_in, own_back, own_vectors)


def solution(mesh):
    trees = mesh.shape["wide"] == 8 and mesh.shape["narrow"] == 4
    return jax.shard_map(
        per_device if trees else per_device_plain,
        mesh=mesh,
        in_specs=(P(ALL, None),) * 2 + (P("wide", "narrow"),) * 4 + (P(ALL), P(ALL, None)),
        out_specs=(P(ALL, None),) * 2 + (P("wide", "narrow"),) * 4 + (P(ALL),),
        check_vma=False,
    )
```

```python
import functools

import jax
import jax.numpy as jnp
from jax import lax
from jax.experimental import pallas as pl
from jax.experimental.pallas import tpu as pltpu
from jax.sharding import PartitionSpec as P

D = 768
HEADS = 12
FF = 3072
TILE = 256
ALL = ("wide", "narrow")
CHIP_STEPS = ((0, 0), (1, 0), (0, 1), (1, 1))
bf16, f32 = jnp.bfloat16, jnp.float32
Shape = jax.ShapeDtypeStruct

epsilon = 1e-06


def cost(us):
    return pl.CostEstimate(flops=0 * us, bytes_accessed=0, transcendentals=0)


def params(mib=60):
    return pltpu.CompilerParams(vmem_limit_bytes=mib * 2**20)


def send(values, z=0, y=0, x=0, core=0):
    flip_wide, flip_narrow = 2 * z + y, 2 * x + core
    pairs = [
        (w * 4 + n, (w ^ flip_wide) * 4 + (n ^ flip_narrow)) for w in range(8) for n in range(4)
    ]
    return lax.ppermute(values, ALL, pairs)


def position():
    wide, narrow = lax.axis_index("wide"), lax.axis_index("narrow")
    return wide // 2, wide % 2, narrow // 2, narrow % 2


def origin():
    zero = jnp.int32(0)
    return zero, zero, zero, zero


def gather_z(values):
    return [values] + [send(values, z=k) for k in (1, 2, 3)]


def gather_chips(lines):
    return [lines] + [send(lines, x=i, y=j) for i, j in CHIP_STEPS[1:]]


def gather_cores(blocks):
    return blocks + [send(block, core=1) for block in blocks]


def pair_kernel(count, *refs):
    core = lax.rem(lax.axis_index("narrow"), 2)
    more, outs = refs[2 * count : -count], refs[-count:]
    for own, other, out in zip(refs[:count], refs[count : 2 * count], outs):
        rows, columns = own.shape[0] // 2, own.shape[1]
        half = pl.ds(pl.multiple_of(core * rows, rows), rows)

        @pl.when(core == 0)
        def _(own=own, other=other, out=out, half=half, columns=columns):
            out[:, :columns] = own[half, :]
            out[:, columns : 2 * columns] = other[half, :]

        @pl.when(core == 1)
        def _(own=own, other=other, out=out, half=half, columns=columns):
            out[:, :columns] = other[half, :]
            out[:, columns : 2 * columns] = own[half, :]

    for vector in more:
        rest, parts = vector[...], []
        for _ in range(3):
            parts.append(rest.astype(bf16).astype(f32))
            rest = rest - parts[-1]
        outs[0][:, 1152:] = rows_of(48, *parts).astype(bf16)


def pair_up(pieces, others, vectors=None):
    more = [0] * len(pieces)
    rows = ()
    if vectors is not None:
        rows = (jnp.pad(vectors, (0, 384 - vectors.shape[0])).reshape(3, 128),)
        more[0] = 128
    return pl.pallas_call(
        functools.partial(pair_kernel, len(pieces)),
        out_shape=[
            Shape((piece.shape[0] // 2, piece.shape[1] * 2 + extra), piece.dtype)
            for piece, extra in zip(pieces, more)
        ],
        cost_estimate=cost(2),
        name="pair_up",
    )(*pieces, *others, *rows)


def block_copies(place, blocks, left, out, sems):
    z, y, x, core = place()
    rows, width = blocks[0].shape[1], out.shape[1] // 2
    copies = []
    for other in range(2):
        for step, (i, j) in enumerate(CHIP_STEPS):
            for k in range(4):
                row = (((z ^ k) * 2 + (y ^ j)) * 2 + (core ^ other)) * rows
                copies.append(
                    pltpu.make_async_copy(
                        blocks[other * 4 + step].at[k, :, pl.ds(left, width)],
                        out.at[
                            pl.ds(pl.multiple_of(row, rows), rows),
                            pl.ds(pl.multiple_of((x ^ i) * width, width), width),
                        ],
                        sems.at[len(copies)],
                    )
                )
    return copies


def start(copies):
    for copy in copies:
        copy.start()


def wait(copies):
    for copy in copies:
        copy.wait()


def anywhere(count):
    return [pl.BlockSpec(memory_space=pl.ANY)] * count


def split_blocks(matrix, rows, columns):
    parts = matrix.reshape(4, 2, 2, rows, 2, columns).transpose(2, 1, 4, 0, 3, 5)
    return [parts[other, j, i] for other in range(2) for i, j in CHIP_STEPS]


def place_kernel(*refs):
    z, y, x, core = position()
    out = refs[8]
    for other in range(2):
        for step, (i, j) in enumerate(CHIP_STEPS):
            for k in range(4):
                row = ((z ^ k) * 2 + (y ^ j)) * 4 + (x ^ i) * 2 + (core ^ other)
                parts = refs[other * 4 + step][k].astype(f32)
                out[row] = parts[:3] + parts[3:6] + parts[6:9]


def place_vectors(blocks):
    table = pl.pallas_call(
        place_kernel,
        grid=(1,),
        in_specs=[pl.BlockSpec((4, 16, 128), lambda i: (0, 0, 9))] * 8,
        out_specs=fixed((32, 3, 128)),
        out_shape=Shape((32, 3, 128), f32),
        cost_estimate=cost(1),
        name="place_vectors",
    )(*blocks)
    return table.reshape(32, 384)[:, :288].reshape(12, D)


def wide_sum(*terms):
    return functools.reduce(lambda a, b: a + b, [t.astype(f32) for t in terms])


def chip_parts(kept, received):
    return [wide_sum(kept[s], received[s]).astype(bf16) for s in range(4)]


def chip_kernel(*refs):
    for kept, received, out in zip(refs[:4], refs[4:8], refs[8:]):
        out[...] = wide_sum(kept[...], received[...]).astype(bf16)


def chip_parts_of(kept, received):
    rows, columns = kept[0].shape[1:]
    line = pl.BlockSpec((1, rows, columns), lambda k: (k, 0, 0))
    return pl.pallas_call(
        chip_kernel,
        grid=(4,),
        in_specs=[line] * 8,
        out_specs=[line] * 4,
        out_shape=[Shape((4, rows, columns), bf16)] * 4,
        compiler_params=params(32),
        cost_estimate=cost(3),
        name="chip_parts",
    )(*kept, *received)


def chip_sends(parts):
    return [send(parts[s], x=i, y=j) for s, (i, j) in enumerate(CHIP_STEPS) if s]


def line_kernel(far, *refs):
    terms, outs = refs[:4], refs[4:]
    for k in range(4):
        total = wide_sum(*[term[k] for term in terms]).astype(bf16)
        if far and k >= 2:
            outs[2][k - 2] = total
        else:
            outs[k][...] = total


def line_parts(own, others, far=False):
    piece = Shape(own.shape[1:], bf16)
    shapes = [piece] * 2 + [Shape((2,) + own.shape[1:], bf16)] if far else [piece] * 4
    return pl.pallas_call(
        functools.partial(line_kernel, far),
        out_shape=shapes,
        compiler_params=params(32),
        cost_estimate=cost(2),
        name="line_parts",
    )(own, *others)


def line_sends(line):
    return [send(line[k], z=k) for k in (1, 2, 3)]


def line_halves(own, others):
    *near, far = line_parts(own, others, True)
    return near, far


def near_parts(near, received):
    return [wide_sum(near[k], received[k]).astype(near[k].dtype) for k in range(2)]


def swap_columns(summed):
    core = lax.axis_index("narrow") % 2
    columns = summed.shape[1] // 2
    left, right = summed[:, :columns], summed[:, columns:]
    mine = jnp.where(core == 0, left, right)
    other = send(jnp.where(core == 0, right, left).astype(bf16), core=1).astype(f32)
    return jnp.concatenate(
        [jnp.where(core == 0, mine, other), jnp.where(core == 0, other, mine)], 0
    )


def dot(left_side, right_side):
    return jnp.dot(left_side, right_side, preferred_element_type=f32)


def dot_t(left_side, right_side):
    return lax.dot_general(
        left_side, right_side, (((1,), (1,)), ((), ())), preferred_element_type=f32
    )


def column_sum(values):
    return jnp.sum(values, 0, keepdims=True)


def normalize(values):
    center = values - jnp.mean(values, -1, keepdims=True)
    inverse = lax.rsqrt(jnp.mean(center * center, -1, keepdims=True) + epsilon)
    return center * inverse, inverse


def normalize_back(grad_norm, normed, inverse):
    return inverse * (
        grad_norm
        - jnp.mean(grad_norm, -1, keepdims=True)
        - normed * jnp.mean(grad_norm * normed, -1, keepdims=True)
    )


def smooth(values):
    density = jnp.exp(-0.5 * values * values) * 0.3989422804014327
    below = 0.5 + 0.5 * lax.erf(values * 0.7071067811865476)
    return values * below, below + values * density


def fixed(shape):
    return pl.BlockSpec(shape, lambda i: (0,) * len(shape))


def tile(columns, rows=TILE):
    return pl.BlockSpec((rows, columns), lambda i: (i, 0))


def rows_of(count, *parts):
    missing = count - sum(part.shape[0] for part in parts)
    return jnp.concatenate(list(parts) + [jnp.zeros((missing, parts[0].shape[1]), f32)], 0)


def segment_marks(segment):
    kinds = lax.broadcasted_iota(jnp.int32, (1, 64), 1)
    mark = (segment.reshape(-1, 1) == kinds).astype(bf16)
    tall = lax.broadcasted_iota(jnp.int32, (1, 64, 1), 1)
    away = (segment[:, None, :] != tall) & (tall < 4)
    return jnp.concatenate([mark, mark], 1), jnp.where(away, -(2.0**30), 0.0).astype(bf16)


def attend_kernel(place, *refs):
    hidden, vectors, key_marks, query_marks = refs[:4]
    blocks, (packed, att, att_t, probs, weight, sems) = refs[4:12], refs[12:]

    @pl.when(pl.program_id(0) == 0)
    def _():
        copies = block_copies(place, blocks, 0, weight, sems)
        start(copies)
        wait(copies)

    length = hidden.shape[0]
    for part in range(3):
        columns = slice(part * D, (part + 1) * D)
        block = dot(hidden[...], weight[:, columns])
        if part != 1:
            block = block + vectors[part // 2 : part // 2 + 1, :]
        block = block.astype(bf16)
        if part == 0:
            block = block * jnp.asarray(0.125, bf16)
        packed[:, columns] = block
    lanes = lax.broadcasted_iota(jnp.int32, (length, 128), 1)

    def pair(p, _):
        at = pl.multiple_of(p * 128, 128)
        q_t = packed[:, pl.ds(at, 128)].T
        k = packed[:, pl.ds(D + at, 128)]
        v_t = packed[:, pl.ds(2 * D + at, 128)].T
        scores = []
        for odd in range(2):
            keys = jnp.where((lanes >= 64) == bool(odd), k, key_marks[...])
            own = q_t[64 * odd : 64 * odd + 64]
            marks = query_marks[0]
            scores.append(dot(keys, jnp.concatenate([marks, own] if odd else [own, marks], 0)))
        outs = []
        for odd in range(2):
            weights = jnp.exp(scores[odd] - jnp.max(scores[odd], 0, keepdims=True))
            low = (weights * (1.0 / column_sum(weights))).astype(bf16)
            probs[p * 2 + odd] = low
            outs.append(dot(v_t[64 * odd : 64 * odd + 64], low))
        out = jnp.concatenate(outs, 0).astype(bf16)
        att_t[pl.ds(at, 128), :] = out
        att[:, pl.ds(at, 128)] = out.T
        return 0

    lax.fori_loop(0, HEADS // 2, pair, 0, unroll=True)


def attend(place, hidden, vectors, key_marks, query_marks, blocks):
    rows, length = query_marks.shape[0], query_marks.shape[2]
    tokens = rows * length
    return pl.pallas_call(
        functools.partial(attend_kernel, place),
        grid=(rows,),
        in_specs=[
            tile(D, length),
            fixed((12, D)),
            tile(128, length),
            pl.BlockSpec((1, 64, length), lambda i: (i, 0, 0)),
        ]
        + anywhere(8),
        scratch_shapes=[pltpu.VMEM((D, 3 * D), bf16), pltpu.SemaphoreType.DMA((32,))],
        out_specs=[
            tile(3 * D, length),
            tile(D, length),
            pl.BlockSpec((D, length), lambda i: (0, i)),
            pl.BlockSpec((HEADS, length, length), lambda i: (i, 0, 0)),
        ],
        out_shape=[
            Shape((tokens, 3 * D), bf16),
            Shape((tokens, D), bf16),
            Shape((D, tokens), bf16),
            Shape((rows * HEADS, length, length), bf16),
        ],
        compiler_params=params(60),
        cost_estimate=cost(20),
        name="attend",
    )(hidden, vectors, key_marks, query_marks, *blocks)


def inner_kernel(place, *refs):
    att, hidden, vectors = refs[:3]
    blocks, (first_low, normed, inverse, activated, slope) = refs[3:11], refs[11:16]
    w_in, w_out, in_sems, out_sems = refs[16:]
    first_step = pl.program_id(0) == 0

    def row(i):
        return vectors[i : i + 1, :]

    def copies_in():
        return block_copies(place, blocks, 0, w_in, in_sems)

    @pl.when(first_step)
    def _():
        copies = block_copies(place, blocks, 1536, w_out, out_sems)
        start(copies)
        start(copies_in())
        wait(copies)

    n1, r1 = normalize(hidden[...].astype(f32) + dot(att[...], w_out[...]) + row(2))
    low = (n1 * row(3) + row(4)).astype(bf16)
    first_low[...] = low
    normed[...] = n1.astype(bf16)
    inverse[...] = jnp.broadcast_to(r1, inverse.shape)

    @pl.when(first_step)
    def _():
        wait(copies_in())

    for c in range(FF // D):
        columns = slice(c * D, c * D + D)
        act, back = smooth(dot(low, w_in[:, columns]) + row(5 + c))
        activated[:, columns] = act.astype(bf16)
        slope[:, columns] = back.astype(bf16)


def inner_forward(place, att, hidden, vectors, blocks):
    tokens = hidden.shape[0]
    return pl.pallas_call(
        functools.partial(inner_kernel, place),
        grid=(tokens // TILE,),
        in_specs=[tile(D)] * 2 + [fixed((12, D))] + anywhere(8),
        out_specs=[tile(D), tile(D), tile(128), tile(FF), tile(FF)],
        out_shape=[
            Shape((tokens, D), bf16),
            Shape((tokens, D), bf16),
            Shape((tokens, 128), f32),
            Shape((tokens, FF), bf16),
            Shape((tokens, FF), bf16),
        ],
        scratch_shapes=[
            pltpu.VMEM((D, FF), bf16),
            pltpu.VMEM((D, D), bf16),
            pltpu.SemaphoreType.DMA((32,)),
            pltpu.SemaphoreType.DMA((32,)),
        ],
        compiler_params=params(60),
        cost_estimate=cost(16),
        name="inner_forward",
    )(att, hidden, vectors, *blocks)


def outer_kernel(place, *refs):
    act, normed, cotangent, vectors = refs[:4]
    blocks, (output, grad_second, sums) = refs[4:12], refs[12:15]
    outs, (w_back, activated, grad_t, sems) = refs[15:23], refs[23:]
    step = pl.program_id(0)
    z, y, x, core = place()

    def row(i):
        return vectors[i : i + 1, :]

    @pl.when(step == 0)
    def _():
        copies = block_copies(place, blocks, 0, w_back, sems)
        start(copies)
        wait(copies)

    here = pl.ds(pl.multiple_of(step * TILE, TILE), TILE)
    activated[here, :] = act[...]
    outward = normed[...].astype(f32) * row(3) + row(4) + dot(act[...], w_back[...]) + row(9)
    n2, r2 = normalize(outward)
    output[...] = (n2 * row(10) + row(11)).astype(bf16)
    cot = cotangent[...].astype(f32)
    g2 = normalize_back(cot * row(10), n2, r2)
    grad_second[...] = g2.astype(bf16)
    part = rows_of(8, column_sum(g2), column_sum(cot * n2), column_sum(cot))

    @pl.when(step == 0)
    def _():
        sums[...] = part

    @pl.when(step > 0)
    def _():
        sums[...] += part

    g2_t = g2.astype(bf16).T
    for n in range(4):
        at = ((n % 2) ^ core) * 2 + ((n // 2) ^ x)
        piece = g2_t[n * 192 : n * 192 + 192]
        grad_t[pl.ds(pl.multiple_of(at * 192, 192), 192), here] = piece

    @pl.when(step == pl.num_programs(0) - 1)
    def _():
        for k in range(4):
            columns = pl.ds(pl.multiple_of((z ^ k) * D, D), D)
            res = dot(grad_t[...], activated[:, columns]).astype(bf16)
            for other in range(2):
                for i in range(2):
                    at = (other * 2 + i) * 192
                    pieces = [res[at : at + 192, half * 384 : half * 384 + 384] for half in range(2)]
                    for bit in range(2):

                        @pl.when(y == bit)
                        def _(other=other, i=i, k=k, pieces=pieces, bit=bit):
                            outs[other * 4 + i][k] = pieces[bit]
                            outs[other * 4 + i + 2][k] = pieces[1 - bit]


def outer_forward(place, activated, normed, cotangent, vectors, blocks):
    tokens = normed.shape[0]
    return pl.pallas_call(
        functools.partial(outer_kernel, place),
        grid=(tokens // TILE,),
        in_specs=[tile(FF), tile(D), tile(D), fixed((12, D))] + anywhere(8),
        out_specs=[tile(D), tile(D), fixed((8, D))] + [fixed((4, 192, 384))] * 8,
        out_shape=[
            Shape((tokens, D), bf16),
            Shape((tokens, D), bf16),
            Shape((8, D), f32),
        ]
        + [Shape((4, 192, 384), bf16)] * 8,
        scratch_shapes=[
            pltpu.VMEM((FF, D), bf16),
            pltpu.VMEM((tokens, FF), bf16),
            pltpu.VMEM((D, tokens), bf16),
            pltpu.SemaphoreType.DMA((32,)),
        ],
        compiler_params=params(40),
        cost_estimate=cost(18),
        name="outer_forward",
    )(activated, normed, cotangent, vectors, *blocks)


def backward_kernel(place, *refs):
    grad_second, slope, normed, inverse, first_low, att_t, vectors = refs[:7]
    blocks, back_blocks = refs[7:15], refs[15:23]
    grad_att, grad_branch, sums, sums_inner = refs[23:27]
    outs = refs[27:35]
    w_in, w_out, w_back, inner_low, first_t, grad_low, turned = refs[35:42]
    in_sems, out_sems, back_sems = refs[42:]
    step = pl.program_id(0)
    z, y, x, core = place()
    here = pl.ds(pl.multiple_of(step * TILE, TILE), TILE)

    def compute(first_step):
        if first_step:
            copies_back = block_copies(place, back_blocks, 0, w_back, back_sems)
            copies_in = block_copies(place, blocks, 0, w_in, in_sems)
            copies_out = block_copies(place, blocks, 1536, w_out, out_sems)
            start(copies_back)
            start(copies_in)
            start(copies_out)
        g2_low = grad_second[...]
        grad_first = g2_low.astype(f32)
        inner_sums = []
        for c in range(FF // D):
            columns = slice(c * D, c * D + D)
            if first_step and c == 0:
                wait(copies_back)
            gi = dot_t(g2_low, w_back[columns, :]) * slope[:, columns].astype(f32)
            inner_sums.append(column_sum(gi))
            gi = gi.astype(bf16)
            inner_low[here, columns] = gi
            if first_step and c == 0:
                wait(copies_in)
            grad_first = grad_first + dot_t(gi, w_in[:, columns])
        n1 = normed[...].astype(f32)
        g1 = normalize_back(grad_first * vectors[3:4, :], n1, inverse[:, :1])
        g1_low = g1.astype(bf16)
        grad_branch[...] = g1_low
        grad_low[here, :] = g1_low
        if first_step:
            wait(copies_out)
        grad_att[...] = dot_t(g1_low, w_out[...]).astype(bf16)
        part = rows_of(8, column_sum(g1), column_sum(grad_first * n1), column_sum(grad_first))
        part_inner = rows_of(8, *inner_sums)
        if first_step:
            sums[...] = part
            sums_inner[...] = part_inner
        else:
            sums[...] += part
            sums_inner[...] += part_inner
        low_t = first_low[...].T
        for w in range(8):
            at = ((w % 2) ^ y) * 4 + ((w // 2) ^ z)
            piece = low_t[w * 96 : w * 96 + 96]
            first_t[pl.ds(pl.multiple_of(at * 96, 96), 96), here] = piece
        turn_rows(place, att_t, turned, here)

    @pl.when(step == 0)
    def _():
        compute(True)

    @pl.when(step > 0)
    def _():
        compute(False)

    @pl.when(step == pl.num_programs(0) - 1)
    def _():
        for i in range(2):
            for other in range(2):
                at = ((x ^ i) * 2 + (core ^ other)) * D
                res = dot(first_t[...], inner_low[:, pl.ds(pl.multiple_of(at, D), D)])
                res = res.astype(bf16)
                for j in range(2):
                    for k in range(4):
                        at = (j * 4 + k) * 96
                        outs[other * 4 + i + 2 * j][k, :, :D] = res[at : at + 48]
                        outs[other * 4 + i + 2 * j][k, :, D : 2 * D] = res[at + 48 : at + 96]
        res = dot(turned[...], grad_low[...]).astype(bf16)
        for bit in range(2):

            @pl.when(x == bit)
            def _(bit=bit):
                for other in range(2):
                    for j in range(2):
                        for k in range(4):
                            at = (other * 8 + j * 4 + k) * 48
                            for half in range(2):
                                piece = res[at : at + 48, half * 384 : half * 384 + 384]
                                outs[other * 4 + (half ^ bit) + 2 * j][k, :, 2 * D :] = piece


def backward(place, grad_second, slope, normed, inverse, first_low, att_t, vectors, *weights):
    blocks, back_blocks = weights
    tokens = normed.shape[0]
    outs = [(4, 48, 1920)] * 8
    return pl.pallas_call(
        functools.partial(backward_kernel, place),
        grid=(tokens // TILE,),
        in_specs=[tile(D), tile(FF), tile(D), tile(128), tile(D)]
        + [pl.BlockSpec((D, TILE), lambda i: (0, i)), fixed((12, D))]
        + anywhere(16),
        out_specs=[tile(D), tile(D)] + [fixed(s) for s in [(8, D)] * 2 + outs],
        out_shape=[Shape((tokens, D), bf16), Shape((tokens, D), bf16)]
        + [Shape((8, D), f32)] * 2
        + [Shape(s, bf16) for s in outs],
        scratch_shapes=[
            pltpu.VMEM((D, FF), bf16),
            pltpu.VMEM((D, D), bf16),
            pltpu.VMEM((FF, D), bf16),
            pltpu.VMEM((tokens, FF), bf16),
            pltpu.VMEM((D, tokens), bf16),
            pltpu.VMEM((tokens, D), bf16),
            pltpu.VMEM((D, tokens), bf16),
        ]
        + [pltpu.SemaphoreType.DMA((32,))] * 3,
        compiler_params=params(32),
        cost_estimate=cost(22),
        name="backward",
    )(grad_second, slope, normed, inverse, first_low, att_t, vectors, *blocks, *back_blocks)


def turn_rows(place, source, turned, columns=slice(None)):
    z, y, _, core = place()
    for w in range(8):
        for half in range(2):
            at = (half ^ core) * 8 + ((w % 2) ^ y) * 4 + ((w // 2) ^ z)
            piece = (w * 2 + half) * 48
            rows = pl.ds(pl.multiple_of(at * 48, 48), 48)
            turned[rows, columns] = source[piece : piece + 48, :]


def attend_back_kernel(packed, grad_att, probs, grad_low, sums):
    length = packed.shape[0]
    lanes = lax.broadcasted_iota(jnp.int32, (length, 128), 1)
    zero = jnp.zeros((length, 128), bf16)
    blank = jnp.zeros((64, length), bf16)

    def pair(p, _):
        at = pl.multiple_of(p * 128, 128)
        q = packed[:, pl.ds(at, 128)]
        k_t = packed[:, pl.ds(D + at, 128)].T
        v = packed[:, pl.ds(2 * D + at, 128)]
        g = grad_att[:, pl.ds(at, 128)]
        g_t = g.T
        grad_probs = []
        for odd in range(2):
            own = g_t[64 * odd : 64 * odd + 64]
            grad_probs.append(dot(v, jnp.concatenate([blank, own] if odd else [own, blank], 0)))
        dk = dv = 0.0
        dq_t = []
        for odd in range(2):
            mine = (lanes >= 64) == bool(odd)
            low = probs[p * 2 + odd]
            wide = low.astype(f32)
            gp = grad_probs[odd]
            ds = (wide * (gp - column_sum(wide * gp))).astype(bf16)
            dv = dv + dot(low, jnp.where(mine, g, zero))
            dk = dk + dot(ds, jnp.where(mine, q, zero))
            dq_t.append(dot(k_t[64 * odd : 64 * odd + 64], ds))
        dq = jnp.concatenate(dq_t, 0).T * 0.125
        sums[0, :, pl.ds(at, 128)] = rows_of(8, column_sum(dq), column_sum(dv))
        grad_low[:, pl.ds(at, 128)] = dq.astype(bf16)
        grad_low[:, pl.ds(D + at, 128)] = dk.astype(bf16)
        grad_low[:, pl.ds(2 * D + at, 128)] = dv.astype(bf16)
        return 0

    lax.fori_loop(0, HEADS // 2, pair, 0, unroll=True)


def attend_back(row, packed, grad_att, probs, low=None):
    length = probs.shape[1]
    kernel, more, specs, alias = attend_back_kernel, (), [], {}
    if low is not None:
        more, specs, alias = (low,), [pl.BlockSpec(memory_space=pl.ANY)], {3: 0}

        def kernel(packed, grad_att, probs, low, grad_low, sums):
            attend_back_kernel(packed, grad_att, probs, grad_low, sums)

    return pl.pallas_call(
        kernel,
        grid=(1,),
        in_specs=[
            pl.BlockSpec((length, 3 * D), lambda i: (row, 0)),
            pl.BlockSpec((length, D), lambda i: (row, 0)),
            pl.BlockSpec((HEADS, length, length), lambda i: (row, 0, 0)),
        ]
        + specs,
        out_specs=[
            pl.BlockSpec((length, 3 * D), lambda i: (row, 0)),
            pl.BlockSpec((1, 8, D), lambda i: (0, 0, 0)),
        ],
        out_shape=[Shape(packed.shape, bf16), Shape((1, 8, D), f32)],
        input_output_aliases=alias,
        compiler_params=params(32),
        cost_estimate=cost(12),
        name="attend_back",
    )(packed, grad_att, probs, *more)


def grad_qkv_kernel(place, hidden, low, *refs):
    sums_zero, sums_one, sums_first, sums_inner, sums_second = refs[:5]
    outs, turned, groups = refs[5:13], refs[13], refs[14]
    z, y, x, core = place()
    turn_rows(place, hidden[...].T, turned)
    rows = [sums_zero[0, i : i + 1, :] + sums_one[0, i : i + 1, :] for i in range(2)]
    rows += [sums_first[i : i + 1, :] for i in range(3)]
    rows += [sums_inner[i : i + 1, :] for i in range(4)]
    rows += [sums_second[i : i + 1, :] for i in range(3)]
    for group in range(72):
        column = group % 6 * 128
        groups[group] = rows[group // 6][:, column : column + 128]
    for group in range(72, 76):
        groups[group] = jnp.zeros((1, 128), f32)
    for i in range(2):
        columns = pl.ds(pl.multiple_of((x ^ i) * 1152, 128), 1152)
        res = dot(turned[...], low[:, columns]).astype(bf16)
        for other in range(2):
            for j in range(2):
                out = outs[other * 4 + i + 2 * j]
                for k in range(4):
                    at = (other * 8 + j * 4 + k) * 48
                    out[k, :, :1152] = res[at : at + 48]
                    device = ((z ^ k) * 2 + (y ^ j)) * 4 + (x ^ i) * 2 + (core ^ other)
                    group = (9 * device) // 4
                    part = jnp.concatenate([groups[group + q] for q in range(4)], 0)
                    out[k, :16, 1152:] = rows_of(16, part).astype(bf16)
                    out[k, 16:, 1152:] = jnp.zeros((32, 128), bf16)


def grad_qkv(place, hidden, low, *sums):
    return pl.pallas_call(
        functools.partial(grad_qkv_kernel, place),
        out_shape=[Shape((4, 48, 1280), bf16)] * 8,
        scratch_shapes=[pltpu.VMEM((D, hidden.shape[0]), bf16), pltpu.VMEM((80, 1, 128), f32)],
        compiler_params=params(32),
        cost_estimate=cost(9),
        name="grad_qkv",
    )(hidden, low, *sums)


def cut_vectors(place, groups):
    z, y, x, core = place()
    at = (((z * 2 + y) * 4 + x * 2 + core) * 288) % 128
    return lax.dynamic_slice(groups.reshape(-1), (at,), (288,))


def hidden_kernel(place, *refs):
    low, grad_branch, blocks, out, weight, sems = *refs[:2], refs[2:10], *refs[10:]

    @pl.when(pl.program_id(0) == 0)
    def _():
        copies = block_copies(place, blocks, 0, weight, sems)
        start(copies)
        wait(copies)

    out[...] = grad_branch[...].astype(f32) + dot_t(low[...], weight[...])


def grad_of_hidden(place, low, grad_branch, blocks):
    tokens = low.shape[0]
    return pl.pallas_call(
        functools.partial(hidden_kernel, place),
        grid=(tokens // TILE,),
        in_specs=[tile(3 * D), tile(D)] + anywhere(8),
        out_specs=tile(D),
        out_shape=Shape((tokens, D), f32),
        scratch_shapes=[pltpu.VMEM((D, 3 * D), bf16), pltpu.SemaphoreType.DMA((32,))],
        compiler_params=params(60),
        cost_estimate=cost(9),
        name="grad_hidden",
    )(low, grad_branch, *blocks)


def gather_plain(w_qkv, w_out, w_in, w_back, vectors):
    def whole(piece):
        return lax.all_gather(
            lax.all_gather(piece, "narrow", axis=1, tiled=True), "wide", axis=0, tiled=True
        )

    full = tuple(whole(piece) for piece in (w_qkv, w_out, w_in, w_back))
    return full + (lax.all_gather(vectors, ALL, axis=0, tiled=True).reshape(12, D),)


def tie(*values):
    return lax.optimization_barrier(values)


def unfold(table, order, shape):
    return table.reshape((2, 2, 2, 4) + table.shape[3:]).transpose(order).reshape(shape)


def scatter_whole(matrix):
    part = lax.psum_scatter(matrix, "wide", scatter_dimension=0, tiled=True)
    part = lax.psum_scatter(part, "narrow", scatter_dimension=1, tiled=True)
    return part.astype(f32)


def per_device(hidden, segment, w_qkv, w_out, w_in, w_back, vectors, cotangent):
    (qkv,) = pair_up([w_qkv], [send(w_qkv, core=1)], vectors)
    rest = [w_out, w_in, w_back]
    other_rest = [send(piece, core=1) for piece in rest]
    qkv, other_rest, segment = tie(qkv, other_rest, segment)
    key_marks, query_marks = segment_marks(segment)
    qkv_line = gather_z(qkv)
    out, inner, back = pair_up(rest, other_rest)
    mid = jnp.concatenate([inner, out], 1)
    qkv_line, mid, back, key_marks, query_marks = tie(
        jnp.stack(qkv_line), mid, back, key_marks, query_marks
    )

    qkv_blocks = gather_chips(qkv_line)
    mid_line = gather_z(mid)
    next_back = send(back, z=1)
    qkv_blocks, mid_line, back, next_back = tie(qkv_blocks, mid_line, back, next_back)

    mid_blocks = gather_chips(jnp.stack(mid_line))
    qkv_blocks = gather_cores(qkv_blocks)
    back_two = jnp.stack([back, next_back])
    all_vectors = place_vectors(qkv_blocks)
    back_two, all_vectors = tie(back_two, all_vectors)
    far_two = send(back_two, z=2)
    attended = attend(position, hidden, all_vectors, key_marks, query_marks, qkv_blocks)
    attended, mid_blocks, far_two = tie(attended, mid_blocks, far_two)
    packed, att, att_t, probs = attended

    back_blocks = gather_chips(jnp.concatenate([back_two, far_two]))
    mid_blocks = gather_cores(mid_blocks)
    inner_outs = inner_forward(position, att, hidden, all_vectors, mid_blocks)
    inner_outs, back_blocks = tie(inner_outs, back_blocks)
    back_blocks = gather_cores(back_blocks)
    first_low, normed, inverse, activated, slope = inner_outs

    output, grad_second, sums_second, *tables_back = outer_forward(
        position, activated, normed, cotangent, all_vectors, back_blocks
    )

    received_back = [send(block, core=1) for block in tables_back[4:]]
    parts_back = chip_parts(tables_back[:4], received_back)
    parts_back, grad_second = tie(parts_back, grad_second)
    others_back = chip_sends(parts_back)
    back_outs = backward(
        position,
        grad_second,
        slope,
        normed,
        inverse,
        first_low,
        att_t,
        all_vectors,
        mid_blocks,
        back_blocks,
    )
    back_outs, others_back = tie(back_outs, others_back)
    grad_att, grad_branch, sums_first, sums_inner, *tables_mid = back_outs

    received_mid = [send(block, core=1) for block in tables_mid[4:]]
    near_back, far_back = line_halves(parts_back[0], others_back)
    parts_mid = chip_parts(tables_mid[:4], received_mid)
    parts_mid, grad_att, near_back, far_back = tie(parts_mid, grad_att, near_back, far_back)

    plane_mid = [send(parts_mid[1], x=1), send(parts_mid[2], y=1)]
    corner_mid = send(parts_mid[3], x=1, y=1)
    far_back = send(far_back, z=2)
    packed_low, sums_zero = attend_back(0, packed, grad_att, probs)
    packed_low, sums_one = attend_back(1, packed, grad_att, probs, packed_low)
    tables_qkv = grad_qkv(
        position, hidden, packed_low, sums_zero, sums_one, sums_first, sums_inner, sums_second
    )
    tables_qkv, far_back, plane_mid = tie(tables_qkv, far_back, plane_mid)
    kept_qkv, sent_qkv = tables_qkv[:4], tables_qkv[4:]

    received_qkv = [send(block, core=1) for block in sent_qkv]
    parts_qkv = chip_parts_of(kept_qkv, received_qkv)
    parts_qkv, grad_branch, near_back, corner_mid = tie(
        parts_qkv, grad_branch, near_back, corner_mid
    )
    others_qkv = chip_sends(parts_qkv)
    near_mid, far_mid = line_halves(parts_mid[0], plane_mid + [corner_mid])
    far_mid = send(far_mid, z=2)
    near_back = near_parts(near_back, far_back)
    next_back = send(near_back[1], z=1)
    near_back, grad_branch = tie(near_back, grad_branch)
    grad_hidden = grad_of_hidden(position, packed_low, grad_branch, qkv_blocks)
    grad_hidden, far_mid, next_back = tie(grad_hidden, far_mid, next_back)

    own_back = wide_sum(near_back[0], next_back).T
    near_mid = near_parts(near_mid, far_mid)
    next_mid = send(near_mid[1], z=1)
    others_qkv, near_mid = tie(others_qkv, near_mid)
    line_qkv = line_parts(parts_qkv[0], others_qkv)
    lines_qkv = line_sends(line_qkv)
    own_mid = wide_sum(near_mid[0], next_mid)
    own_in = jnp.concatenate([own_mid[:, :D], own_mid[:, D : 2 * D]], 0)
    own_out = swap_columns(own_mid[:, 2 * D :])
    own_in, own_out, own_back, lines_qkv = tie(own_in, own_out, own_back, lines_qkv)
    own_qkv = wide_sum(line_qkv[0], *lines_qkv)
    own_vectors = cut_vectors(position, own_qkv[:4, 1152:])
    own_qkv = swap_columns(own_qkv[:, :1152])
    return (output, grad_hidden, own_qkv, own_out, own_in, own_back, own_vectors)


def per_device_plain(hidden, segment, w_qkv, w_out, w_in, w_back, vectors, cotangent):
    key_marks, query_marks = segment_marks(segment)
    full_qkv, full_out, full_in, full_back, all_vectors = gather_plain(
        w_qkv, w_out, w_in, w_back, vectors
    )
    qkv_blocks = split_blocks(full_qkv, 48, 1152)
    mid_blocks = [
        jnp.concatenate(pair, 2)
        for pair in zip(split_blocks(full_in, 48, 1536), split_blocks(full_out, 48, 384))
    ]
    back_pieces = split_blocks(full_back, 192, 384)
    packed, att, att_t, probs = attend(
        origin, hidden, all_vectors, key_marks, query_marks, qkv_blocks
    )
    first_low, normed, inverse, activated, slope = inner_forward(
        origin, att, hidden, all_vectors, mid_blocks
    )
    output, grad_second, sums_second, *back_table = outer_forward(
        origin, activated, normed, cotangent, all_vectors, back_pieces
    )
    grad_att, grad_branch, sums_first, sums_inner, *tables = backward(
        origin,
        grad_second,
        slope,
        normed,
        inverse,
        first_low,
        att_t,
        all_vectors,
        mid_blocks,
        back_pieces,
    )
    mid_table = jnp.stack(tables).reshape(2, 4, 4, 48, 1920)
    packed_low, sums_zero = attend_back(0, packed, grad_att, probs)
    packed_low, sums_one = attend_back(1, packed, grad_att, probs, packed_low)
    grad_hidden = grad_of_hidden(origin, packed_low, grad_branch, qkv_blocks)
    tables = grad_qkv(
        origin, hidden, packed_low, sums_zero, sums_one, sums_first, sums_inner, sums_second
    )
    grad_vectors = jnp.concatenate(
        [(sums_zero + sums_one)[0, :2], sums_first[:3], sums_inner[:4], sums_second[:3]], 0
    )
    qkv_table = jnp.stack(tables)
    qkv_table = qkv_table.reshape(2, 4, 4, 48, 1280)
    halves = jnp.stack([mid_table[..., :D], mid_table[..., D : 2 * D]], 4)
    own_qkv = scatter_whole(unfold(qkv_table[..., :1152], (3, 1, 0, 4, 2, 5), (D, 3 * D)))
    own_out = scatter_whole(unfold(mid_table[..., 2 * D :], (3, 1, 0, 4, 2, 5), (D, D)))
    own_in = scatter_whole(unfold(halves, (3, 1, 4, 5, 2, 0, 6), (D, FF)))
    back_table = jnp.stack(back_table).reshape(2, 4, 4, 192, 384)
    back_t = unfold(back_table, (2, 0, 4, 3, 1, 5), (D, FF))
    own_back = scatter_whole(back_t.T)
    own_vectors = lax.psum_scatter(
        grad_vectors.reshape(-1), ALL, scatter_dimension=0, tiled=True
    )
    return (output, grad_hidden, own_qkv, own_out, own_in, own_back, own_vectors)


def solution(mesh):
    trees = mesh.shape["wide"] == 8 and mesh.shape["narrow"] == 4
    return jax.shard_map(
        per_device if trees else per_device_plain,
        mesh=mesh,
        in_specs=(P(ALL, None),) * 2 + (P("wide", "narrow"),) * 4 + (P(ALL), P(ALL, None)),
        out_specs=(P(ALL, None),) * 2 + (P("wide", "narrow"),) * 4 + (P(ALL),),
        check_vma=False,
    )
```

```python
import functools

import jax
import jax.numpy as jnp
from jax import lax
from jax.experimental import pallas as pl
from jax.experimental.pallas import tpu as pltpu
from jax.sharding import PartitionSpec as P

D = 768
HEADS = 12
FF = 3072
TILE = 256
ALL = ("wide", "narrow")
CHIP_STEPS = ((0, 0), (1, 0), (0, 1), (1, 1))
bf16, f32 = jnp.bfloat16, jnp.float32
Shape = jax.ShapeDtypeStruct

epsilon = 1e-06


def cost(us):
    return pl.CostEstimate(flops=0 * us, bytes_accessed=0, transcendentals=0)


def params(mib=60):
    return pltpu.CompilerParams(vmem_limit_bytes=mib * 2**20)


def send(values, z=0, y=0, x=0, core=0):
    flip_wide, flip_narrow = 2 * z + y, 2 * x + core
    pairs = [
        (w * 4 + n, (w ^ flip_wide) * 4 + (n ^ flip_narrow)) for w in range(8) for n in range(4)
    ]
    return lax.ppermute(values, ALL, pairs)


def position():
    wide, narrow = lax.axis_index("wide"), lax.axis_index("narrow")
    return wide // 2, wide % 2, narrow // 2, narrow % 2


def origin():
    zero = jnp.int32(0)
    return zero, zero, zero, zero


def gather_z(values):
    return [values] + [send(values, z=k) for k in (1, 2, 3)]


def gather_chips(lines):
    return [lines] + [send(lines, x=i, y=j) for i, j in CHIP_STEPS[1:]]


def gather_cores(blocks):
    return blocks + [send(block, core=1) for block in blocks]


def pair_kernel(count, *refs):
    core = lax.rem(lax.axis_index("narrow"), 2)
    more, outs = refs[2 * count : -count], refs[-count:]
    for own, other, out in zip(refs[:count], refs[count : 2 * count], outs):
        rows, columns = own.shape[0] // 2, own.shape[1]
        half = pl.ds(pl.multiple_of(core * rows, rows), rows)

        @pl.when(core == 0)
        def _(own=own, other=other, out=out, half=half, columns=columns):
            out[:, :columns] = own[half, :]
            out[:, columns : 2 * columns] = other[half, :]

        @pl.when(core == 1)
        def _(own=own, other=other, out=out, half=half, columns=columns):
            out[:, :columns] = other[half, :]
            out[:, columns : 2 * columns] = own[half, :]

    for vector in more:
        rest, parts = vector[...], []
        for _ in range(3):
            parts.append(rest.astype(bf16).astype(f32))
            rest = rest - parts[-1]
        outs[0][:, 1152:] = rows_of(48, *parts).astype(bf16)


def pair_up(pieces, others, vectors=None):
    more = [0] * len(pieces)
    rows = ()
    if vectors is not None:
        rows = (jnp.pad(vectors, (0, 384 - vectors.shape[0])).reshape(3, 128),)
        more[0] = 128
    return pl.pallas_call(
        functools.partial(pair_kernel, len(pieces)),
        out_shape=[
            Shape((piece.shape[0] // 2, piece.shape[1] * 2 + extra), piece.dtype)
            for piece, extra in zip(pieces, more)
        ],
        cost_estimate=cost(2),
        name="pair_up",
    )(*pieces, *others, *rows)


def block_copies(place, blocks, left, out, sems):
    z, y, x, core = place()
    rows, width = blocks[0].shape[1], out.shape[1] // 2
    copies = []
    for other in range(2):
        for step, (i, j) in enumerate(CHIP_STEPS):
            for k in range(4):
                row = (((z ^ k) * 2 + (y ^ j)) * 2 + (core ^ other)) * rows
                copies.append(
                    pltpu.make_async_copy(
                        blocks[other * 4 + step].at[k, :, pl.ds(left, width)],
                        out.at[
                            pl.ds(pl.multiple_of(row, rows), rows),
                            pl.ds(pl.multiple_of((x ^ i) * width, width), width),
                        ],
                        sems.at[len(copies)],
                    )
                )
    return copies


def start(copies):
    for copy in copies:
        copy.start()


def wait(copies):
    for copy in copies:
        copy.wait()


def anywhere(count):
    return [pl.BlockSpec(memory_space=pl.ANY)] * count


def split_blocks(matrix, rows, columns):
    parts = matrix.reshape(4, 2, 2, rows, 2, columns).transpose(2, 1, 4, 0, 3, 5)
    return [parts[other, j, i] for other in range(2) for i, j in CHIP_STEPS]


def place_kernel(*refs):
    z, y, x, core = position()
    out = refs[8]
    for other in range(2):
        for step, (i, j) in enumerate(CHIP_STEPS):
            for k in range(4):
                row = ((z ^ k) * 2 + (y ^ j)) * 4 + (x ^ i) * 2 + (core ^ other)
                parts = refs[other * 4 + step][k].astype(f32)
                out[row] = parts[:3] + parts[3:6] + parts[6:9]


def place_vectors(blocks):
    table = pl.pallas_call(
        place_kernel,
        grid=(1,),
        in_specs=[pl.BlockSpec((4, 16, 128), lambda i: (0, 0, 9))] * 8,
        out_specs=fixed((32, 3, 128)),
        out_shape=Shape((32, 3, 128), f32),
        cost_estimate=cost(1),
        name="place_vectors",
    )(*blocks)
    return table.reshape(32, 384)[:, :288].reshape(12, D)


def wide_sum(*terms):
    return functools.reduce(lambda a, b: a + b, [t.astype(f32) for t in terms])


def chip_parts(kept, received):
    return [wide_sum(kept[s], received[s]).astype(bf16) for s in range(4)]


def chip_kernel(*refs):
    for kept, received, out in zip(refs[:4], refs[4:8], refs[8:]):
        out[...] = wide_sum(kept[...], received[...]).astype(bf16)


def chip_parts_of(kept, received):
    rows, columns = kept[0].shape[1:]
    line = pl.BlockSpec((1, rows, columns), lambda k: (k, 0, 0))
    return pl.pallas_call(
        chip_kernel,
        grid=(4,),
        in_specs=[line] * 8,
        out_specs=[line] * 4,
        out_shape=[Shape((4, rows, columns), bf16)] * 4,
        compiler_params=params(32),
        cost_estimate=cost(3),
        name="chip_parts",
    )(*kept, *received)


def chip_sends(parts):
    return [send(parts[s], x=i, y=j) for s, (i, j) in enumerate(CHIP_STEPS) if s]


def line_kernel(far, *refs):
    terms, outs = refs[:4], refs[4:]
    for k in range(4):
        total = wide_sum(*[term[k] for term in terms]).astype(bf16)
        if far and k >= 2:
            outs[2][k - 2] = total
        else:
            outs[k][...] = total


def line_parts(own, others, far=False):
    piece = Shape(own.shape[1:], bf16)
    shapes = [piece] * 2 + [Shape((2,) + own.shape[1:], bf16)] if far else [piece] * 4
    return pl.pallas_call(
        functools.partial(line_kernel, far),
        out_shape=shapes,
        compiler_params=params(32),
        cost_estimate=cost(2),
        name="line_parts",
    )(own, *others)


def line_sends(line):
    return [send(line[k], z=k) for k in (1, 2, 3)]


def line_halves(own, others):
    *near, far = line_parts(own, others, True)
    return near, far


def near_parts(near, received):
    return [wide_sum(near[k], received[k]).astype(near[k].dtype) for k in range(2)]


def swap_columns(summed):
    core = lax.axis_index("narrow") % 2
    columns = summed.shape[1] // 2
    left, right = summed[:, :columns], summed[:, columns:]
    mine = jnp.where(core == 0, left, right)
    other = send(jnp.where(core == 0, right, left).astype(bf16), core=1).astype(f32)
    return jnp.concatenate(
        [jnp.where(core == 0, mine, other), jnp.where(core == 0, other, mine)], 0
    )


def dot(left_side, right_side):
    return jnp.dot(left_side, right_side, preferred_element_type=f32)


def dot_t(left_side, right_side):
    return lax.dot_general(
        left_side, right_side, (((1,), (1,)), ((), ())), preferred_element_type=f32
    )


def column_sum(values):
    return jnp.sum(values, 0, keepdims=True)


def normalize(values):
    center = values - jnp.mean(values, -1, keepdims=True)
    inverse = lax.rsqrt(jnp.mean(center * center, -1, keepdims=True) + epsilon)
    return center * inverse, inverse


def normalize_back(grad_norm, normed, inverse):
    return inverse * (
        grad_norm
        - jnp.mean(grad_norm, -1, keepdims=True)
        - normed * jnp.mean(grad_norm * normed, -1, keepdims=True)
    )


def smooth(values):
    density = jnp.exp(-0.5 * values * values) * 0.3989422804014327
    below = 0.5 + 0.5 * lax.erf(values * 0.7071067811865476)
    return values * below, below + values * density


def fixed(shape):
    return pl.BlockSpec(shape, lambda i: (0,) * len(shape))


def tile(columns, rows=TILE):
    return pl.BlockSpec((rows, columns), lambda i: (i, 0))


def rows_of(count, *parts):
    missing = count - sum(part.shape[0] for part in parts)
    return jnp.concatenate(list(parts) + [jnp.zeros((missing, parts[0].shape[1]), f32)], 0)


def segment_marks(segment):
    kinds = lax.broadcasted_iota(jnp.int32, (1, 64), 1)
    mark = (segment.reshape(-1, 1) == kinds).astype(bf16)
    tall = lax.broadcasted_iota(jnp.int32, (1, 64, 1), 1)
    away = (segment[:, None, :] != tall) & (tall < 4)
    return jnp.concatenate([mark, mark], 1), jnp.where(away, -(2.0**30), 0.0).astype(bf16)


def attend_kernel(place, *refs):
    hidden, vectors, key_marks, query_marks = refs[:4]
    blocks, (packed, att, att_t, probs, weight, sems) = refs[4:12], refs[12:]

    @pl.when(pl.program_id(0) == 0)
    def _():
        copies = block_copies(place, blocks, 0, weight, sems)
        start(copies)
        wait(copies)

    length = hidden.shape[0]
    for part in range(3):
        columns = slice(part * D, (part + 1) * D)
        block = dot(hidden[...], weight[:, columns])
        if part != 1:
            block = block + vectors[part // 2 : part // 2 + 1, :]
        block = block.astype(bf16)
        if part == 0:
            block = block * jnp.asarray(0.125, bf16)
        packed[:, columns] = block
    lanes = lax.broadcasted_iota(jnp.int32, (length, 128), 1)

    def pair(p, _):
        at = pl.multiple_of(p * 128, 128)
        q_t = packed[:, pl.ds(at, 128)].T
        k = packed[:, pl.ds(D + at, 128)]
        v_t = packed[:, pl.ds(2 * D + at, 128)].T
        scores = []
        for odd in range(2):
            keys = jnp.where((lanes >= 64) == bool(odd), k, key_marks[...])
            own = q_t[64 * odd : 64 * odd + 64]
            marks = query_marks[0]
            scores.append(dot(keys, jnp.concatenate([marks, own] if odd else [own, marks], 0)))
        outs = []
        for odd in range(2):
            weights = jnp.exp(scores[odd] - jnp.max(scores[odd], 0, keepdims=True))
            low = (weights * (1.0 / column_sum(weights))).astype(bf16)
            probs[p * 2 + odd] = low
            outs.append(dot(v_t[64 * odd : 64 * odd + 64], low))
        out = jnp.concatenate(outs, 0).astype(bf16)
        att_t[pl.ds(at, 128), :] = out
        att[:, pl.ds(at, 128)] = out.T
        return 0

    lax.fori_loop(0, HEADS // 2, pair, 0, unroll=True)


def attend(place, hidden, vectors, key_marks, query_marks, blocks):
    rows, length = query_marks.shape[0], query_marks.shape[2]
    tokens = rows * length
    return pl.pallas_call(
        functools.partial(attend_kernel, place),
        grid=(rows,),
        in_specs=[
            tile(D, length),
            fixed((12, D)),
            tile(128, length),
            pl.BlockSpec((1, 64, length), lambda i: (i, 0, 0)),
        ]
        + anywhere(8),
        scratch_shapes=[pltpu.VMEM((D, 3 * D), bf16), pltpu.SemaphoreType.DMA((32,))],
        out_specs=[
            tile(3 * D, length),
            tile(D, length),
            pl.BlockSpec((D, length), lambda i: (0, i)),
            pl.BlockSpec((HEADS, length, length), lambda i: (i, 0, 0)),
        ],
        out_shape=[
            Shape((tokens, 3 * D), bf16),
            Shape((tokens, D), bf16),
            Shape((D, tokens), bf16),
            Shape((rows * HEADS, length, length), bf16),
        ],
        compiler_params=params(60),
        cost_estimate=cost(20),
        name="attend",
    )(hidden, vectors, key_marks, query_marks, *blocks)


def inner_kernel(place, *refs):
    att, hidden, vectors = refs[:3]
    blocks, (first_low, normed, inverse, activated, slope) = refs[3:11], refs[11:16]
    w_in, w_out, in_sems, out_sems = refs[16:]
    first_step = pl.program_id(0) == 0

    def row(i):
        return vectors[i : i + 1, :]

    def copies_in():
        return block_copies(place, blocks, 0, w_in, in_sems)

    @pl.when(first_step)
    def _():
        copies = block_copies(place, blocks, 1536, w_out, out_sems)
        start(copies)
        start(copies_in())
        wait(copies)

    n1, r1 = normalize(hidden[...].astype(f32) + dot(att[...], w_out[...]) + row(2))
    low = (n1 * row(3) + row(4)).astype(bf16)
    first_low[...] = low
    normed[...] = n1.astype(bf16)
    inverse[...] = jnp.broadcast_to(r1, inverse.shape)

    @pl.when(first_step)
    def _():
        wait(copies_in())

    for c in range(FF // D):
        columns = slice(c * D, c * D + D)
        act, back = smooth(dot(low, w_in[:, columns]) + row(5 + c))
        activated[:, columns] = act.astype(bf16)
        slope[:, columns] = back.astype(bf16)


def inner_forward(place, att, hidden, vectors, blocks):
    tokens = hidden.shape[0]
    return pl.pallas_call(
        functools.partial(inner_kernel, place),
        grid=(tokens // TILE,),
        in_specs=[tile(D)] * 2 + [fixed((12, D))] + anywhere(8),
        out_specs=[tile(D), tile(D), tile(128), tile(FF), tile(FF)],
        out_shape=[
            Shape((tokens, D), bf16),
            Shape((tokens, D), bf16),
            Shape((tokens, 128), f32),
            Shape((tokens, FF), bf16),
            Shape((tokens, FF), bf16),
        ],
        scratch_shapes=[
            pltpu.VMEM((D, FF), bf16),
            pltpu.VMEM((D, D), bf16),
            pltpu.SemaphoreType.DMA((32,)),
            pltpu.SemaphoreType.DMA((32,)),
        ],
        compiler_params=params(60),
        cost_estimate=cost(16),
        name="inner_forward",
    )(att, hidden, vectors, *blocks)


def outer_kernel(place, *refs):
    act, normed, cotangent, vectors = refs[:4]
    blocks, (output, grad_second, sums) = refs[4:12], refs[12:15]
    outs, (w_back, activated, grad_t, sems) = refs[15:23], refs[23:]
    step = pl.program_id(0)
    z, y, x, core = place()

    def row(i):
        return vectors[i : i + 1, :]

    @pl.when(step == 0)
    def _():
        copies = block_copies(place, blocks, 0, w_back, sems)
        start(copies)
        wait(copies)

    here = pl.ds(pl.multiple_of(step * TILE, TILE), TILE)
    activated[here, :] = act[...]
    outward = normed[...].astype(f32) * row(3) + row(4) + dot(act[...], w_back[...]) + row(9)
    n2, r2 = normalize(outward)
    output[...] = (n2 * row(10) + row(11)).astype(bf16)
    cot = cotangent[...].astype(f32)
    g2 = normalize_back(cot * row(10), n2, r2)
    grad_second[...] = g2.astype(bf16)
    part = rows_of(8, column_sum(g2), column_sum(cot * n2), column_sum(cot))

    @pl.when(step == 0)
    def _():
        sums[...] = part

    @pl.when(step > 0)
    def _():
        sums[...] += part

    g2_t = g2.astype(bf16).T
    for n in range(4):
        at = ((n % 2) ^ core) * 2 + ((n // 2) ^ x)
        piece = g2_t[n * 192 : n * 192 + 192]
        grad_t[pl.ds(pl.multiple_of(at * 192, 192), 192), here] = piece

    @pl.when(step == pl.num_programs(0) - 1)
    def _():
        for k in range(4):
            columns = pl.ds(pl.multiple_of((z ^ k) * D, D), D)
            res = dot(grad_t[...], activated[:, columns]).astype(bf16)
            for other in range(2):
                for i in range(2):
                    at = (other * 2 + i) * 192
                    pieces = [res[at : at + 192, half * 384 : half * 384 + 384] for half in range(2)]
                    for bit in range(2):

                        @pl.when(y == bit)
                        def _(other=other, i=i, k=k, pieces=pieces, bit=bit):
                            outs[other * 4 + i][k] = pieces[bit]
                            outs[other * 4 + i + 2][k] = pieces[1 - bit]


def outer_forward(place, activated, normed, cotangent, vectors, blocks):
    tokens = normed.shape[0]
    return pl.pallas_call(
        functools.partial(outer_kernel, place),
        grid=(tokens // TILE,),
        in_specs=[tile(FF), tile(D), tile(D), fixed((12, D))] + anywhere(8),
        out_specs=[tile(D), tile(D), fixed((8, D))] + [fixed((4, 192, 384))] * 8,
        out_shape=[
            Shape((tokens, D), bf16),
            Shape((tokens, D), bf16),
            Shape((8, D), f32),
        ]
        + [Shape((4, 192, 384), bf16)] * 8,
        scratch_shapes=[
            pltpu.VMEM((FF, D), bf16),
            pltpu.VMEM((tokens, FF), bf16),
            pltpu.VMEM((D, tokens), bf16),
            pltpu.SemaphoreType.DMA((32,)),
        ],
        compiler_params=params(40),
        cost_estimate=cost(18),
        name="outer_forward",
    )(activated, normed, cotangent, vectors, *blocks)


def backward_kernel(place, *refs):
    grad_second, slope, normed, inverse, first_low, att_t, vectors = refs[:7]
    blocks, back_blocks = refs[7:15], refs[15:23]
    grad_att, grad_branch, sums, sums_inner = refs[23:27]
    outs = refs[27:35]
    w_in, w_out, w_back, inner_low, first_t, grad_low, turned = refs[35:42]
    in_sems, out_sems, back_sems = refs[42:]
    step = pl.program_id(0)
    z, y, x, core = place()
    here = pl.ds(pl.multiple_of(step * TILE, TILE), TILE)

    def compute(first_step):
        if first_step:
            copies_back = block_copies(place, back_blocks, 0, w_back, back_sems)
            copies_in = block_copies(place, blocks, 0, w_in, in_sems)
            copies_out = block_copies(place, blocks, 1536, w_out, out_sems)
            start(copies_back)
            start(copies_in)
            start(copies_out)
        g2_low = grad_second[...]
        grad_first = g2_low.astype(f32)
        inner_sums = []
        for c in range(FF // D):
            columns = slice(c * D, c * D + D)
            if first_step and c == 0:
                wait(copies_back)
            gi = dot_t(g2_low, w_back[columns, :]) * slope[:, columns].astype(f32)
            inner_sums.append(column_sum(gi))
            gi = gi.astype(bf16)
            inner_low[here, columns] = gi
            if first_step and c == 0:
                wait(copies_in)
            grad_first = grad_first + dot_t(gi, w_in[:, columns])
        n1 = normed[...].astype(f32)
        g1 = normalize_back(grad_first * vectors[3:4, :], n1, inverse[:, :1])
        g1_low = g1.astype(bf16)
        grad_branch[...] = g1_low
        grad_low[here, :] = g1_low
        if first_step:
            wait(copies_out)
        grad_att[...] = dot_t(g1_low, w_out[...]).astype(bf16)
        part = rows_of(8, column_sum(g1), column_sum(grad_first * n1), column_sum(grad_first))
        part_inner = rows_of(8, *inner_sums)
        if first_step:
            sums[...] = part
            sums_inner[...] = part_inner
        else:
            sums[...] += part
            sums_inner[...] += part_inner
        low_t = first_low[...].T
        for w in range(8):
            at = ((w % 2) ^ y) * 4 + ((w // 2) ^ z)
            piece = low_t[w * 96 : w * 96 + 96]
            first_t[pl.ds(pl.multiple_of(at * 96, 96), 96), here] = piece
        turn_rows(place, att_t, turned, here)

    @pl.when(step == 0)
    def _():
        compute(True)

    @pl.when(step > 0)
    def _():
        compute(False)

    @pl.when(step == pl.num_programs(0) - 1)
    def _():
        for i in range(2):
            for other in range(2):
                at = ((x ^ i) * 2 + (core ^ other)) * D
                res = dot(first_t[...], inner_low[:, pl.ds(pl.multiple_of(at, D), D)])
                res = res.astype(bf16)
                for j in range(2):
                    for k in range(4):
                        at = (j * 4 + k) * 96
                        outs[other * 4 + i + 2 * j][k, :, :D] = res[at : at + 48]
                        outs[other * 4 + i + 2 * j][k, :, D : 2 * D] = res[at + 48 : at + 96]
        res = dot(turned[...], grad_low[...]).astype(bf16)
        for bit in range(2):

            @pl.when(x == bit)
            def _(bit=bit):
                for other in range(2):
                    for j in range(2):
                        for k in range(4):
                            at = (other * 8 + j * 4 + k) * 48
                            for half in range(2):
                                piece = res[at : at + 48, half * 384 : half * 384 + 384]
                                outs[other * 4 + (half ^ bit) + 2 * j][k, :, 2 * D :] = piece


def backward(place, grad_second, slope, normed, inverse, first_low, att_t, vectors, *weights):
    blocks, back_blocks = weights
    tokens = normed.shape[0]
    outs = [(4, 48, 1920)] * 8
    return pl.pallas_call(
        functools.partial(backward_kernel, place),
        grid=(tokens // TILE,),
        in_specs=[tile(D), tile(FF), tile(D), tile(128), tile(D)]
        + [pl.BlockSpec((D, TILE), lambda i: (0, i)), fixed((12, D))]
        + anywhere(16),
        out_specs=[tile(D), tile(D)] + [fixed(s) for s in [(8, D)] * 2 + outs],
        out_shape=[Shape((tokens, D), bf16), Shape((tokens, D), bf16)]
        + [Shape((8, D), f32)] * 2
        + [Shape(s, bf16) for s in outs],
        scratch_shapes=[
            pltpu.VMEM((D, FF), bf16),
            pltpu.VMEM((D, D), bf16),
            pltpu.VMEM((FF, D), bf16),
            pltpu.VMEM((tokens, FF), bf16),
            pltpu.VMEM((D, tokens), bf16),
            pltpu.VMEM((tokens, D), bf16),
            pltpu.VMEM((D, tokens), bf16),
        ]
        + [pltpu.SemaphoreType.DMA((32,))] * 3,
        compiler_params=params(32),
        cost_estimate=cost(22),
        name="backward",
    )(grad_second, slope, normed, inverse, first_low, att_t, vectors, *blocks, *back_blocks)


def turn_rows(place, source, turned, columns=slice(None)):
    z, y, _, core = place()
    for w in range(8):
        for half in range(2):
            at = (half ^ core) * 8 + ((w % 2) ^ y) * 4 + ((w // 2) ^ z)
            piece = (w * 2 + half) * 48
            rows = pl.ds(pl.multiple_of(at * 48, 48), 48)
            turned[rows, columns] = source[piece : piece + 48, :]


def attend_back_kernel(packed, grad_att, probs, grad_low, sums):
    length = packed.shape[0]
    lanes = lax.broadcasted_iota(jnp.int32, (length, 128), 1)
    zero = jnp.zeros((length, 128), bf16)
    blank = jnp.zeros((64, length), bf16)

    def pair(p, _):
        at = pl.multiple_of(p * 128, 128)
        q = packed[:, pl.ds(at, 128)]
        k_t = packed[:, pl.ds(D + at, 128)].T
        v = packed[:, pl.ds(2 * D + at, 128)]
        g = grad_att[:, pl.ds(at, 128)]
        g_t = g.T
        grad_probs = []
        for odd in range(2):
            own = g_t[64 * odd : 64 * odd + 64]
            grad_probs.append(dot(v, jnp.concatenate([blank, own] if odd else [own, blank], 0)))
        dk = dv = 0.0
        dq_t = []
        for odd in range(2):
            mine = (lanes >= 64) == bool(odd)
            low = probs[p * 2 + odd]
            wide = low.astype(f32)
            gp = grad_probs[odd]
            ds = (wide * (gp - column_sum(wide * gp))).astype(bf16)
            dv = dv + dot(low, jnp.where(mine, g, zero))
            dk = dk + dot(ds, jnp.where(mine, q, zero))
            dq_t.append(dot(k_t[64 * odd : 64 * odd + 64], ds))
        dq = jnp.concatenate(dq_t, 0).T * 0.125
        sums[0, :, pl.ds(at, 128)] = rows_of(8, column_sum(dq), column_sum(dv))
        grad_low[:, pl.ds(at, 128)] = dq.astype(bf16)
        grad_low[:, pl.ds(D + at, 128)] = dk.astype(bf16)
        grad_low[:, pl.ds(2 * D + at, 128)] = dv.astype(bf16)
        return 0

    lax.fori_loop(0, HEADS // 2, pair, 0, unroll=True)


def attend_back(row, packed, grad_att, probs, low=None):
    length = probs.shape[1]
    kernel, more, specs, alias = attend_back_kernel, (), [], {}
    if low is not None:
        more, specs, alias = (low,), [pl.BlockSpec(memory_space=pl.ANY)], {3: 0}

        def kernel(packed, grad_att, probs, low, grad_low, sums):
            attend_back_kernel(packed, grad_att, probs, grad_low, sums)

    return pl.pallas_call(
        kernel,
        grid=(1,),
        in_specs=[
            pl.BlockSpec((length, 3 * D), lambda i: (row, 0)),
            pl.BlockSpec((length, D), lambda i: (row, 0)),
            pl.BlockSpec((HEADS, length, length), lambda i: (row, 0, 0)),
        ]
        + specs,
        out_specs=[
            pl.BlockSpec((length, 3 * D), lambda i: (row, 0)),
            pl.BlockSpec((1, 8, D), lambda i: (0, 0, 0)),
        ],
        out_shape=[Shape(packed.shape, bf16), Shape((1, 8, D), f32)],
        input_output_aliases=alias,
        compiler_params=params(32),
        cost_estimate=cost(12),
        name="attend_back",
    )(packed, grad_att, probs, *more)


def grad_qkv_kernel(place, hidden, low, *refs):
    sums_zero, sums_one, sums_first, sums_inner, sums_second = refs[:5]
    outs, turned, groups = refs[5:13], refs[13], refs[14]
    z, y, x, core = place()
    turn_rows(place, hidden[...].T, turned)
    rows = [sums_zero[0, i : i + 1, :] + sums_one[0, i : i + 1, :] for i in range(2)]
    rows += [sums_first[i : i + 1, :] for i in range(3)]
    rows += [sums_inner[i : i + 1, :] for i in range(4)]
    rows += [sums_second[i : i + 1, :] for i in range(3)]
    for group in range(72):
        column = group % 6 * 128
        groups[group] = rows[group // 6][:, column : column + 128]
    for group in range(72, 76):
        groups[group] = jnp.zeros((1, 128), f32)
    for i in range(2):
        columns = pl.ds(pl.multiple_of((x ^ i) * 1152, 128), 1152)
        res = dot(turned[...], low[:, columns]).astype(bf16)
        for other in range(2):
            for j in range(2):
                out = outs[other * 4 + i + 2 * j]
                for k in range(4):
                    at = (other * 8 + j * 4 + k) * 48
                    out[k, :, :1152] = res[at : at + 48]
                    device = ((z ^ k) * 2 + (y ^ j)) * 4 + (x ^ i) * 2 + (core ^ other)
                    group = (9 * device) // 4
                    part = jnp.concatenate([groups[group + q] for q in range(4)], 0)
                    out[k, :16, 1152:] = rows_of(16, part).astype(bf16)
                    out[k, 16:, 1152:] = jnp.zeros((32, 128), bf16)


def grad_qkv(place, hidden, low, *sums):
    return pl.pallas_call(
        functools.partial(grad_qkv_kernel, place),
        out_shape=[Shape((4, 48, 1280), bf16)] * 8,
        scratch_shapes=[pltpu.VMEM((D, hidden.shape[0]), bf16), pltpu.VMEM((80, 1, 128), f32)],
        compiler_params=params(32),
        cost_estimate=cost(9),
        name="grad_qkv",
    )(hidden, low, *sums)


def cut_vectors(place, groups):
    z, y, x, core = place()
    at = (((z * 2 + y) * 4 + x * 2 + core) * 288) % 128
    return lax.dynamic_slice(groups.reshape(-1), (at,), (288,))


def hidden_kernel(place, *refs):
    low, grad_branch, blocks, out, weight, sems = *refs[:2], refs[2:10], *refs[10:]

    @pl.when(pl.program_id(0) == 0)
    def _():
        copies = block_copies(place, blocks, 0, weight, sems)
        start(copies)
        wait(copies)

    out[...] = grad_branch[...].astype(f32) + dot_t(low[...], weight[...])


def grad_of_hidden(place, low, grad_branch, blocks):
    tokens = low.shape[0]
    return pl.pallas_call(
        functools.partial(hidden_kernel, place),
        grid=(tokens // TILE,),
        in_specs=[tile(3 * D), tile(D)] + anywhere(8),
        out_specs=tile(D),
        out_shape=Shape((tokens, D), f32),
        scratch_shapes=[pltpu.VMEM((D, 3 * D), bf16), pltpu.SemaphoreType.DMA((32,))],
        compiler_params=params(60),
        cost_estimate=cost(9),
        name="grad_hidden",
    )(low, grad_branch, *blocks)


def gather_plain(w_qkv, w_out, w_in, w_back, vectors):
    def whole(piece):
        return lax.all_gather(
            lax.all_gather(piece, "narrow", axis=1, tiled=True), "wide", axis=0, tiled=True
        )

    full = tuple(whole(piece) for piece in (w_qkv, w_out, w_in, w_back))
    return full + (lax.all_gather(vectors, ALL, axis=0, tiled=True).reshape(12, D),)


def tie(*values):
    return lax.optimization_barrier(values)


def unfold(table, order, shape):
    return table.reshape((2, 2, 2, 4) + table.shape[3:]).transpose(order).reshape(shape)


def scatter_whole(matrix):
    part = lax.psum_scatter(matrix, "wide", scatter_dimension=0, tiled=True)
    part = lax.psum_scatter(part, "narrow", scatter_dimension=1, tiled=True)
    return part.astype(f32)


def per_device(hidden, segment, w_qkv, w_out, w_in, w_back, vectors, cotangent):
    (qkv,) = pair_up([w_qkv], [send(w_qkv, core=1)], vectors)
    rest = [w_out, w_in, w_back]
    other_rest = [send(piece, core=1) for piece in rest]
    qkv, other_rest, segment = tie(qkv, other_rest, segment)
    key_marks, query_marks = segment_marks(segment)
    qkv_line = gather_z(qkv)
    out, inner, back = pair_up(rest, other_rest)
    mid = jnp.concatenate([inner, out], 1)
    qkv_line, mid, back, key_marks, query_marks = tie(
        jnp.stack(qkv_line), mid, back, key_marks, query_marks
    )

    qkv_blocks = gather_chips(qkv_line)
    mid_line = gather_z(mid)
    back, mid_line[2] = tie(back, mid_line[2])
    next_back = send(back, z=1)
    qkv_blocks, mid_line, back, next_back = tie(qkv_blocks, mid_line, back, next_back)

    mid_blocks = gather_chips(jnp.stack(mid_line))
    qkv_blocks = gather_cores(qkv_blocks)
    back_two = jnp.stack([back, next_back])
    all_vectors = place_vectors(qkv_blocks)
    back_two, all_vectors = tie(back_two, all_vectors)
    far_two = send(back_two, z=2)
    attended = attend(position, hidden, all_vectors, key_marks, query_marks, qkv_blocks)
    own_mid = send(mid_blocks[0], core=1)
    attended, mid_blocks, far_two, own_mid = tie(attended, mid_blocks, far_two, own_mid)
    packed, att, att_t, probs = attended

    back_blocks = gather_chips(jnp.concatenate([back_two, far_two]))
    mid_blocks = mid_blocks + [own_mid] + [send(block, core=1) for block in mid_blocks[1:]]
    inner_outs = inner_forward(position, att, hidden, all_vectors, mid_blocks)
    own_back = send(back_blocks[0], core=1)
    inner_outs, back_blocks, own_back = tie(inner_outs, back_blocks, own_back)
    back_blocks = back_blocks + [own_back] + [send(block, core=1) for block in back_blocks[1:]]
    first_low, normed, inverse, activated, slope = inner_outs

    output, grad_second, sums_second, *tables_back = outer_forward(
        position, activated, normed, cotangent, all_vectors, back_blocks
    )

    received_back = [send(block, core=1) for block in tables_back[4:]]
    parts_back = chip_parts(tables_back[:4], received_back)
    parts_back, grad_second = tie(parts_back, grad_second)
    others_back = chip_sends(parts_back)
    back_outs = backward(
        position,
        grad_second,
        slope,
        normed,
        inverse,
        first_low,
        att_t,
        all_vectors,
        mid_blocks,
        back_blocks,
    )
    back_outs, others_back = tie(back_outs, others_back)
    grad_att, grad_branch, sums_first, sums_inner, *tables_mid = back_outs

    received_mid = [send(block, core=1) for block in tables_mid[4:]]
    near_back, far_back = line_halves(parts_back[0], others_back)
    parts_mid = chip_parts(tables_mid[:4], received_mid)
    parts_mid, grad_att, near_back, far_back = tie(parts_mid, grad_att, near_back, far_back)

    plane_mid = [send(parts_mid[1], x=1), send(parts_mid[2], y=1)]
    corner_mid = send(parts_mid[3], x=1, y=1)
    far_back = send(far_back, z=2)
    packed_low, sums_zero = attend_back(0, packed, grad_att, probs)
    packed_low, sums_one = attend_back(1, packed, grad_att, probs, packed_low)
    tables_qkv = grad_qkv(
        position, hidden, packed_low, sums_zero, sums_one, sums_first, sums_inner, sums_second
    )
    tables_qkv, far_back, plane_mid = tie(tables_qkv, far_back, plane_mid)
    kept_qkv, sent_qkv = tables_qkv[:4], tables_qkv[4:]

    received_qkv = [send(block, core=1) for block in sent_qkv]
    parts_qkv = chip_parts_of(kept_qkv, received_qkv)
    parts_qkv, grad_branch, near_back, corner_mid = tie(
        parts_qkv, grad_branch, near_back, corner_mid
    )
    others_qkv = chip_sends(parts_qkv)
    near_mid, far_mid = line_halves(parts_mid[0], plane_mid + [corner_mid])
    far_mid = send(far_mid, z=2)
    near_back = near_parts(near_back, far_back)
    next_back = send(near_back[1], z=1)
    near_back, grad_branch = tie(near_back, grad_branch)
    grad_hidden = grad_of_hidden(position, packed_low, grad_branch, qkv_blocks)
    grad_hidden, far_mid, next_back = tie(grad_hidden, far_mid, next_back)

    own_back = wide_sum(near_back[0], next_back).T
    near_mid = near_parts(near_mid, far_mid)
    next_mid = send(near_mid[1], z=1)
    others_qkv, near_mid = tie(others_qkv, near_mid)
    line_qkv = line_parts(parts_qkv[0], others_qkv)
    lines_qkv = line_sends(line_qkv)
    own_mid = wide_sum(near_mid[0], next_mid)
    own_in = jnp.concatenate([own_mid[:, :D], own_mid[:, D : 2 * D]], 0)
    own_out = swap_columns(own_mid[:, 2 * D :])
    own_in, own_out, own_back, lines_qkv = tie(own_in, own_out, own_back, lines_qkv)
    own_qkv = wide_sum(line_qkv[0], *lines_qkv)
    own_vectors = cut_vectors(position, own_qkv[:4, 1152:])
    own_qkv = swap_columns(own_qkv[:, :1152])
    return (output, grad_hidden, own_qkv, own_out, own_in, own_back, own_vectors)


def per_device_plain(hidden, segment, w_qkv, w_out, w_in, w_back, vectors, cotangent):
    key_marks, query_marks = segment_marks(segment)
    full_qkv, full_out, full_in, full_back, all_vectors = gather_plain(
        w_qkv, w_out, w_in, w_back, vectors
    )
    qkv_blocks = split_blocks(full_qkv, 48, 1152)
    mid_blocks = [
        jnp.concatenate(pair, 2)
        for pair in zip(split_blocks(full_in, 48, 1536), split_blocks(full_out, 48, 384))
    ]
    back_pieces = split_blocks(full_back, 192, 384)
    packed, att, att_t, probs = attend(
        origin, hidden, all_vectors, key_marks, query_marks, qkv_blocks
    )
    first_low, normed, inverse, activated, slope = inner_forward(
        origin, att, hidden, all_vectors, mid_blocks
    )
    output, grad_second, sums_second, *back_table = outer_forward(
        origin, activated, normed, cotangent, all_vectors, back_pieces
    )
    grad_att, grad_branch, sums_first, sums_inner, *tables = backward(
        origin,
        grad_second,
        slope,
        normed,
        inverse,
        first_low,
        att_t,
        all_vectors,
        mid_blocks,
        back_pieces,
    )
    mid_table = jnp.stack(tables).reshape(2, 4, 4, 48, 1920)
    packed_low, sums_zero = attend_back(0, packed, grad_att, probs)
    packed_low, sums_one = attend_back(1, packed, grad_att, probs, packed_low)
    grad_hidden = grad_of_hidden(origin, packed_low, grad_branch, qkv_blocks)
    tables = grad_qkv(
        origin, hidden, packed_low, sums_zero, sums_one, sums_first, sums_inner, sums_second
    )
    grad_vectors = jnp.concatenate(
        [(sums_zero + sums_one)[0, :2], sums_first[:3], sums_inner[:4], sums_second[:3]], 0
    )
    qkv_table = jnp.stack(tables)
    qkv_table = qkv_table.reshape(2, 4, 4, 48, 1280)
    halves = jnp.stack([mid_table[..., :D], mid_table[..., D : 2 * D]], 4)
    own_qkv = scatter_whole(unfold(qkv_table[..., :1152], (3, 1, 0, 4, 2, 5), (D, 3 * D)))
    own_out = scatter_whole(unfold(mid_table[..., 2 * D :], (3, 1, 0, 4, 2, 5), (D, D)))
    own_in = scatter_whole(unfold(halves, (3, 1, 4, 5, 2, 0, 6), (D, FF)))
    back_table = jnp.stack(back_table).reshape(2, 4, 4, 192, 384)
    back_t = unfold(back_table, (2, 0, 4, 3, 1, 5), (D, FF))
    own_back = scatter_whole(back_t.T)
    own_vectors = lax.psum_scatter(
        grad_vectors.reshape(-1), ALL, scatter_dimension=0, tiled=True
    )
    return (output, grad_hidden, own_qkv, own_out, own_in, own_back, own_vectors)


def solution(mesh):
    trees = mesh.shape["wide"] == 8 and mesh.shape["narrow"] == 4
    return jax.shard_map(
        per_device if trees else per_device_plain,
        mesh=mesh,
        in_specs=(P(ALL, None),) * 2 + (P("wide", "narrow"),) * 4 + (P(ALL), P(ALL, None)),
        out_specs=(P(ALL, None),) * 2 + (P("wide", "narrow"),) * 4 + (P(ALL),),
        check_vma=False,
    )
```

```python
import functools

import jax
import jax.numpy as jnp
from jax import lax
from jax.experimental import pallas as pl
from jax.experimental.pallas import tpu as pltpu
from jax.sharding import PartitionSpec as P

D = 768
HEADS = 12
FF = 3072
TILE = 256
ALL = ("wide", "narrow")
CHIP_STEPS = ((0, 0), (1, 0), (0, 1), (1, 1))
bf16, f32 = jnp.bfloat16, jnp.float32
Shape = jax.ShapeDtypeStruct

epsilon = 1e-06


def cost(us):
    return pl.CostEstimate(flops=0 * us, bytes_accessed=0, transcendentals=0)


def params(mib=60):
    return pltpu.CompilerParams(vmem_limit_bytes=mib * 2**20)


def send(values, z=0, y=0, x=0, core=0):
    flip_wide, flip_narrow = 2 * z + y, 2 * x + core
    pairs = [
        (w * 4 + n, (w ^ flip_wide) * 4 + (n ^ flip_narrow)) for w in range(8) for n in range(4)
    ]
    return lax.ppermute(values, ALL, pairs)


def position():
    wide, narrow = lax.axis_index("wide"), lax.axis_index("narrow")
    return wide // 2, wide % 2, narrow // 2, narrow % 2


def origin():
    zero = jnp.int32(0)
    return zero, zero, zero, zero


def gather_z(values):
    return [values] + [send(values, z=k) for k in (1, 2, 3)]


def gather_chips(lines):
    return [lines] + [send(lines, x=i, y=j) for i, j in CHIP_STEPS[1:]]


def gather_cores(blocks):
    return blocks + [send(block, core=1) for block in blocks]


def pair_kernel(count, *refs):
    core = lax.rem(lax.axis_index("narrow"), 2)
    more, outs = refs[2 * count : -count], refs[-count:]
    for own, other, out in zip(refs[:count], refs[count : 2 * count], outs):
        rows, columns = own.shape[0] // 2, own.shape[1]
        half = pl.ds(pl.multiple_of(core * rows, rows), rows)

        @pl.when(core == 0)
        def _(own=own, other=other, out=out, half=half, columns=columns):
            out[:, :columns] = own[half, :]
            out[:, columns : 2 * columns] = other[half, :]

        @pl.when(core == 1)
        def _(own=own, other=other, out=out, half=half, columns=columns):
            out[:, :columns] = other[half, :]
            out[:, columns : 2 * columns] = own[half, :]

    for vector in more:
        rest, parts = vector[...], []
        for _ in range(3):
            parts.append(rest.astype(bf16).astype(f32))
            rest = rest - parts[-1]
        outs[0][:, 1152:] = rows_of(48, *parts).astype(bf16)


def pair_up(pieces, others, vectors=None):
    more = [0] * len(pieces)
    rows = ()
    if vectors is not None:
        rows = (jnp.pad(vectors, (0, 384 - vectors.shape[0])).reshape(3, 128),)
        more[0] = 128
    return pl.pallas_call(
        functools.partial(pair_kernel, len(pieces)),
        out_shape=[
            Shape((piece.shape[0] // 2, piece.shape[1] * 2 + extra), piece.dtype)
            for piece, extra in zip(pieces, more)
        ],
        cost_estimate=cost(2),
        name="pair_up",
    )(*pieces, *others, *rows)


def block_copies(place, blocks, left, out, sems):
    z, y, x, core = place()
    rows, width = blocks[0].shape[1], out.shape[1] // 2
    copies = []
    for other in range(2):
        for step, (i, j) in enumerate(CHIP_STEPS):
            for k in range(4):
                row = (((z ^ k) * 2 + (y ^ j)) * 2 + (core ^ other)) * rows
                copies.append(
                    pltpu.make_async_copy(
                        blocks[other * 4 + step].at[k, :, pl.ds(left, width)],
                        out.at[
                            pl.ds(pl.multiple_of(row, rows), rows),
                            pl.ds(pl.multiple_of((x ^ i) * width, width), width),
                        ],
                        sems.at[len(copies)],
                    )
                )
    return copies


def start(copies):
    for copy in copies:
        copy.start()


def wait(copies):
    for copy in copies:
        copy.wait()


def anywhere(count):
    return [pl.BlockSpec(memory_space=pl.ANY)] * count


def split_blocks(matrix, rows, columns):
    parts = matrix.reshape(4, 2, 2, rows, 2, columns).transpose(2, 1, 4, 0, 3, 5)
    return [parts[other, j, i] for other in range(2) for i, j in CHIP_STEPS]


def place_kernel(*refs):
    z, y, x, core = position()
    out = refs[8]
    for other in range(2):
        for step, (i, j) in enumerate(CHIP_STEPS):
            for k in range(4):
                row = ((z ^ k) * 2 + (y ^ j)) * 4 + (x ^ i) * 2 + (core ^ other)
                parts = refs[other * 4 + step][k].astype(f32)
                out[row] = parts[:3] + parts[3:6] + parts[6:9]


def place_vectors(blocks):
    table = pl.pallas_call(
        place_kernel,
        grid=(1,),
        in_specs=[pl.BlockSpec((4, 16, 128), lambda i: (0, 0, 9))] * 8,
        out_specs=fixed((32, 3, 128)),
        out_shape=Shape((32, 3, 128), f32),
        cost_estimate=cost(1),
        name="place_vectors",
    )(*blocks)
    return table.reshape(32, 384)[:, :288].reshape(12, D)


def wide_sum(*terms):
    return functools.reduce(lambda a, b: a + b, [t.astype(f32) for t in terms])


def chip_parts(kept, received):
    return [wide_sum(kept[s], received[s]).astype(bf16) for s in range(4)]


def chip_kernel(*refs):
    for kept, received, out in zip(refs[:4], refs[4:8], refs[8:]):
        out[...] = wide_sum(kept[...], received[...]).astype(bf16)


def chip_parts_of(kept, received):
    rows, columns = kept[0].shape[1:]
    line = pl.BlockSpec((1, rows, columns), lambda k: (k, 0, 0))
    return pl.pallas_call(
        chip_kernel,
        grid=(4,),
        in_specs=[line] * 8,
        out_specs=[line] * 4,
        out_shape=[Shape((4, rows, columns), bf16)] * 4,
        compiler_params=params(32),
        cost_estimate=cost(3),
        name="chip_parts",
    )(*kept, *received)


def chip_sends(parts):
    return [send(parts[s], x=i, y=j) for s, (i, j) in enumerate(CHIP_STEPS) if s]


def line_kernel(far, *refs):
    terms, outs = refs[:4], refs[4:]
    for k in range(4):
        total = wide_sum(*[term[k] for term in terms]).astype(bf16)
        if far and k >= 2:
            outs[2][k - 2] = total
        else:
            outs[k][...] = total


def line_parts(own, others, far=False):
    piece = Shape(own.shape[1:], bf16)
    shapes = [piece] * 2 + [Shape((2,) + own.shape[1:], bf16)] if far else [piece] * 4
    return pl.pallas_call(
        functools.partial(line_kernel, far),
        out_shape=shapes,
        compiler_params=params(32),
        cost_estimate=cost(2),
        name="line_parts",
    )(own, *others)


def line_sends(line):
    return [send(line[k], z=k) for k in (1, 2, 3)]


def line_halves(own, others):
    *near, far = line_parts(own, others, True)
    return near, far


def near_parts(near, received):
    return [wide_sum(near[k], received[k]).astype(near[k].dtype) for k in range(2)]


def swap_columns(summed):
    core = lax.axis_index("narrow") % 2
    columns = summed.shape[1] // 2
    left, right = summed[:, :columns], summed[:, columns:]
    mine = jnp.where(core == 0, left, right)
    other = send(jnp.where(core == 0, right, left).astype(bf16), core=1).astype(f32)
    return jnp.concatenate(
        [jnp.where(core == 0, mine, other), jnp.where(core == 0, other, mine)], 0
    )


def dot(left_side, right_side):
    return jnp.dot(left_side, right_side, preferred_element_type=f32)


def dot_t(left_side, right_side):
    return lax.dot_general(
        left_side, right_side, (((1,), (1,)), ((), ())), preferred_element_type=f32
    )


def column_sum(values):
    return jnp.sum(values, 0, keepdims=True)


def normalize(values):
    center = values - jnp.mean(values, -1, keepdims=True)
    inverse = lax.rsqrt(jnp.mean(center * center, -1, keepdims=True) + epsilon)
    return center * inverse, inverse


def normalize_back(grad_norm, normed, inverse):
    return inverse * (
        grad_norm
        - jnp.mean(grad_norm, -1, keepdims=True)
        - normed * jnp.mean(grad_norm * normed, -1, keepdims=True)
    )


def smooth(values):
    density = jnp.exp(-0.5 * values * values) * 0.3989422804014327
    below = 0.5 + 0.5 * lax.erf(values * 0.7071067811865476)
    return values * below, below + values * density


def fixed(shape):
    return pl.BlockSpec(shape, lambda i: (0,) * len(shape))


def tile(columns, rows=TILE):
    return pl.BlockSpec((rows, columns), lambda i: (i, 0))


def rows_of(count, *parts):
    missing = count - sum(part.shape[0] for part in parts)
    return jnp.concatenate(list(parts) + [jnp.zeros((missing, parts[0].shape[1]), f32)], 0)


def segment_marks(segment):
    kinds = lax.broadcasted_iota(jnp.int32, (1, 64), 1)
    mark = (segment.reshape(-1, 1) == kinds).astype(bf16)
    tall = lax.broadcasted_iota(jnp.int32, (1, 64, 1), 1)
    away = (segment[:, None, :] != tall) & (tall < 4)
    return jnp.concatenate([mark, mark], 1), jnp.where(away, -(2.0**30), 0.0).astype(bf16)


def attend_kernel(place, *refs):
    hidden, vectors, key_marks, query_marks = refs[:4]
    blocks, (packed, att, att_t, probs, weight, sems) = refs[4:12], refs[12:]

    @pl.when(pl.program_id(0) == 0)
    def _():
        copies = block_copies(place, blocks, 0, weight, sems)
        start(copies)
        wait(copies)

    length = hidden.shape[0]
    for part in range(3):
        columns = slice(part * D, (part + 1) * D)
        block = dot(hidden[...], weight[:, columns])
        if part != 1:
            block = block + vectors[part // 2 : part // 2 + 1, :]
        block = block.astype(bf16)
        if part == 0:
            block = block * jnp.asarray(0.125, bf16)
        packed[:, columns] = block
    lanes = lax.broadcasted_iota(jnp.int32, (length, 128), 1)

    def pair(p, _):
        at = pl.multiple_of(p * 128, 128)
        q_t = packed[:, pl.ds(at, 128)].T
        k = packed[:, pl.ds(D + at, 128)]
        v_t = packed[:, pl.ds(2 * D + at, 128)].T
        scores = []
        for odd in range(2):
            keys = jnp.where((lanes >= 64) == bool(odd), k, key_marks[...])
            own = q_t[64 * odd : 64 * odd + 64]
            marks = query_marks[0]
            scores.append(dot(keys, jnp.concatenate([marks, own] if odd else [own, marks], 0)))
        outs = []
        for odd in range(2):
            weights = jnp.exp(scores[odd] - jnp.max(scores[odd], 0, keepdims=True))
            low = (weights * (1.0 / column_sum(weights))).astype(bf16)
            probs[p * 2 + odd] = low
            outs.append(dot(v_t[64 * odd : 64 * odd + 64], low))
        out = jnp.concatenate(outs, 0).astype(bf16)
        att_t[pl.ds(at, 128), :] = out
        att[:, pl.ds(at, 128)] = out.T
        return 0

    lax.fori_loop(0, HEADS // 2, pair, 0, unroll=True)


def attend(place, hidden, vectors, key_marks, query_marks, blocks):
    rows, length = query_marks.shape[0], query_marks.shape[2]
    tokens = rows * length
    return pl.pallas_call(
        functools.partial(attend_kernel, place),
        grid=(rows,),
        in_specs=[
            tile(D, length),
            fixed((12, D)),
            tile(128, length),
            pl.BlockSpec((1, 64, length), lambda i: (i, 0, 0)),
        ]
        + anywhere(8),
        scratch_shapes=[pltpu.VMEM((D, 3 * D), bf16), pltpu.SemaphoreType.DMA((32,))],
        out_specs=[
            tile(3 * D, length),
            tile(D, length),
            pl.BlockSpec((D, length), lambda i: (0, i)),
            pl.BlockSpec((HEADS, length, length), lambda i: (i, 0, 0)),
        ],
        out_shape=[
            Shape((tokens, 3 * D), bf16),
            Shape((tokens, D), bf16),
            Shape((D, tokens), bf16),
            Shape((rows * HEADS, length, length), bf16),
        ],
        compiler_params=params(60),
        cost_estimate=cost(20),
        name="attend",
    )(hidden, vectors, key_marks, query_marks, *blocks)


def inner_kernel(place, *refs):
    att, hidden, vectors = refs[:3]
    blocks, (first_low, normed, inverse, activated, slope) = refs[3:11], refs[11:16]
    w_in, w_out, in_sems, out_sems = refs[16:]
    first_step = pl.program_id(0) == 0

    def row(i):
        return vectors[i : i + 1, :]

    def copies_in():
        return block_copies(place, blocks, 0, w_in, in_sems)

    @pl.when(first_step)
    def _():
        copies = block_copies(place, blocks, 1536, w_out, out_sems)
        start(copies)
        start(copies_in())
        wait(copies)

    n1, r1 = normalize(hidden[...].astype(f32) + dot(att[...], w_out[...]) + row(2))
    low = (n1 * row(3) + row(4)).astype(bf16)
    first_low[...] = low
    normed[...] = n1.astype(bf16)
    inverse[...] = jnp.broadcast_to(r1, inverse.shape)

    @pl.when(first_step)
    def _():
        wait(copies_in())

    for c in range(FF // D):
        columns = slice(c * D, c * D + D)
        act, back = smooth(dot(low, w_in[:, columns]) + row(5 + c))
        activated[:, columns] = act.astype(bf16)
        slope[:, columns] = back.astype(bf16)


def inner_forward(place, att, hidden, vectors, blocks):
    tokens = hidden.shape[0]
    return pl.pallas_call(
        functools.partial(inner_kernel, place),
        grid=(tokens // TILE,),
        in_specs=[tile(D)] * 2 + [fixed((12, D))] + anywhere(8),
        out_specs=[tile(D), tile(D), tile(128), tile(FF), tile(FF)],
        out_shape=[
            Shape((tokens, D), bf16),
            Shape((tokens, D), bf16),
            Shape((tokens, 128), f32),
            Shape((tokens, FF), bf16),
            Shape((tokens, FF), bf16),
        ],
        scratch_shapes=[
            pltpu.VMEM((D, FF), bf16),
            pltpu.VMEM((D, D), bf16),
            pltpu.SemaphoreType.DMA((32,)),
            pltpu.SemaphoreType.DMA((32,)),
        ],
        compiler_params=params(57),
        cost_estimate=cost(16),
        name="inner_forward",
    )(att, hidden, vectors, *blocks)


def outer_kernel(place, *refs):
    act, normed, cotangent, vectors = refs[:4]
    blocks, (output, grad_second, sums) = refs[4:12], refs[12:15]
    outs, (w_back, activated, grad_t, sems) = refs[15:23], refs[23:]
    step = pl.program_id(0)
    z, y, x, core = place()

    def row(i):
        return vectors[i : i + 1, :]

    @pl.when(step == 0)
    def _():
        copies = block_copies(place, blocks, 0, w_back, sems)
        start(copies)
        wait(copies)

    here = pl.ds(pl.multiple_of(step * TILE, TILE), TILE)
    activated[here, :] = act[...]
    outward = normed[...].astype(f32) * row(3) + row(4) + dot(act[...], w_back[...]) + row(9)
    n2, r2 = normalize(outward)
    output[...] = (n2 * row(10) + row(11)).astype(bf16)
    cot = cotangent[...].astype(f32)
    g2 = normalize_back(cot * row(10), n2, r2)
    grad_second[...] = g2.astype(bf16)
    part = rows_of(8, column_sum(g2), column_sum(cot * n2), column_sum(cot))

    @pl.when(step == 0)
    def _():
        sums[...] = part

    @pl.when(step > 0)
    def _():
        sums[...] += part

    g2_t = g2.astype(bf16).T
    for n in range(4):
        at = ((n % 2) ^ core) * 2 + ((n // 2) ^ x)
        piece = g2_t[n * 192 : n * 192 + 192]
        grad_t[pl.ds(pl.multiple_of(at * 192, 192), 192), here] = piece

    @pl.when(step == pl.num_programs(0) - 1)
    def _():
        for k in range(4):
            columns = pl.ds(pl.multiple_of((z ^ k) * D, D), D)
            res = dot(grad_t[...], activated[:, columns]).astype(bf16)
            for other in range(2):
                for i in range(2):
                    at = (other * 2 + i) * 192
                    pieces = [res[at : at + 192, half * 384 : half * 384 + 384] for half in range(2)]
                    for bit in range(2):

                        @pl.when(y == bit)
                        def _(other=other, i=i, k=k, pieces=pieces, bit=bit):
                            outs[other * 4 + i][k] = pieces[bit]
                            outs[other * 4 + i + 2][k] = pieces[1 - bit]


def outer_forward(place, activated, normed, cotangent, vectors, blocks):
    tokens = normed.shape[0]
    return pl.pallas_call(
        functools.partial(outer_kernel, place),
        grid=(tokens // TILE,),
        in_specs=[tile(FF), tile(D), tile(D), fixed((12, D))] + anywhere(8),
        out_specs=[tile(D), tile(D), fixed((8, D))] + [fixed((4, 192, 384))] * 8,
        out_shape=[
            Shape((tokens, D), bf16),
            Shape((tokens, D), bf16),
            Shape((8, D), f32),
        ]
        + [Shape((4, 192, 384), bf16)] * 8,
        scratch_shapes=[
            pltpu.VMEM((FF, D), bf16),
            pltpu.VMEM((tokens, FF), bf16),
            pltpu.VMEM((D, tokens), bf16),
            pltpu.SemaphoreType.DMA((32,)),
        ],
        compiler_params=params(40),
        cost_estimate=cost(18),
        name="outer_forward",
    )(activated, normed, cotangent, vectors, *blocks)


def backward_kernel(place, *refs):
    grad_second, slope, normed, inverse, first_low, att_t, vectors = refs[:7]
    blocks, back_blocks = refs[7:15], refs[15:23]
    grad_att, grad_branch, sums, sums_inner = refs[23:27]
    outs = refs[27:35]
    w_in, w_out, w_back, inner_low, first_t, grad_low, turned = refs[35:42]
    in_sems, out_sems, back_sems = refs[42:]
    step = pl.program_id(0)
    z, y, x, core = place()
    here = pl.ds(pl.multiple_of(step * TILE, TILE), TILE)

    def compute(first_step):
        if first_step:
            copies_back = block_copies(place, back_blocks, 0, w_back, back_sems)
            copies_in = block_copies(place, blocks, 0, w_in, in_sems)
            copies_out = block_copies(place, blocks, 1536, w_out, out_sems)
            start(copies_back)
            start(copies_in)
            start(copies_out)
        g2_low = grad_second[...]
        grad_first = g2_low.astype(f32)
        inner_sums = []
        for c in range(FF // D):
            columns = slice(c * D, c * D + D)
            if first_step and c == 0:
                wait(copies_back)
            gi = dot_t(g2_low, w_back[columns, :]) * slope[:, columns].astype(f32)
            inner_sums.append(column_sum(gi))
            gi = gi.astype(bf16)
            inner_low[here, columns] = gi
            if first_step and c == 0:
                wait(copies_in)
            grad_first = grad_first + dot_t(gi, w_in[:, columns])
        n1 = normed[...].astype(f32)
        g1 = normalize_back(grad_first * vectors[3:4, :], n1, inverse[:, :1])
        g1_low = g1.astype(bf16)
        grad_branch[...] = g1_low
        grad_low[here, :] = g1_low
        if first_step:
            wait(copies_out)
        grad_att[...] = dot_t(g1_low, w_out[...]).astype(bf16)
        part = rows_of(8, column_sum(g1), column_sum(grad_first * n1), column_sum(grad_first))
        part_inner = rows_of(8, *inner_sums)
        if first_step:
            sums[...] = part
            sums_inner[...] = part_inner
        else:
            sums[...] += part
            sums_inner[...] += part_inner
        low_t = first_low[...].T
        for w in range(8):
            at = ((w % 2) ^ y) * 4 + ((w // 2) ^ z)
            piece = low_t[w * 96 : w * 96 + 96]
            first_t[pl.ds(pl.multiple_of(at * 96, 96), 96), here] = piece
        turn_rows(place, att_t, turned, here)

    @pl.when(step == 0)
    def _():
        compute(True)

    @pl.when(step > 0)
    def _():
        compute(False)

    @pl.when(step == pl.num_programs(0) - 1)
    def _():
        for i in range(2):
            for other in range(2):
                at = ((x ^ i) * 2 + (core ^ other)) * D
                res = dot(first_t[...], inner_low[:, pl.ds(pl.multiple_of(at, D), D)])
                res = res.astype(bf16)
                for j in range(2):
                    for k in range(4):
                        at = (j * 4 + k) * 96
                        outs[other * 4 + i + 2 * j][k, :, :D] = res[at : at + 48]
                        outs[other * 4 + i + 2 * j][k, :, D : 2 * D] = res[at + 48 : at + 96]
        res = dot(turned[...], grad_low[...]).astype(bf16)
        for bit in range(2):

            @pl.when(x == bit)
            def _(bit=bit):
                for other in range(2):
                    for j in range(2):
                        for k in range(4):
                            at = (other * 8 + j * 4 + k) * 48
                            for half in range(2):
                                piece = res[at : at + 48, half * 384 : half * 384 + 384]
                                outs[other * 4 + (half ^ bit) + 2 * j][k, :, 2 * D :] = piece


def backward(place, grad_second, slope, normed, inverse, first_low, att_t, vectors, *weights):
    blocks, back_blocks = weights
    tokens = normed.shape[0]
    outs = [(4, 48, 1920)] * 8
    return pl.pallas_call(
        functools.partial(backward_kernel, place),
        grid=(tokens // TILE,),
        in_specs=[tile(D), tile(FF), tile(D), tile(128), tile(D)]
        + [pl.BlockSpec((D, TILE), lambda i: (0, i)), fixed((12, D))]
        + anywhere(16),
        out_specs=[tile(D), tile(D)] + [fixed(s) for s in [(8, D)] * 2 + outs],
        out_shape=[Shape((tokens, D), bf16), Shape((tokens, D), bf16)]
        + [Shape((8, D), f32)] * 2
        + [Shape(s, bf16) for s in outs],
        scratch_shapes=[
            pltpu.VMEM((D, FF), bf16),
            pltpu.VMEM((D, D), bf16),
            pltpu.VMEM((FF, D), bf16),
            pltpu.VMEM((tokens, FF), bf16),
            pltpu.VMEM((D, tokens), bf16),
            pltpu.VMEM((tokens, D), bf16),
            pltpu.VMEM((D, tokens), bf16),
        ]
        + [pltpu.SemaphoreType.DMA((32,))] * 3,
        compiler_params=params(32),
        cost_estimate=cost(22),
        name="backward",
    )(grad_second, slope, normed, inverse, first_low, att_t, vectors, *blocks, *back_blocks)


def turn_rows(place, source, turned, columns=slice(None)):
    z, y, _, core = place()
    for w in range(8):
        for half in range(2):
            at = (half ^ core) * 8 + ((w % 2) ^ y) * 4 + ((w // 2) ^ z)
            piece = (w * 2 + half) * 48
            rows = pl.ds(pl.multiple_of(at * 48, 48), 48)
            turned[rows, columns] = source[piece : piece + 48, :]


def attend_back_kernel(packed, grad_att, probs, grad_low, sums):
    length = packed.shape[0]
    lanes = lax.broadcasted_iota(jnp.int32, (length, 128), 1)
    zero = jnp.zeros((length, 128), bf16)
    blank = jnp.zeros((64, length), bf16)

    def pair(p, _):
        at = pl.multiple_of(p * 128, 128)
        q = packed[:, pl.ds(at, 128)]
        k_t = packed[:, pl.ds(D + at, 128)].T
        v = packed[:, pl.ds(2 * D + at, 128)]
        g = grad_att[:, pl.ds(at, 128)]
        g_t = g.T
        grad_probs = []
        for odd in range(2):
            own = g_t[64 * odd : 64 * odd + 64]
            grad_probs.append(dot(v, jnp.concatenate([blank, own] if odd else [own, blank], 0)))
        dk = dv = 0.0
        dq_t = []
        for odd in range(2):
            mine = (lanes >= 64) == bool(odd)
            low = probs[p * 2 + odd]
            wide = low.astype(f32)
            gp = grad_probs[odd]
            ds = (wide * (gp - column_sum(wide * gp))).astype(bf16)
            dv = dv + dot(low, jnp.where(mine, g, zero))
            dk = dk + dot(ds, jnp.where(mine, q, zero))
            dq_t.append(dot(k_t[64 * odd : 64 * odd + 64], ds))
        dq = jnp.concatenate(dq_t, 0).T * 0.125
        sums[0, :, pl.ds(at, 128)] = rows_of(8, column_sum(dq), column_sum(dv))
        grad_low[:, pl.ds(at, 128)] = dq.astype(bf16)
        grad_low[:, pl.ds(D + at, 128)] = dk.astype(bf16)
        grad_low[:, pl.ds(2 * D + at, 128)] = dv.astype(bf16)
        return 0

    lax.fori_loop(0, HEADS // 2, pair, 0, unroll=True)


def attend_back(row, packed, grad_att, probs, low=None):
    length = probs.shape[1]
    kernel, more, specs, alias = attend_back_kernel, (), [], {}
    if low is not None:
        more, specs, alias = (low,), [pl.BlockSpec(memory_space=pl.ANY)], {3: 0}

        def kernel(packed, grad_att, probs, low, grad_low, sums):
            attend_back_kernel(packed, grad_att, probs, grad_low, sums)

    return pl.pallas_call(
        kernel,
        grid=(1,),
        in_specs=[
            pl.BlockSpec((length, 3 * D), lambda i: (row, 0)),
            pl.BlockSpec((length, D), lambda i: (row, 0)),
            pl.BlockSpec((HEADS, length, length), lambda i: (row, 0, 0)),
        ]
        + specs,
        out_specs=[
            pl.BlockSpec((length, 3 * D), lambda i: (row, 0)),
            pl.BlockSpec((1, 8, D), lambda i: (0, 0, 0)),
        ],
        out_shape=[Shape(packed.shape, bf16), Shape((1, 8, D), f32)],
        input_output_aliases=alias,
        compiler_params=params(32),
        cost_estimate=cost(12),
        name="attend_back",
    )(packed, grad_att, probs, *more)


def grad_qkv_kernel(place, hidden, low, *refs):
    sums_zero, sums_one, sums_first, sums_inner, sums_second = refs[:5]
    outs, turned, groups = refs[5:13], refs[13], refs[14]
    z, y, x, core = place()
    turn_rows(place, hidden[...].T, turned)
    rows = [sums_zero[0, i : i + 1, :] + sums_one[0, i : i + 1, :] for i in range(2)]
    rows += [sums_first[i : i + 1, :] for i in range(3)]
    rows += [sums_inner[i : i + 1, :] for i in range(4)]
    rows += [sums_second[i : i + 1, :] for i in range(3)]
    for group in range(72):
        column = group % 6 * 128
        groups[group] = rows[group // 6][:, column : column + 128]
    for group in range(72, 76):
        groups[group] = jnp.zeros((1, 128), f32)
    for i in range(2):
        columns = pl.ds(pl.multiple_of((x ^ i) * 1152, 128), 1152)
        res = dot(turned[...], low[:, columns]).astype(bf16)
        for other in range(2):
            for j in range(2):
                out = outs[other * 4 + i + 2 * j]
                for k in range(4):
                    at = (other * 8 + j * 4 + k) * 48
                    out[k, :, :1152] = res[at : at + 48]
                    device = ((z ^ k) * 2 + (y ^ j)) * 4 + (x ^ i) * 2 + (core ^ other)
                    group = (9 * device) // 4
                    part = jnp.concatenate([groups[group + q] for q in range(4)], 0)
                    out[k, :16, 1152:] = rows_of(16, part).astype(bf16)
                    out[k, 16:, 1152:] = jnp.zeros((32, 128), bf16)


def grad_qkv(place, hidden, low, *sums):
    return pl.pallas_call(
        functools.partial(grad_qkv_kernel, place),
        out_shape=[Shape((4, 48, 1280), bf16)] * 8,
        scratch_shapes=[pltpu.VMEM((D, hidden.shape[0]), bf16), pltpu.VMEM((80, 1, 128), f32)],
        compiler_params=params(32),
        cost_estimate=cost(9),
        name="grad_qkv",
    )(hidden, low, *sums)


def cut_vectors(place, groups):
    z, y, x, core = place()
    at = (((z * 2 + y) * 4 + x * 2 + core) * 288) % 128
    return lax.dynamic_slice(groups.reshape(-1), (at,), (288,))


def hidden_kernel(place, *refs):
    low, grad_branch, blocks, out, weight, sems = *refs[:2], refs[2:10], *refs[10:]

    @pl.when(pl.program_id(0) == 0)
    def _():
        copies = block_copies(place, blocks, 0, weight, sems)
        start(copies)
        wait(copies)

    out[...] = grad_branch[...].astype(f32) + dot_t(low[...], weight[...])


def grad_of_hidden(place, low, grad_branch, blocks):
    tokens = low.shape[0]
    return pl.pallas_call(
        functools.partial(hidden_kernel, place),
        grid=(tokens // TILE,),
        in_specs=[tile(3 * D), tile(D)] + anywhere(8),
        out_specs=tile(D),
        out_shape=Shape((tokens, D), f32),
        scratch_shapes=[pltpu.VMEM((D, 3 * D), bf16), pltpu.SemaphoreType.DMA((32,))],
        compiler_params=params(60),
        cost_estimate=cost(9),
        name="grad_hidden",
    )(low, grad_branch, *blocks)


def gather_plain(w_qkv, w_out, w_in, w_back, vectors):
    def whole(piece):
        return lax.all_gather(
            lax.all_gather(piece, "narrow", axis=1, tiled=True), "wide", axis=0, tiled=True
        )

    full = tuple(whole(piece) for piece in (w_qkv, w_out, w_in, w_back))
    return full + (lax.all_gather(vectors, ALL, axis=0, tiled=True).reshape(12, D),)


def tie(*values):
    return lax.optimization_barrier(values)


def unfold(table, order, shape):
    return table.reshape((2, 2, 2, 4) + table.shape[3:]).transpose(order).reshape(shape)


def scatter_whole(matrix):
    part = lax.psum_scatter(matrix, "wide", scatter_dimension=0, tiled=True)
    part = lax.psum_scatter(part, "narrow", scatter_dimension=1, tiled=True)
    return part.astype(f32)


def per_device(hidden, segment, w_qkv, w_out, w_in, w_back, vectors, cotangent):
    (qkv,) = pair_up([w_qkv], [send(w_qkv, core=1)], vectors)
    rest = [w_out, w_in, w_back]
    other_rest = [send(piece, core=1) for piece in rest]
    qkv, other_rest, segment = tie(qkv, other_rest, segment)
    key_marks, query_marks = segment_marks(segment)
    qkv_line = gather_z(qkv)
    out, inner, back = pair_up(rest, other_rest)
    mid = jnp.concatenate([inner, out], 1)
    qkv_line, mid, back, key_marks, query_marks = tie(
        jnp.stack(qkv_line), mid, back, key_marks, query_marks
    )

    qkv_blocks = gather_chips(qkv_line)
    mid_line = gather_z(mid)
    back, mid_line[2] = tie(back, mid_line[2])
    next_back = send(back, z=1)
    qkv_blocks, mid_line, back, next_back = tie(qkv_blocks, mid_line, back, next_back)

    mid_blocks = gather_chips(jnp.stack(mid_line))
    qkv_blocks = gather_cores(qkv_blocks)
    back_two = jnp.stack([back, next_back])
    all_vectors = place_vectors(qkv_blocks)
    back_two, all_vectors = tie(back_two, all_vectors)
    far_two = send(back_two, z=2)
    attended = attend(position, hidden, all_vectors, key_marks, query_marks, qkv_blocks)
    own_mid = send(mid_blocks[0], core=1)
    attended, mid_blocks, far_two, own_mid = tie(attended, mid_blocks, far_two, own_mid)
    packed, att, att_t, probs = attended

    back_blocks = gather_chips(jnp.concatenate([back_two, far_two]))
    mid_blocks = mid_blocks + [own_mid] + [send(block, core=1) for block in mid_blocks[1:]]
    inner_outs = inner_forward(position, att, hidden, all_vectors, mid_blocks)
    own_back = send(back_blocks[0], core=1)
    inner_outs, back_blocks, own_back = tie(inner_outs, back_blocks, own_back)
    back_blocks = back_blocks + [own_back] + [send(block, core=1) for block in back_blocks[1:]]
    first_low, normed, inverse, activated, slope = inner_outs

    output, grad_second, sums_second, *tables_back = outer_forward(
        position, activated, normed, cotangent, all_vectors, back_blocks
    )

    received_back = [send(block, core=1) for block in tables_back[4:]]
    parts_back = chip_parts(tables_back[:4], received_back)
    parts_back, grad_second = tie(parts_back, grad_second)
    others_back = chip_sends(parts_back)
    back_outs = backward(
        position,
        grad_second,
        slope,
        normed,
        inverse,
        first_low,
        att_t,
        all_vectors,
        mid_blocks,
        back_blocks,
    )
    back_outs, others_back = tie(back_outs, others_back)
    grad_att, grad_branch, sums_first, sums_inner, *tables_mid = back_outs

    received_mid = [send(block, core=1) for block in tables_mid[4:]]
    near_back, far_back = line_halves(parts_back[0], others_back)
    parts_mid = chip_parts(tables_mid[:4], received_mid)
    parts_mid, grad_att, near_back, far_back = tie(parts_mid, grad_att, near_back, far_back)

    plane_mid = [send(parts_mid[1], x=1), send(parts_mid[2], y=1)]
    corner_mid = send(parts_mid[3], x=1, y=1)
    packed_low, sums_zero = attend_back(0, packed, grad_att, probs)
    packed_low, far_back = tie(packed_low, far_back)
    far_back = send(far_back, z=2)
    packed_low, sums_one = attend_back(1, packed, grad_att, probs, packed_low)
    tables_qkv = grad_qkv(
        position, hidden, packed_low, sums_zero, sums_one, sums_first, sums_inner, sums_second
    )
    tables_qkv, far_back, plane_mid = tie(tables_qkv, far_back, plane_mid)
    kept_qkv, sent_qkv = tables_qkv[:4], tables_qkv[4:]

    received_qkv = [send(block, core=1) for block in sent_qkv]
    parts_qkv = chip_parts_of(kept_qkv, received_qkv)
    parts_qkv, grad_branch, near_back, corner_mid = tie(
        parts_qkv, grad_branch, near_back, corner_mid
    )
    others_qkv = chip_sends(parts_qkv)
    near_mid, far_mid = line_halves(parts_mid[0], plane_mid + [corner_mid])
    far_mid = send(far_mid, z=2)
    near_back = near_parts(near_back, far_back)
    next_back = send(near_back[1], z=1)
    near_back, grad_branch = tie(near_back, grad_branch)
    grad_hidden = grad_of_hidden(position, packed_low, grad_branch, qkv_blocks)
    grad_hidden, far_mid, next_back, others_qkv = tie(
        grad_hidden, far_mid, next_back, others_qkv
    )

    own_back = wide_sum(near_back[0], next_back).T
    near_mid = near_parts(near_mid, far_mid)
    next_mid = send(near_mid[1], z=1)
    others_qkv, near_mid = tie(others_qkv, near_mid)
    line_qkv = line_parts(parts_qkv[0], others_qkv)
    lines_qkv = line_sends(line_qkv)
    own_mid = wide_sum(near_mid[0], next_mid)
    own_in = jnp.concatenate([own_mid[:, :D], own_mid[:, D : 2 * D]], 0)
    own_out = swap_columns(own_mid[:, 2 * D :])
    own_in, own_out, own_back, lines_qkv = tie(own_in, own_out, own_back, lines_qkv)
    own_qkv = wide_sum(line_qkv[0], *lines_qkv)
    own_vectors = cut_vectors(position, own_qkv[:4, 1152:])
    own_qkv = swap_columns(own_qkv[:, :1152])
    return (output, grad_hidden, own_qkv, own_out, own_in, own_back, own_vectors)


def per_device_plain(hidden, segment, w_qkv, w_out, w_in, w_back, vectors, cotangent):
    key_marks, query_marks = segment_marks(segment)
    full_qkv, full_out, full_in, full_back, all_vectors = gather_plain(
        w_qkv, w_out, w_in, w_back, vectors
    )
    qkv_blocks = split_blocks(full_qkv, 48, 1152)
    mid_blocks = [
        jnp.concatenate(pair, 2)
        for pair in zip(split_blocks(full_in, 48, 1536), split_blocks(full_out, 48, 384))
    ]
    back_pieces = split_blocks(full_back, 192, 384)
    packed, att, att_t, probs = attend(
        origin, hidden, all_vectors, key_marks, query_marks, qkv_blocks
    )
    first_low, normed, inverse, activated, slope = inner_forward(
        origin, att, hidden, all_vectors, mid_blocks
    )
    output, grad_second, sums_second, *back_table = outer_forward(
        origin, activated, normed, cotangent, all_vectors, back_pieces
    )
    grad_att, grad_branch, sums_first, sums_inner, *tables = backward(
        origin,
        grad_second,
        slope,
        normed,
        inverse,
        first_low,
        att_t,
        all_vectors,
        mid_blocks,
        back_pieces,
    )
    mid_table = jnp.stack(tables).reshape(2, 4, 4, 48, 1920)
    packed_low, sums_zero = attend_back(0, packed, grad_att, probs)
    packed_low, sums_one = attend_back(1, packed, grad_att, probs, packed_low)
    grad_hidden = grad_of_hidden(origin, packed_low, grad_branch, qkv_blocks)
    tables = grad_qkv(
        origin, hidden, packed_low, sums_zero, sums_one, sums_first, sums_inner, sums_second
    )
    grad_vectors = jnp.concatenate(
        [(sums_zero + sums_one)[0, :2], sums_first[:3], sums_inner[:4], sums_second[:3]], 0
    )
    qkv_table = jnp.stack(tables)
    qkv_table = qkv_table.reshape(2, 4, 4, 48, 1280)
    halves = jnp.stack([mid_table[..., :D], mid_table[..., D : 2 * D]], 4)
    own_qkv = scatter_whole(unfold(qkv_table[..., :1152], (3, 1, 0, 4, 2, 5), (D, 3 * D)))
    own_out = scatter_whole(unfold(mid_table[..., 2 * D :], (3, 1, 0, 4, 2, 5), (D, D)))
    own_in = scatter_whole(unfold(halves, (3, 1, 4, 5, 2, 0, 6), (D, FF)))
    back_table = jnp.stack(back_table).reshape(2, 4, 4, 192, 384)
    back_t = unfold(back_table, (2, 0, 4, 3, 1, 5), (D, FF))
    own_back = scatter_whole(back_t.T)
    own_vectors = lax.psum_scatter(
        grad_vectors.reshape(-1), ALL, scatter_dimension=0, tiled=True
    )
    return (output, grad_hidden, own_qkv, own_out, own_in, own_back, own_vectors)


def solution(mesh):
    trees = mesh.shape["wide"] == 8 and mesh.shape["narrow"] == 4
    return jax.shard_map(
        per_device if trees else per_device_plain,
        mesh=mesh,
        in_specs=(P(ALL, None),) * 2 + (P("wide", "narrow"),) * 4 + (P(ALL), P(ALL, None)),
        out_specs=(P(ALL, None),) * 2 + (P("wide", "narrow"),) * 4 + (P(ALL),),
        check_vma=False,
    )
```
